32 devices in a mesh: seq: 2 (over y), blk: 4 (over z), uly: 4 (over x, core).
Axes of the slice: x: 2, y: 2, z: 4, core: 2. Of those that a mesh axis runs over, the one named last changes fastest.
Arguments:
- inputs: bfloat16 [8, 1024, 2048], P('seq', ('blk', 'uly')), may hold values from -6 to 6
- doc_lengths: int32 [8, 3], P('seq'), may hold values from 1 to 896, 1024 in all within a row
- ln1_gain: bfloat16 [2048], P(('seq', 'blk', 'uly')), may hold values from 0.099609375 to 1.8984375
- ln1_shift: bfloat16 [2048], P(('seq', 'blk', 'uly')), may hold values from -1.5 to 1.5
- w_query: bfloat16 [2048, 2048], P(('seq', 'blk', 'uly')), may hold values from -0.125 to 0.125
- b_query: bfloat16 [2048], P(('seq', 'blk', 'uly')), may hold values from -1.5 to 1.5
- w_key: bfloat16 [2048, 2048], P(('seq', 'blk', 'uly')), may hold values from -0.125 to 0.125
- w_value: bfloat16 [2048, 2048], P(('seq', 'blk', 'uly')), may hold values from -0.125 to 0.125
- b_value: bfloat16 [2048], P(('seq', 'blk', 'uly')), may hold values from -1.5 to 1.5
- w_out: bfloat16 [2048, 2048], P(('seq', 'blk', 'uly')), may hold values from -1.5 to 1.5
- b_out: bfloat16 [2048], P(('seq', 'blk', 'uly')), may hold values from -1.5 to 1.5
- ln2_gain: bfloat16 [2048], P(('seq', 'blk', 'uly')), may hold values from 0.099609375 to 1.8984375
- ln2_shift: bfloat16 [2048], P(('seq', 'blk', 'uly')), may hold values from -1.5 to 1.5
- w_fc: bfloat16 [2048, 8192], P(('seq', 'blk', 'uly')), may hold values from -0.125 to 0.125
- b_fc: bfloat16 [8192], P(('seq', 'blk', 'uly')), may hold values from -1.5 to 1.5
- w_proj: bfloat16 [8192, 2048], P(('seq', 'blk', 'uly')), may hold values from -0.0625 to 0.0625
- b_proj: bfloat16 [2048], P(('seq', 'blk', 'uly')), may hold values from -1.5 to 1.5
- cotangent: bfloat16 [8, 1024, 2048], P('seq', ('blk', 'uly')), may hold values from -6 to 6
Outputs:
- output: bfloat16 [8, 1024, 2048], P('seq', ('blk', 'uly'))
- grad_inputs: bfloat16 [8, 1024, 2048], P('seq', ('blk', 'uly'))
- grad_ln1_gain: float32 [2048], P(('seq', 'blk', 'uly'))
- grad_ln1_shift: float32 [2048], P(('seq', 'blk', 'uly'))
- grad_w_query: float32 [2048, 2048], P(('seq', 'blk', 'uly'))
- grad_b_query: float32 [2048], P(('seq', 'blk', 'uly'))
- grad_w_key: float32 [2048, 2048], P(('seq', 'blk', 'uly'))
- grad_w_value: float32 [2048, 2048], P(('seq', 'blk', 'uly'))
- grad_b_value: float32 [2048], P(('seq', 'blk', 'uly'))
- grad_w_out: float32 [2048, 2048], P(('seq', 'blk', 'uly'))
- grad_b_out: float32 [2048], P(('seq', 'blk', 'uly'))
- grad_ln2_gain: float32 [2048], P(('seq', 'blk', 'uly'))
- grad_ln2_shift: float32 [2048], P(('seq', 'blk', 'uly'))
- grad_w_fc: float32 [2048, 8192], P(('seq', 'blk', 'uly'))
- grad_b_fc: float32 [8192], P(('seq', 'blk', 'uly'))
- grad_w_proj: float32 [8192, 2048], P(('seq', 'blk', 'uly'))
- grad_b_proj: float32 [2048], P(('seq', 'blk', 'uly'))
The draws below stay inside these ranges and needn't reach their ends.
Inputs may be any that keep to these rules, and one draw needn't show every extreme that they name: `doc_lengths`: each row holds the lengths of the 3 documents packed in order into one sequence; they sum to 1024, and the longest is exactly 896 positions long.
All inputs are finite; a program needn't handle non-finite values.
Results may differ from the reference program's by a relative error of at most 0.02.
Values may be sent and summed in bfloat16 or wider, within the bound.
A program may use at most 448 MiB of HBM per device.

```python
import math
import jax
import jax.numpy as jnp
import numpy as np
from jax import lax

D = 2048
HEADS = 16
HD = 128
FF = 8192
NDOC = 3
LEN = 1024
BLK_ROWS = 256
NSEQ = 8


def with_spikes(values, own_key, source, target, shards_of, factor):
    owner, partner = [(jnp.arange(values.shape[axis_at]) // (values.shape[axis_at] // shards_of)).reshape([-1 if axis == axis_at else 1 for axis in range(values.ndim)]) for axis_at in (source, target)]
    chosen = jax.random.permutation(own_key, shards_of)[partner]
    strong = (owner == chosen) | (owner == (partner + shards_of // 2) % shards_of)
    return jnp.where(strong, factor * values, values)


def levels(rng, extent, pieces, smallest, top_value):
    level = 1.0
    for axis_at, parts in pieces:
        draws = jax.random.uniform(jax.random.fold_in(jax.random.fold_in(rng, 6), axis_at), (parts,), jnp.float32, smallest / len(pieces), top_value / len(pieces))
        level = level * jnp.repeat(jnp.exp(draws), extent[axis_at] // parts).reshape((-1,) + (1,) * (len(extent) - 1 - axis_at))
    return level


def length_profile(number_of, total, reach, skew):
    weights = [(1 << 20) // math.isqrt(rank ** skew) + 1 for rank in range(2, number_of + 1)]
    rest, counts = total - reach - (number_of - 1), [1] * (number_of - 1)
    while rest > 0:
        candidates = [i for i in range(number_of - 1) if counts[i] < reach]
        mass, remaining = sum([weights[i] for i in candidates]), rest
        for i in candidates:
            more = min(reach - counts[i], max(1, remaining * weights[i] // mass), rest)
            counts[i] = counts[i] + more
            rest = rest - more
    return np.array([reach] + counts)


def ragged_sizes(key, count, total, limit, skew):
    if count == 2:
        one = jax.random.randint(key, (), max(1, total - limit), min(limit, total - 1) + 1)
        return jnp.stack([one, total - one])
    tallies = jnp.asarray(length_profile(count, total, limit, skew), jnp.int32)
    pairs = (count - 1) // 2
    donor, sink = tallies[1:1 + 2 * pairs:2], tallies[2:2 + 2 * pairs:2]
    slack = jnp.minimum(donor - 1, limit - sink)
    passed = jax.random.randint(jax.random.fold_in(key, 1), (pairs,), 0, 1 << 20) % (slack + 1)
    tallies = tallies.at[1:1 + 2 * pairs:2].set(donor - passed).at[2:2 + 2 * pairs:2].set(sink + passed)
    return tallies[jax.random.permutation(jax.random.fold_in(key, 2), count)]


def scatter_about(own_key, dims, scale, reach, pieces=(), kind=jnp.bfloat16):
    values = scale * jax.random.normal(own_key, dims, jnp.float32)
    if pieces:
        values = values * levels(own_key, dims, pieces, -0.22, 0.18)
    return jnp.clip(values, -reach, reach).astype(kind)


def noise_with(key, shape, spread, limit, pieces, heavy, held_as=jnp.bfloat16):
    entries = spread * jax.random.normal(key, shape, jnp.float32)
    if pieces:
        entries = entries * levels(key, shape, pieces, -0.22, 0.18)
    return jnp.clip(with_spikes(entries, jax.random.fold_in(key, 3), *heavy), -limit, limit).astype(held_as)


def setup_inputs(seed: int = 0) -> dict:
    arg_keys = jax.random.split(jax.random.key(seed), 19)
    inputs = scatter_about(arg_keys[0], (NSEQ, LEN, D), 1.0, 6.0, ((0, 2), (1, 16)))
    doc_lengths = jax.vmap(lambda own: ragged_sizes(own, NDOC, LEN, LEN - BLK_ROWS // 2, 0))(jax.random.split(arg_keys[1], NSEQ)).reshape((NSEQ, NDOC)).astype(jnp.int32)
    ln1_gain = jnp.clip(1.0 + 0.18 * jax.random.normal(arg_keys[2], (D,), jnp.float32), 0.099609375, 1.8984375).astype(jnp.bfloat16)
    ln1_shift = scatter_about(arg_keys[3], (D,), 0.3, 1.5, ((0, 32),))
    w_query = scatter_about(arg_keys[4], (D, D), D ** -0.5, 0.125, ((0, 32),))
    b_query = scatter_about(arg_keys[5], (D,), 0.3, 1.5, ((0, 32),))
    w_key = scatter_about(arg_keys[6], (D, D), D ** -0.5, 0.125, ((0, 32),))
    w_value = scatter_about(arg_keys[7], (D, D), D ** -0.5, 0.125, ((0, 32),))
    b_value = scatter_about(arg_keys[8], (D,), 0.3, 1.5, ((0, 32),))
    w_out = scatter_about(arg_keys[9], (D, D), (max(1, D * 8 // LEN)) ** -0.5, 1.5, ((0, 32),))
    b_out = scatter_about(arg_keys[10], (D,), 0.3, 1.5, ((0, 32),))
    ln2_gain = jnp.clip(1.0 + 0.18 * jax.random.normal(arg_keys[11], (D,), jnp.float32), 0.099609375, 1.8984375).astype(jnp.bfloat16)
    ln2_shift = scatter_about(arg_keys[12], (D,), 0.3, 1.5, ((0, 32),))
    w_fc = scatter_about(arg_keys[13], (D, FF), D ** -0.5, 0.125, ((0, 32),))
    b_fc = scatter_about(arg_keys[14], (FF,), 0.3, 1.5, ((0, 32),))
    w_proj = scatter_about(arg_keys[15], (FF, D), FF ** -0.5, 0.0625, ((0, 32),))
    b_proj = scatter_about(arg_keys[16], (D,), 0.3, 1.5, ((0, 32),))
    cotangent = noise_with(arg_keys[17], (NSEQ, LEN, D), 1.0, 6.0, ((0, 2), (1, 16)), (1, 2, 16, 2.0))
    return {"inputs": inputs, "doc_lengths": doc_lengths, "ln1_gain": ln1_gain, "ln1_shift": ln1_shift, "w_query": w_query, "b_query": b_query, "w_key": w_key, "w_value": w_value, "b_value": b_value, "w_out": w_out, "b_out": b_out, "ln2_gain": ln2_gain, "ln2_shift": ln2_shift, "w_fc": w_fc, "b_fc": b_fc, "w_proj": w_proj, "b_proj": b_proj, "cotangent": cotangent}


@jax.custom_vjp
def low(v):
    return lax.optimization_barrier(v.astype(jnp.bfloat16)).astype(jnp.float32)

@jax.custom_vjp
def low_back(v):
    return v

def low_keep(v):
    return (low(v), None)

def low_pass(kept, grad):
    return (grad,)

def back_keep(v):
    return (v, None)

def back_low(kept, grad):
    return (low(grad),)
low.defvjp(low_keep, low_pass)
low_back.defvjp(back_keep, back_low)
EPS = 1e-05
NEGATIVE = -1e+30

def matmul(left_side, right_side):
    return jnp.dot(left_side, right_side, precision=lax.Precision.HIGHEST, preferred_element_type=jnp.float32)

def layer_norm(values, norm_gain, norm_shift):
    average = lax.optimization_barrier(jnp.mean(values, axis=-1, keepdims=True))
    centred = values - average
    variance = lax.optimization_barrier(jnp.mean(centred * centred, axis=-1, keepdims=True))
    return centred * lax.rsqrt(variance + EPS) * norm_gain + norm_shift

def gelu_tanh(values):
    return jax.nn.gelu(values, approximate=True)

def head_attention(query_rows, key_rows, value_rows, allowed):
    scores = low_back(matmul(query_rows, key_rows.T))
    scores = jnp.where(allowed, scores, NEGATIVE)
    highest = lax.optimization_barrier(jnp.max(scores, axis=1, keepdims=True))
    powered = jnp.exp(scores - highest)
    chances = low(powered / lax.optimization_barrier(jnp.sum(powered, axis=1, keepdims=True)))
    return matmul(chances, value_rows)

def sequence_layer(params, tokens, allowed):
    ln1_gain, ln1_shift, w_query, b_query, w_key, w_value, b_value, w_out, b_out, ln2_gain, ln2_shift, w_fc, b_fc, w_proj, b_proj = params
    scale = 1.0 / math.sqrt(HD)
    normed = low(layer_norm(tokens, ln1_gain, ln1_shift))
    queries = low(low_back((matmul(normed, w_query) + b_query) * scale))
    key_rows = low(low_back(matmul(normed, w_key)))
    value_rows = low(low_back(matmul(normed, w_value) + b_value))

    def by_head(matrix):
        return matrix.reshape(LEN, HEADS, HD).transpose(1, 0, 2)

    def one_head(triple):
        return head_attention(triple[0], triple[1], triple[2], allowed)
    heads_out = lax.map(jax.checkpoint(one_head), (by_head(queries), by_head(key_rows), by_head(value_rows)))
    attended = low(low_back(heads_out.transpose(1, 0, 2).reshape(LEN, HEADS * HD)))
    hidden = tokens + low_back(matmul(attended, w_out) + b_out)
    normed_two = low(layer_norm(hidden, ln2_gain, ln2_shift))
    inner = low_back(matmul(normed_two, w_fc) + b_fc)
    active = low(gelu_tanh(inner))
    return hidden + low_back(matmul(active, w_proj) + b_proj)

def reference(inputs, doc_lengths, ln1_gain, ln1_shift, w_query, b_query, w_key, w_value, b_value, w_out, b_out, ln2_gain, ln2_shift, w_fc, b_fc, w_proj, b_proj, cotangent):
    params = tuple((tensor.astype(jnp.float32) for tensor in (ln1_gain, ln1_shift, w_query, b_query, w_key, w_value, b_value, w_out, b_out, ln2_gain, ln2_shift, w_fc, b_fc, w_proj, b_proj)))
    positions = jnp.arange(LEN, dtype=jnp.int32)

    def sequence_step(totals, inputs_here):
        tokens, lengths, grad_out = inputs_here
        bounds = jnp.cumsum(lengths).astype(jnp.int32)
        doc_ids = (positions >= bounds[0]).astype(jnp.int32) + (positions >= bounds[1]).astype(jnp.int32)
        allowed = (positions[None, :] <= positions[:, None]) & (doc_ids[None, :] == doc_ids[:, None])

        def layer_of(param_set, token_set):
            return sequence_layer(param_set, token_set, allowed)
        result, pullback = jax.vjp(layer_of, params, tokens.astype(jnp.float32))
        grad_set, grad_tokens = pullback(grad_out.astype(jnp.float32))
        totals = jax.tree.map(jnp.add, totals, grad_set)
        return (totals, (result.astype(jnp.bfloat16), grad_tokens.astype(jnp.bfloat16)))
    zeros = tuple((jnp.zeros(tensor.shape, jnp.float32) for tensor in params))
    totals, outputs_pair = lax.scan(sequence_step, zeros, (inputs, doc_lengths, cotangent))
    return (outputs_pair[0], outputs_pair[1], totals[0], totals[1], totals[2], totals[3], totals[4], totals[5], totals[6], totals[7], totals[8], totals[9], totals[10], totals[11], totals[12], totals[13], totals[14])
```

```python
import math

import jax
import jax.numpy as jnp
from jax import lax
from jax.sharding import PartitionSpec as P

HD = 128
EPS = 1e-05
NEGATIVE = -1e30
ALL = ("seq", "blk", "uly")
PLANE = ("seq", "uly")
BF = jnp.bfloat16
F32 = jnp.float32


def layer_norm(values, norm_gain, norm_shift):
    average = jnp.mean(values, axis=-1, keepdims=True)
    centred = values - average
    variance = jnp.mean(centred * centred, axis=-1, keepdims=True)
    return centred * lax.rsqrt(variance + EPS) * norm_gain + norm_shift


def gelu_tanh(values):
    return jax.nn.gelu(values, approximate=True)


def product(left_side, right_side):
    return jnp.dot(left_side, right_side, preferred_element_type=F32)


def transposed(left_side, right_side):
    return lax.dot_general(
        left_side, right_side, (((0,), (0,)), ((), ())), preferred_element_type=F32
    )


def against(left_side, right_side):
    return lax.dot_general(
        left_side, right_side, (((1,), (1,)), ((), ())), preferred_element_type=F32
    )


def gather_plane(rows):
    return lax.all_gather(rows, PLANE, axis=0, tiled=True)


def scatter_plane(rows):
    return lax.psum_scatter(rows.astype(BF), PLANE, scatter_dimension=0, tiled=True)


def on_device(
    inputs,
    doc_lengths,
    ln1_gain,
    ln1_shift,
    w_query,
    b_query,
    w_key,
    w_value,
    b_value,
    w_out,
    b_out,
    ln2_gain,
    ln2_shift,
    w_fc,
    b_fc,
    w_proj,
    b_proj,
    cotangent,
):
    seqs, tok, width = inputs.shape
    n_seq, n_blk, n_uly = (lax.axis_size(a) for a in ALL)
    plane = n_seq * n_uly
    devices = plane * n_blk
    here_seq, here_blk, here_uly = (lax.axis_index(a) for a in ALL)
    here = here_seq * n_uly + here_uly
    scale = 1.0 / math.sqrt(HD)
    rows = w_query.shape[0]
    hidden_rows = w_proj.shape[0]
    share = width // plane
    heads = share // HD
    ff_share = hidden_rows * n_blk
    sharing = max(1, n_blk // seqs)
    held = seqs * sharing // n_blk
    part = tok // sharing
    n_rows = n_blk * held * part

    high = doc_lengths // 16
    vectors = (ln1_gain, ln1_shift, b_query, b_value, b_out, ln2_gain, ln2_shift, b_proj)
    small = jnp.concatenate(
        vectors
        + (
            b_fc,
            high.reshape(-1).astype(BF),
            (doc_lengths - 16 * high).reshape(-1).astype(BF),
        )
    )
    small = lax.all_gather(small, ALL, axis=0, tiled=False)
    whole = [small[:, i * rows : (i + 1) * rows].reshape(-1).astype(F32) for i in range(8)]
    at = 8 * rows
    bias_fc = small[:, at : at + hidden_rows].reshape(n_seq, n_blk, n_uly, hidden_rows)
    bias_fc = lax.dynamic_slice(
        bias_fc, (here_seq, 0, here_uly, 0), (1, n_blk, 1, hidden_rows)
    ).reshape(ff_share).astype(F32)
    at += hidden_rows
    count = doc_lengths.size
    digits = small[:: n_blk * n_uly, at:].astype(F32).astype(jnp.int32)
    lengths = (16 * digits[:, :count] + digits[:, count:]).reshape(n_seq, *doc_lengths.shape)
    gain_one, shift_one, bias_q, bias_v, bias_out, gain_two, shift_two, bias_proj = whole
    mine = lambda v: lax.dynamic_slice(v, (here * share,), (share,))
    bias_q, bias_v = mine(bias_q), mine(bias_v)

    def to_planes(block):
        block = block.reshape(n_blk // sharing, held, sharing, part, width)
        block = block.transpose(0, 2, 1, 3, 4).reshape(n_blk, held * part, width)
        moved = lax.all_to_all(block, "blk", split_axis=0, concat_axis=0, tiled=True)
        return moved.reshape(n_rows, width)

    def from_planes(block):
        block = block.reshape(n_blk, held * part, width)
        moved = lax.all_to_all(block, "blk", split_axis=0, concat_axis=0, tiled=True)
        moved = moved.reshape(n_blk // sharing, sharing, held, part, width)
        return moved.transpose(0, 2, 1, 3, 4).reshape(seqs, tok, width)

    def columns_in(matrix, cols):
        moved = lax.all_to_all(matrix, PLANE, split_axis=1, concat_axis=0, tiled=True)
        moved = lax.all_gather(
            moved.reshape(plane * rows, cols), "blk", axis=0, tiled=True
        )
        moved = moved.reshape(n_blk, n_seq, n_uly * rows, cols)
        return moved.transpose(1, 0, 2, 3).reshape(width, cols)

    def columns_out(grad, cols):
        grad = grad.astype(BF).reshape(n_seq, n_blk, n_uly * rows, cols)
        grad = grad.transpose(1, 0, 2, 3).reshape(n_blk * plane * rows, cols)
        grad = lax.psum_scatter(grad, "blk", scatter_dimension=0, tiled=True)
        grad = grad.reshape(plane, rows, cols)
        return lax.all_to_all(grad, PLANE, split_axis=0, concat_axis=0, tiled=True)

    tokens = to_planes(inputs).astype(F32)
    qkv = jnp.stack([w.reshape(rows, plane, share) for w in (w_query, w_key, w_value)], axis=2)
    qkv = columns_in(qkv.reshape(rows, plane, 3 * share), 3 * share)
    out_part = lax.all_gather(w_out, "blk", axis=0, tiled=True)
    out_part = out_part.reshape(n_uly, n_blk // n_uly, rows, width)
    out_part = lax.all_to_all(out_part, "uly", split_axis=0, concat_axis=0, tiled=True)
    out_part = out_part.transpose(1, 0, 2, 3).reshape(share, width)
    fc = w_fc.reshape(rows, n_seq, n_blk, n_uly, hidden_rows).transpose(0, 1, 3, 2, 4)
    fc = columns_in(fc.reshape(rows, plane, ff_share), ff_share)
    proj = lax.all_gather(w_proj, "blk", axis=0, tiled=True)

    normed_value, norm_back_one = jax.vjp(layer_norm, tokens, gain_one, shift_one)
    normed = gather_plane(normed_value.astype(BF))
    grad_out = to_planes(cotangent)
    grad_all = gather_plane(grad_out)

    made = product(normed, qkv)
    queries = ((made[:, :share] + bias_q) * scale).astype(BF)
    keys = made[:, share : 2 * share].astype(BF)
    values = (made[:, 2 * share :] + bias_v).astype(BF)

    groups = [
        [g * sharing + i for i in range(sharing)] for g in range(n_blk // sharing)
    ]
    pairs = n_seq * held * heads // sharing
    length = n_blk * n_uly * tok

    def to_heads(matrix):
        matrix = matrix.reshape(n_seq, n_uly, n_blk, held, part, heads, HD)
        matrix = matrix.transpose(0, 3, 5, 2, 1, 4, 6)
        matrix = matrix.reshape(n_seq * held * heads, n_blk, n_uly, 1, part, HD)
        if sharing > 1:
            matrix = lax.all_to_all(
                matrix, "blk", split_axis=0, concat_axis=3, axis_index_groups=groups, tiled=True
            )
        return matrix.reshape(pairs, length, HD)

    def from_heads(matrix):
        matrix = matrix.reshape(pairs, n_blk, n_uly, sharing, part, HD)
        if sharing > 1:
            matrix = lax.all_to_all(
                matrix, "blk", split_axis=3, concat_axis=0, axis_index_groups=groups, tiled=True
            )
        matrix = matrix.reshape(n_seq, held, heads, n_blk, n_uly, part, HD)
        return matrix.transpose(0, 4, 3, 1, 5, 2, 6).reshape(plane * n_rows, share)

    hq, hk, hv = to_heads(queries), to_heads(keys), to_heads(values)
    turn = here_blk % sharing
    pair_at = turn * pairs + jnp.arange(pairs)
    seq_of = pair_at // (held * heads)
    held_of = (pair_at // heads) % held
    which = (here_blk // sharing) * held + held_of
    own_lengths = lengths[seq_of, which]
    first = own_lengths[:, 0:1]
    second = first + own_lengths[:, 1:2]
    position = jnp.arange(length, dtype=jnp.int32)[None]
    doc = (position >= first).astype(jnp.int32) + (position >= second).astype(jnp.int32)
    allowed = (doc[:, :, None] == doc[:, None, :]) & (
        position[:, None, :] <= position[:, :, None]
    )

    def head_forward(args):
        q, k, v, ok = args
        scores = jnp.where(ok, against(q, k), NEGATIVE)
        top = jnp.max(scores, axis=1, keepdims=True)
        powered = jnp.exp(scores - top)
        total = jnp.sum(powered, axis=1, keepdims=True)
        result = product(powered.astype(BF), v) / total
        return result, top + jnp.log(total)

    attended, log_total = lax.map(head_forward, (hq, hk, hv, allowed))
    attended_low = from_heads(attended.astype(BF))
    branch = scatter_plane(product(attended_low, out_part))
    hidden = tokens + branch.astype(F32) + bias_out
    normed_two_value, norm_back_two = jax.vjp(layer_norm, hidden, gain_two, shift_two)
    normed_two = gather_plane(normed_two_value.astype(BF))
    inner = product(normed_two, fc) + bias_fc
    gelu_value, gelu_back = jax.vjp(gelu_tanh, inner)
    active = gelu_value.astype(BF)
    fed = scatter_plane(product(active, proj))
    result = from_planes((hidden + fed.astype(F32) + bias_proj).astype(BF))

    grad_b_proj = jnp.sum(grad_out.astype(F32), axis=0)
    grad_inner = gelu_back(against(grad_all, proj))[0].astype(BF)
    grad_w_proj = lax.psum_scatter(
        transposed(active, grad_all).astype(BF), "blk", scatter_dimension=0, tiled=True
    ).astype(F32)
    grad_b_fc = jnp.sum(grad_inner.astype(F32), axis=0)
    grad_w_fc = columns_out(transposed(normed_two, grad_inner), ff_share)
    grad_w_fc = grad_w_fc.reshape(n_seq, n_uly, rows, n_blk, hidden_rows)
    grad_w_fc = grad_w_fc.transpose(2, 0, 3, 1, 4).reshape(rows, -1).astype(F32)
    grad_normed_two = scatter_plane(against(grad_inner, fc)).astype(F32)
    hidden_part, grad_ln2_gain, grad_ln2_shift = norm_back_two(grad_normed_two)
    grad_hidden = grad_out.astype(F32) + hidden_part
    grad_branch = grad_hidden.astype(BF)
    grad_b_out = jnp.sum(grad_branch.astype(F32), axis=0)
    branch_all = gather_plane(grad_branch)
    grad_w_out = transposed(attended_low, branch_all).astype(BF)
    grad_w_out = grad_w_out.reshape(n_blk // n_uly, n_uly, rows, width).transpose(1, 0, 2, 3)
    grad_w_out = lax.all_to_all(grad_w_out, "uly", split_axis=0, concat_axis=0, tiled=True)
    grad_w_out = lax.psum_scatter(
        grad_w_out.reshape(n_blk * rows, width), "blk", scatter_dimension=0, tiled=True
    ).astype(F32)
    grad_heads = to_heads(against(branch_all, out_part).astype(BF))

    def head_backward(args):
        q, k, v, ok, grad, kept, logs = args
        dots = jnp.sum(grad.astype(F32) * kept, axis=1, keepdims=True)
        scores = jnp.where(ok, against(q, k), NEGATIVE)
        chances = jnp.exp(scores - logs)
        grad_v = transposed(chances.astype(BF), grad)
        grad_scores = (chances * (against(grad, v) - dots)).astype(BF)
        grad_q = product(grad_scores, k)
        grad_k = transposed(grad_scores, q)
        return grad_q.astype(BF), grad_k.astype(BF), grad_v.astype(BF)

    backs = lax.map(head_backward, (hq, hk, hv, allowed, grad_heads, attended, log_total))
    query_back, key_back, value_back = (from_heads(b) for b in backs)
    grad_b_query = jnp.sum(query_back.astype(F32), axis=0) * scale
    grad_b_value = jnp.sum(value_back.astype(F32), axis=0)
    grad_normed = (
        against(query_back, qkv[:, :share]) * scale
        + against(key_back, qkv[:, share : 2 * share])
        + against(value_back, qkv[:, 2 * share :])
    )
    grad_qkv = jnp.concatenate(
        [
            transposed(normed, query_back) * scale,
            transposed(normed, key_back),
            transposed(normed, value_back),
        ],
        axis=1,
    )
    grad_qkv = columns_out(grad_qkv, 3 * share).reshape(plane, rows, 3, share)
    grad_qkv = grad_qkv.transpose(2, 1, 0, 3).reshape(3, rows, width).astype(F32)
    grad_normed = scatter_plane(grad_normed).astype(F32)
    token_part, grad_ln1_gain, grad_ln1_shift = norm_back_one(grad_normed)
    grad_inputs = from_planes((grad_hidden + token_part).astype(BF))

    def widened(vector):
        return lax.dynamic_update_slice(jnp.zeros((width,), F32), vector, (here * share,))

    parts = (
        grad_ln1_gain,
        grad_ln1_shift,
        widened(grad_b_query),
        widened(grad_b_value),
        grad_b_out,
        grad_ln2_gain,
        grad_ln2_shift,
        grad_b_proj,
    )
    wide_fc = lax.dynamic_update_slice(
        jnp.zeros((n_seq, n_blk, n_uly, hidden_rows), F32),
        grad_b_fc.reshape(1, n_blk, 1, hidden_rows),
        (here_seq, 0, here_uly, 0),
    ).reshape(devices, hidden_rows)
    sums = jnp.concatenate([p.reshape(devices, rows) for p in parts] + [wide_fc], axis=1)
    sums = lax.psum_scatter(
        sums.reshape(-1), ALL, scatter_dimension=0, tiled=True
    )
    each = [sums[i * rows : (i + 1) * rows] for i in range(8)]
    return (
        result,
        grad_inputs,
        each[0],
        each[1],
        grad_qkv[0],
        each[2],
        grad_qkv[1],
        grad_qkv[2],
        each[3],
        grad_w_out,
        each[4],
        each[5],
        each[6],
        grad_w_fc,
        sums[8 * rows :],
        grad_w_proj,
        each[7],
    )


def solution(mesh):
    tokens = P("seq", ("blk", "uly"), None)
    vector = P(ALL)
    matrix = P(ALL, None)
    return jax.shard_map(
        on_device,
        mesh=mesh,
        in_specs=(
            tokens, P("seq", None), vector, vector, matrix, vector, matrix, matrix, vector,
            matrix, vector, vector, vector, matrix, vector, matrix, vector, tokens,
        ),
        out_specs=(
            tokens, tokens, vector, vector, matrix, vector, matrix, matrix, vector,
            matrix, vector, vector, vector, matrix, vector, matrix, vector,
        ),
        check_vma=False,
    )
```

```python
import functools
import math

import jax
import jax.numpy as jnp
from jax import lax
from jax.experimental import pallas as pl
from jax.experimental.pallas import tpu as pltpu
from jax.sharding import PartitionSpec as P

HD = 128
EPS = 1e-05
NEGATIVE = -1e30
ALL = ("seq", "blk", "uly")
PLANE = ("seq", "uly")
BF = jnp.bfloat16
F32 = jnp.float32
MESH = pl.DeviceIdType.MESH
ANY = pl.BlockSpec(memory_space=pl.ANY)
VMEM = pl.BlockSpec(memory_space=pltpu.VMEM)
MIB = 2**20
CHUNK = 16
TILE = 512


def gelu_tanh(values):
    return jax.nn.gelu(values, approximate=True)


def product(left_side, right_side):
    return jnp.dot(left_side, right_side, preferred_element_type=F32)


def transposed(left_side, right_side):
    return lax.dot_general(
        left_side, right_side, (((0,), (0,)), ((), ())), preferred_element_type=F32
    )


def against(left_side, right_side):
    return lax.dot_general(
        left_side, right_side, (((1,), (1,)), ((), ())), preferred_element_type=F32
    )


def meet(peers):
    barrier = pltpu.get_barrier_semaphore()
    for peer in peers:
        pl.semaphore_signal(barrier, inc=1, device_id=peer, device_id_type=MESH)
    pl.semaphore_wait(barrier, len(peers))


def sender(send, recv):
    def copy(i, source, target, device):
        made = pltpu.make_async_remote_copy(
            src_ref=source,
            dst_ref=target,
            send_sem=send.at[i],
            recv_sem=recv.at[i],
            device_id=device,
            device_id_type=MESH,
        )
        made.start()
        return made

    return copy


def place():
    s, b, u = (lax.axis_index(a) for a in ALL)
    a, c = u // 2, u % 2
    beside = (s, b, 2 * (1 - a) + c)
    across = (1 - s, b, u)
    twin = (s, b, 2 * a + 1 - c)

    def blocks(core):
        own = 4 * s + 2 * a + core
        on_x = 4 * s + 2 * (1 - a) + core
        on_y = 4 * (1 - s) + 2 * a + core
        diagonal = 4 * (1 - s) + 2 * (1 - a) + core
        return diagonal, on_x, on_y, own

    return (s, b, u), (beside, across, twin), blocks(c), blocks(1 - c)


def spread(own, out, send, recv, local):
    _, (beside, across, twin), (diag, on_x, on_y, me), _ = place()
    half = own.shape[0] // 2
    parts = (pl.ds(0, half), pl.ds(half, half))
    copy = sender(send, recv)
    x0 = copy(0, own.at[parts[0]], out.at[me, parts[0]], beside)
    y1 = copy(1, own.at[parts[1]], out.at[me, parts[1]], across)
    x1 = copy(2, own.at[parts[1]], out.at[me, parts[1]], beside)
    y0 = copy(3, own.at[parts[0]], out.at[me, parts[0]], across)
    started = [x0, y1, x1, y0, copy(4, own, out.at[me], twin)]
    kept = pltpu.make_async_copy(own, out.at[me], local)
    kept.start()

    def pass_on(i, block, part, device):
        made = copy(i, out.at[block, parts[part]], out.at[block, parts[part]], device)
        started.append(made)
        return made

    x0.wait_recv()
    d0 = pass_on(5, on_x, 0, across)
    pass_on(6, on_x, 0, twin)
    y1.wait_recv()
    d1 = pass_on(7, on_y, 1, beside)
    pass_on(8, on_y, 1, twin)
    x1.wait_recv()
    pass_on(9, on_x, 1, twin)
    y0.wait_recv()
    pass_on(10, on_y, 0, twin)
    d0.wait_recv()
    pass_on(11, diag, 0, twin)
    d1.wait_recv()
    pass_on(12, diag, 1, twin)
    for i in (4, 6, 8, 9, 10, 11, 12):
        started[i].wait_recv()
    for made in started:
        made.wait_send()
    kept.wait()


SPREAD = 13


def collect(multiply, total, to_twin, from_twin, mine, in_x, in_y, send, recv):
    _, (beside, across, twin), here, other = place()
    rows, width = total.shape
    half = rows // 2
    parts = (pl.ds(0, half), pl.ds(half, half))
    copy = sender(send, recv)
    tiles = width // TILE

    def each_tile(body):
        def step(t, carry):
            body(pl.ds(pl.multiple_of(t * TILE, TILE), TILE))
            return carry

        lax.fori_loop(0, tiles, step, 0)

    to_twins = []
    for k in range(4):

        def first(cols, k=k):
            to_twin[k, :, cols] = multiply(other[k], cols).astype(BF)

        each_tile(first)
        to_twins.append(copy(k, to_twin.at[k], from_twin.at[k], twin))
    started = []
    for k in range(4):
        to_twins[k].wait_recv()
        if k < 3:

            def second(cols, k=k):
                term = multiply(here[k], cols) + from_twin[k, :, cols].astype(F32)
                mine[k, :, cols] = term.astype(BF)

            each_tile(second)
        else:

            def third(cols):
                total[:, cols] = multiply(here[3], cols) + from_twin[3, :, cols].astype(F32)

            each_tile(third)
        if k == 0:
            dx = copy(4, mine.at[0, parts[0]], in_x.at[0], beside)
            dy = copy(5, mine.at[0, parts[1]], in_y.at[0], across)
        elif k == 1:
            started.append(copy(6, mine.at[1, parts[0]], in_x.at[1], beside))
        elif k == 2:
            started.append(copy(7, mine.at[2, parts[1]], in_y.at[1], across))

    def add(k, part, arrived):
        def step(t, carry):
            at = pl.ds(pl.multiple_of(t * CHUNK, CHUNK), CHUNK)
            to = pl.ds(pl.multiple_of(part * half + t * CHUNK, CHUNK), CHUNK)
            mine[k, to] = (mine[k, to].astype(F32) + arrived[0, at].astype(F32)).astype(BF)
            return carry

        lax.fori_loop(0, half // CHUNK, step, 0)

    dy.wait_recv()
    add(1, 1, in_y)
    started.append(copy(8, mine.at[1, parts[1]], in_x.at[2], beside))
    dx.wait_recv()
    add(2, 0, in_x)
    started.append(copy(9, mine.at[2, parts[0]], in_y.at[2], across))
    for made in started:
        made.wait_recv()

    def finish(t, carry):
        at = pl.ds(pl.multiple_of(t * CHUNK, CHUNK), CHUNK)
        low = pl.ds(pl.multiple_of(half + t * CHUNK, CHUNK), CHUNK)
        total[at] += in_x[1, at].astype(F32) + in_y[2, at].astype(F32)
        total[low] += in_x[2, at].astype(F32) + in_y[1, at].astype(F32)
        return carry

    lax.fori_loop(0, half // CHUNK, finish, 0)
    for made in to_twins + started + [dx, dy]:
        made.wait_send()


COLLECT = 10


def collect_scratch(rows, width):
    return [
        pltpu.VMEM((rows, width), F32),
        pltpu.VMEM((4, rows, width), BF),
        pltpu.VMEM((4, rows, width), BF),
        pltpu.VMEM((3, rows, width), BF),
        pltpu.VMEM((3, rows // 2, width), BF),
        pltpu.VMEM((3, rows // 2, width), BF),
        pltpu.SemaphoreType.DMA((COLLECT,)),
        pltpu.SemaphoreType.DMA((COLLECT,)),
    ]


def reorder(values, outer, inner, lanes):
    return jnp.concatenate(
        [
            values[:, (o * inner + i) * lanes : (o * inner + i + 1) * lanes]
            for i in range(inner)
            for o in range(outer)
        ],
        axis=1,
    )


def norm_parts(values):
    average = jnp.mean(values, axis=-1, keepdims=True)
    centred = values - average
    variance = jnp.mean(centred * centred, axis=-1, keepdims=True)
    spread_back = lax.rsqrt(variance + EPS)
    return centred * spread_back, spread_back


def norm_back(grad, values, gain):
    unit, spread_back = norm_parts(values)
    scaled = grad * gain
    back = spread_back * (
        scaled
        - jnp.mean(scaled, axis=-1, keepdims=True)
        - unit * jnp.mean(scaled * unit, axis=-1, keepdims=True)
    )
    return back, grad * unit


def each_chunk(rows, body):
    def step(t, carry):
        body(pl.ds(pl.multiple_of(t * CHUNK, CHUNK), CHUNK))
        return carry

    lax.fori_loop(0, rows // CHUNK, step, 0)


def row_sum(values):
    return jnp.sum(values, axis=0, keepdims=True)


def return_rows(block, out, n_blk, send, recv, local):
    (s, b, u), _, _, _ = place()
    count = block.shape[0] // n_blk
    copy = sender(send, recv)
    started = []
    for j in range(1, n_blk):
        to = (b + j) % n_blk
        rows = pl.ds(pl.multiple_of(to * count, count), count)
        started.append(copy(j - 1, block.at[rows], out.at[b], (s, to, u)))
    rows = pl.ds(pl.multiple_of(b * count, count), count)
    kept = pltpu.make_async_copy(block.at[rows], out.at[b], local)
    kept.start()
    for made in started:
        made.wait()
    kept.wait()


def blk_peers(n_blk):
    (s, b, u), _, _, _ = place()
    return [(s, (b + j) % n_blk, u) for j in range(1, n_blk)]


def entry_kernel(
    n_blk, x_ref, qkv_ref, fc_ref, small_ref, tok, qkv, fc, small,
    blk_send, blk_recv, plane_send, plane_recv, local,
):
    (s, b, u), _, (_, _, _, me), _ = place()
    plane = qkv_ref.shape[0]
    n_uly = plane // 2
    others = [(me + j) % plane for j in range(1, plane)]
    friends = [(p // n_uly, b, p % n_uly) for p in others]
    column = blk_peers(n_blk)
    meet(friends + column)
    by_blk = sender(blk_send, blk_recv)
    by_plane = sender(plane_send, plane_recv)
    kept = [
        pltpu.make_async_copy(small_ref, small.at[me, b], local.at[0]),
        pltpu.make_async_copy(x_ref.at[b], tok.at[b], local.at[1]),
        pltpu.make_async_copy(qkv_ref.at[me], qkv.at[me], local.at[2]),
        pltpu.make_async_copy(fc_ref.at[me], fc.at[me], local.at[3]),
    ]
    for made in kept:
        made.start()
    vectors, started = [], []
    for j, peer in enumerate(column):
        vectors.append(by_blk(j, small_ref, small.at[me, b], peer))
    for j, peer in enumerate(column):
        started.append(by_blk(n_blk - 1 + j, x_ref.at[peer[1]], tok.at[b], peer))
    for j, (p, peer) in enumerate(zip(others, friends)):
        started.append(by_plane(3 * j, qkv_ref.at[p], qkv.at[me], peer))
        started.append(by_plane(3 * j + 1, fc_ref.at[p], fc.at[me], peer))
    kept[0].wait()
    for made in vectors:
        made.wait()
    for j, peer in enumerate(friends):
        started.append(by_plane(3 * j + 2, small.at[me], small.at[me], peer))
    for made in kept[1:] + started:
        made.wait()


def enter(x, qkv, fc, small, n_blk):
    plane = qkv.shape[0]
    return pl.pallas_call(
        functools.partial(entry_kernel, n_blk),
        name="enter",
        out_shape=(
            jax.ShapeDtypeStruct(x.shape, x.dtype),
            jax.ShapeDtypeStruct(qkv.shape, qkv.dtype),
            jax.ShapeDtypeStruct(fc.shape, fc.dtype),
            jax.ShapeDtypeStruct((plane, n_blk) + small.shape, small.dtype),
        ),
        in_specs=[ANY] * 4,
        out_specs=(ANY,) * 4,
        scratch_shapes=[
            pltpu.SemaphoreType.DMA((2 * (n_blk - 1),)),
            pltpu.SemaphoreType.DMA((2 * (n_blk - 1),)),
            pltpu.SemaphoreType.DMA((3 * (plane - 1),)),
            pltpu.SemaphoreType.DMA((3 * (plane - 1),)),
            pltpu.SemaphoreType.DMA((4,)),
        ],
        compiler_params=pltpu.CompilerParams(collective_id=0, has_side_effects=True),
        cost_estimate=pl.CostEstimate(flops=0, bytes_accessed=60 * MIB, transcendentals=0),
    )(x, qkv, fc, small)


def norm_kernel(order, tok, gain, shift, out, own, send, recv, local):
    _, near, _, _ = place()

    def chunk(at):
        unit, _ = norm_parts(tok[at].astype(F32))
        own[at] = reorder(unit * gain[...] + shift[...], *order).astype(BF)

    each_chunk(own.shape[0], chunk)
    meet(near)
    spread(own, out, send, recv, local)


def norm_gather(tok, gain, shift, plane, order):
    rows, width = tok.shape
    return pl.pallas_call(
        functools.partial(norm_kernel, order),
        name="norm_gather",
        out_shape=jax.ShapeDtypeStruct((plane, rows, width), BF),
        in_specs=[VMEM] * 3,
        out_specs=ANY,
        scratch_shapes=[
            pltpu.VMEM((rows, width), BF),
            pltpu.SemaphoreType.DMA((SPREAD,)),
            pltpu.SemaphoreType.DMA((SPREAD,)),
            pltpu.SemaphoreType.DMA,
        ],
        compiler_params=pltpu.CompilerParams(
            collective_id=1, has_side_effects=True, vmem_limit_bytes=16 * MIB
        ),
        cost_estimate=pl.CostEstimate(flops=0, bytes_accessed=100 * MIB, transcendentals=0),
    )(tok, gain, shift)


def cot_kernel(n_blk, x_ref, tok, out, send, recv, local, g_send, g_recv):
    (s, b, u), near, _, _ = place()
    column = blk_peers(n_blk)
    meet(list(near) + column)
    copy = sender(g_send, g_recv)
    count = x_ref.shape[1]
    own_rows = pl.ds(pl.multiple_of(b * count, count), count)
    started = [
        copy(j, x_ref.at[peer[1]], tok.at[own_rows], peer) for j, peer in enumerate(column)
    ]
    kept = pltpu.make_async_copy(x_ref.at[b], tok.at[own_rows], local)
    kept.start()
    kept.wait()
    for made in started:
        made.wait()
    spread(tok, out, send, recv, local)


def cot_gather(x, plane):
    n_blk, count, width = x.shape
    rows = n_blk * count
    return pl.pallas_call(
        functools.partial(cot_kernel, n_blk),
        name="cot_gather",
        out_shape=(
            jax.ShapeDtypeStruct((rows, width), BF),
            jax.ShapeDtypeStruct((plane, rows, width), BF),
        ),
        in_specs=[ANY],
        out_specs=(ANY, ANY),
        scratch_shapes=[
            pltpu.SemaphoreType.DMA((SPREAD,)),
            pltpu.SemaphoreType.DMA((SPREAD,)),
            pltpu.SemaphoreType.DMA,
            pltpu.SemaphoreType.DMA((n_blk - 1,)),
            pltpu.SemaphoreType.DMA((n_blk - 1,)),
        ],
        compiler_params=pltpu.CompilerParams(collective_id=2, has_side_effects=True),
        cost_estimate=pl.CostEstimate(flops=0, bytes_accessed=120 * MIB, transcendentals=0),
    )(x)


def rows_of(ref, block, rows):
    return ref[pl.ds(pl.multiple_of(block * rows, rows), rows), :]


def hidden_kernel(
    order, act, weight, tok, bias, gain, shift, hidden, out,
    total, to_twin, from_twin, mine, in_x, in_y, c_send, c_recv, own, send, recv, local,
):
    _, near, _, _ = place()
    rows = total.shape[0]
    meet(near)

    def multiply(block, cols):
        return product(rows_of(act, block, rows), weight[:, cols])

    collect(multiply, total, to_twin, from_twin, mine, in_x, in_y, c_send, c_recv)

    def chunk(at):
        values = total[at] + tok[at].astype(F32) + bias[...]
        hidden[at] = values
        unit, _ = norm_parts(values)
        own[at] = reorder(unit * gain[...] + shift[...], *order).astype(BF)

    each_chunk(rows, chunk)
    spread(own, out, send, recv, local)


def hidden_gather(act, weight, tok, bias, gain, shift, plane, order):
    rows, width = tok.shape
    return pl.pallas_call(
        functools.partial(hidden_kernel, order),
        name="hidden_gather",
        out_shape=(
            jax.ShapeDtypeStruct((rows, width), F32),
            jax.ShapeDtypeStruct((plane, rows, width), BF),
        ),
        in_specs=[VMEM] * 6,
        out_specs=(VMEM, ANY),
        scratch_shapes=collect_scratch(rows, width)
        + [
            pltpu.VMEM((rows, width), BF),
            pltpu.SemaphoreType.DMA((SPREAD,)),
            pltpu.SemaphoreType.DMA((SPREAD,)),
            pltpu.SemaphoreType.DMA,
        ],
        compiler_params=pltpu.CompilerParams(
            collective_id=3, has_side_effects=True, vmem_limit_bytes=40 * MIB
        ),
        cost_estimate=pl.CostEstimate(flops=0, bytes_accessed=250 * MIB, transcendentals=0),
    )(act, weight, tok, bias, gain, shift)


def branch_kernel(
    order, act, weight, hid, cot, gain, grad_hidden, sums, out,
    total, to_twin, from_twin, mine, in_x, in_y, c_send, c_recv, own, send, recv, local,
):
    _, near, _, _ = place()
    rows = total.shape[0]
    meet(near)

    def multiply(block, cols):
        return against(rows_of(act, block, rows), weight[cols, :])

    collect(multiply, total, to_twin, from_twin, mine, in_x, in_y, c_send, c_recv)
    sums[...] = jnp.zeros_like(sums)
    inner, outer, lanes = order[1], order[0], order[2]

    def chunk(at):
        grad = reorder(total[at], inner, outer, lanes)
        back, by_gain = norm_back(grad, hid[at], gain[...])
        passed = cot[at].astype(F32)
        back = back + passed
        grad_hidden[at] = back
        low = back.astype(BF)
        own[at] = low
        sums[0:1] += row_sum(by_gain)
        sums[1:2] += row_sum(grad)
        sums[2:3] += row_sum(low.astype(F32))
        sums[3:4] += row_sum(passed)

    each_chunk(rows, chunk)
    spread(own, out, send, recv, local)


def branch_gather(act, weight, hid, cot, gain, plane, order):
    rows, width = cot.shape
    return pl.pallas_call(
        functools.partial(branch_kernel, order),
        name="branch_gather",
        out_shape=(
            jax.ShapeDtypeStruct((rows, width), F32),
            jax.ShapeDtypeStruct((8, width), F32),
            jax.ShapeDtypeStruct((plane, rows, width), BF),
        ),
        in_specs=[VMEM] * 5,
        out_specs=(VMEM, VMEM, ANY),
        scratch_shapes=collect_scratch(rows, width)
        + [
            pltpu.VMEM((rows, width), BF),
            pltpu.SemaphoreType.DMA((SPREAD,)),
            pltpu.SemaphoreType.DMA((SPREAD,)),
            pltpu.SemaphoreType.DMA,
        ],
        compiler_params=pltpu.CompilerParams(
            collective_id=4, has_side_effects=True, vmem_limit_bytes=48 * MIB
        ),
        cost_estimate=pl.CostEstimate(flops=0, bytes_accessed=250 * MIB, transcendentals=0),
    )(act, weight, hid, cot, gain)


def result_kernel(
    n_blk, act, weight, hid, bias, out,
    total, to_twin, from_twin, mine, in_x, in_y, c_send, c_recv, own, send, recv, local,
):
    _, near, _, _ = place()
    rows = total.shape[0]
    meet(list(near) + blk_peers(n_blk))

    def multiply(block, cols):
        return product(rows_of(act, block, rows), weight[:, cols])

    collect(multiply, total, to_twin, from_twin, mine, in_x, in_y, c_send, c_recv)

    def chunk(at):
        own[at] = (total[at] + hid[at] + bias[...]).astype(BF)

    each_chunk(rows, chunk)
    return_rows(own, out, n_blk, send, recv, local)


def result_return(act, weight, hid, bias, n_blk):
    rows, width = hid.shape
    return pl.pallas_call(
        functools.partial(result_kernel, n_blk),
        name="result_return",
        out_shape=jax.ShapeDtypeStruct((n_blk, rows // n_blk, width), BF),
        in_specs=[VMEM] * 4,
        out_specs=ANY,
        scratch_shapes=collect_scratch(rows, width)
        + [
            pltpu.VMEM((rows, width), BF),
            pltpu.SemaphoreType.DMA((n_blk - 1,)),
            pltpu.SemaphoreType.DMA((n_blk - 1,)),
            pltpu.SemaphoreType.DMA,
        ],
        compiler_params=pltpu.CompilerParams(
            collective_id=5, has_side_effects=True, vmem_limit_bytes=40 * MIB
        ),
        cost_estimate=pl.CostEstimate(flops=0, bytes_accessed=180 * MIB, transcendentals=0),
    )(act, weight, hid, bias)


def inputs_kernel(
    n_blk, order, act, weight, tok, grad_hidden, gain, sums, out,
    total, to_twin, from_twin, mine, in_x, in_y, c_send, c_recv, own, send, recv, local,
):
    _, near, _, _ = place()
    rows = total.shape[0]
    meet(list(near) + blk_peers(n_blk))

    def multiply(block, cols):
        return against(rows_of(act, block, rows), weight[cols, :])

    collect(multiply, total, to_twin, from_twin, mine, in_x, in_y, c_send, c_recv)
    sums[...] = jnp.zeros_like(sums)
    inner, outer, lanes = order[1], order[0], order[2]

    def chunk(at):
        grad = reorder(total[at], inner, outer, lanes)
        back, by_gain = norm_back(grad, tok[at].astype(F32), gain[...])
        own[at] = (grad_hidden[at] + back).astype(BF)
        sums[0:1] += row_sum(by_gain)
        sums[1:2] += row_sum(grad)

    each_chunk(rows, chunk)
    return_rows(own, out, n_blk, send, recv, local)


def inputs_return(act, weight, tok, grad_hidden, gain, n_blk, order):
    rows, width = tok.shape
    return pl.pallas_call(
        functools.partial(inputs_kernel, n_blk, order),
        name="inputs_return",
        out_shape=(
            jax.ShapeDtypeStruct((8, width), F32),
            jax.ShapeDtypeStruct((n_blk, rows // n_blk, width), BF),
        ),
        in_specs=[VMEM] * 5,
        out_specs=(VMEM, ANY),
        scratch_shapes=collect_scratch(rows, width)
        + [
            pltpu.VMEM((rows, width), BF),
            pltpu.SemaphoreType.DMA((n_blk - 1,)),
            pltpu.SemaphoreType.DMA((n_blk - 1,)),
            pltpu.SemaphoreType.DMA,
        ],
        compiler_params=pltpu.CompilerParams(
            collective_id=6, has_side_effects=True, vmem_limit_bytes=40 * MIB
        ),
        cost_estimate=pl.CostEstimate(flops=0, bytes_accessed=180 * MIB, transcendentals=0),
    )(act, weight, tok, grad_hidden, gain)


def end_kernel(
    n_blk, qkv_ref, fc_ref, small_ref, qkv, fc, small, gathered, partial, arrived,
    blk_send, blk_recv, plane_send, plane_recv, local,
):
    (s, b, u), _, (_, _, _, me), _ = place()
    plane = qkv_ref.shape[0]
    n_uly = plane // 2
    others = [(me + j) % plane for j in range(1, plane)]
    friends = [(p // n_uly, b, p % n_uly) for p in others]
    column = blk_peers(n_blk)
    meet(friends + column)
    by_blk = sender(blk_send, blk_recv)
    by_plane = sender(plane_send, plane_recv)
    kept = [
        pltpu.make_async_copy(small_ref.at[me], gathered.at[me], local.at[0]),
        pltpu.make_async_copy(qkv_ref.at[me], qkv.at[me], local.at[1]),
        pltpu.make_async_copy(fc_ref.at[me], fc.at[me], local.at[2]),
    ]
    for made in kept:
        made.start()
    vectors, started = [], []
    for j, (p, peer) in enumerate(zip(others, friends)):
        vectors.append(by_plane(3 * j, small_ref.at[p], gathered.at[me], peer))
    for j, (p, peer) in enumerate(zip(others, friends)):
        started.append(by_plane(3 * j + 1, qkv_ref.at[p], qkv.at[me], peer))
        started.append(by_plane(3 * j + 2, fc_ref.at[p], fc.at[me], peer))
    kept[0].wait()
    for made in vectors:
        made.wait()
    partial[...] = jnp.sum(gathered[...], axis=0)
    own = pltpu.make_async_copy(partial.at[b], arrived.at[b], local.at[3])
    own.start()
    sent = [
        by_blk(j, partial.at[peer[1]], arrived.at[b], peer) for j, peer in enumerate(column)
    ]
    own.wait()
    for made in sent:
        made.wait()
    small[...] = jnp.sum(arrived[...], axis=0)
    for made in kept[1:] + started:
        made.wait()


def finish(qkv, fc, small):
    plane, n_blk = small.shape[:2]
    tail = small.shape[2:]
    return pl.pallas_call(
        functools.partial(end_kernel, n_blk),
        name="finish",
        out_shape=(
            jax.ShapeDtypeStruct(qkv.shape, qkv.dtype),
            jax.ShapeDtypeStruct(fc.shape, fc.dtype),
            jax.ShapeDtypeStruct(tail, small.dtype),
        ),
        in_specs=[ANY, ANY, ANY],
        out_specs=(ANY, ANY, VMEM),
        scratch_shapes=[
            pltpu.VMEM((plane, n_blk) + tail, F32),
            pltpu.VMEM((n_blk,) + tail, F32),
            pltpu.VMEM((n_blk,) + tail, F32),
            pltpu.SemaphoreType.DMA((n_blk - 1,)),
            pltpu.SemaphoreType.DMA((n_blk - 1,)),
            pltpu.SemaphoreType.DMA((3 * (plane - 1),)),
            pltpu.SemaphoreType.DMA((3 * (plane - 1),)),
            pltpu.SemaphoreType.DMA((4,)),
        ],
        compiler_params=pltpu.CompilerParams(
            collective_id=7, has_side_effects=True, vmem_limit_bytes=16 * MIB
        ),
        cost_estimate=pl.CostEstimate(flops=0, bytes_accessed=60 * MIB, transcendentals=0),
    )(qkv, fc, small)


def on_device(
    inputs,
    doc_lengths,
    ln1_gain,
    ln1_shift,
    w_query,
    b_query,
    w_key,
    w_value,
    b_value,
    w_out,
    b_out,
    ln2_gain,
    ln2_shift,
    w_fc,
    b_fc,
    w_proj,
    b_proj,
    cotangent,
):
    seqs, tok, width = inputs.shape
    n_seq, n_blk, n_uly = (lax.axis_size(a) for a in ALL)
    plane = n_seq * n_uly
    here_seq, here_blk, here_uly = (lax.axis_index(a) for a in ALL)
    here = here_seq * n_uly + here_uly
    scale = 1.0 / math.sqrt(HD)
    rows = w_query.shape[0]
    hidden_rows = w_proj.shape[0]
    share = width // plane
    heads = share // HD
    ff_share = hidden_rows * n_blk
    sharing = max(1, n_blk // seqs)
    held = seqs * sharing // n_blk
    part = tok // sharing
    n_rows = n_blk * held * part
    order = (n_seq, n_blk, n_uly * rows)

    def by_plane(block):
        block = block.reshape(n_blk // sharing, held, sharing, part, width)
        return block.transpose(0, 2, 1, 3, 4).reshape(n_blk, held * part, width)

    def from_plane(block):
        block = block.reshape(n_blk // sharing, sharing, held, part, width)
        return block.transpose(0, 2, 1, 3, 4).reshape(seqs, tok, width)

    vectors = (ln1_gain, ln1_shift, b_query, b_value, b_out, ln2_gain, ln2_shift, b_proj)
    small = jnp.concatenate(
        [v.astype(F32) for v in vectors + (b_fc, doc_lengths.reshape(-1))]
    )
    lanes = -(-small.size // 1024) * 8
    small = jnp.pad(small, (0, lanes * 128 - small.size)).reshape(lanes, 128)
    qkv = jnp.stack([w.reshape(rows, plane, share) for w in (w_query, w_key, w_value)], axis=2)
    qkv = qkv.transpose(1, 0, 2, 3).reshape(plane, rows, 3 * share)
    fc = w_fc.reshape(rows, n_seq, n_blk, n_uly, hidden_rows).transpose(1, 3, 0, 2, 4)
    fc = fc.reshape(plane, rows, ff_share)
    tokens, qkv, fc, small = enter(by_plane(inputs), qkv, fc, small, n_blk)
    tokens = tokens.reshape(n_rows, width)

    def over_blk(matrix):
        return lax.all_gather(matrix, "blk", axis=0, tiled=True)

    qkv = over_blk(qkv.reshape(plane * rows, 3 * share))
    out_part = over_blk(w_out).reshape(n_uly, n_blk // n_uly, rows, width)
    out_part = lax.all_to_all(out_part, "uly", split_axis=0, concat_axis=0, tiled=True)
    out_part = out_part.transpose(1, 0, 2, 3).reshape(share, width)
    fc = over_blk(fc.reshape(plane * rows, ff_share))
    proj = over_blk(w_proj)

    small = small.reshape(n_seq, n_uly, n_blk, lanes * 128)
    flat = small.transpose(0, 2, 1, 3).reshape(n_seq * n_blk * n_uly, lanes * 128)
    whole = [flat[:, i * rows : (i + 1) * rows].reshape(1, width) for i in range(8)]
    at = 8 * rows
    bias_fc = lax.dynamic_slice(
        small, (here_seq, here_uly, 0, at), (1, 1, n_blk, hidden_rows)
    ).reshape(1, ff_share)
    at += hidden_rows
    lengths = small[:, 0, 0, at : at + doc_lengths.size].astype(jnp.int32)
    lengths = lengths.reshape(n_seq, *doc_lengths.shape)
    gain_one, shift_one, bias_q, bias_v, bias_out, gain_two, shift_two, bias_proj = whole
    mine = lambda v: lax.dynamic_slice(v, (0, here * share), (1, share))
    bias_q, bias_v = mine(bias_q), mine(bias_v)

    normed = norm_gather(tokens, gain_one, shift_one, plane, order)
    normed = normed.reshape(plane * n_rows, width)
    grad_out, grad_all = cot_gather(by_plane(cotangent), plane)
    grad_all = grad_all.reshape(plane * n_rows, width)

    made = product(normed, qkv)
    queries = ((made[:, :share] + bias_q) * scale).astype(BF)
    keys = made[:, share : 2 * share].astype(BF)
    values = (made[:, 2 * share :] + bias_v).astype(BF)

    groups = [
        [g * sharing + i for i in range(sharing)] for g in range(n_blk // sharing)
    ]
    pairs = n_seq * held * heads // sharing
    length = n_blk * n_uly * tok

    def to_heads(matrix):
        matrix = matrix.reshape(n_seq, n_uly, n_blk, held, part, heads, HD)
        matrix = matrix.transpose(0, 3, 5, 2, 1, 4, 6)
        matrix = matrix.reshape(n_seq * held * heads, n_blk, n_uly, 1, part, HD)
        if sharing > 1:
            matrix = lax.all_to_all(
                matrix, "blk", split_axis=0, concat_axis=3, axis_index_groups=groups, tiled=True
            )
        return matrix.reshape(pairs, length, HD)

    def from_heads(matrix):
        matrix = matrix.reshape(pairs, n_blk, n_uly, sharing, part, HD)
        if sharing > 1:
            matrix = lax.all_to_all(
                matrix, "blk", split_axis=3, concat_axis=0, axis_index_groups=groups, tiled=True
            )
        matrix = matrix.reshape(n_seq, held, heads, n_blk, n_uly, part, HD)
        return matrix.transpose(0, 4, 3, 1, 5, 2, 6).reshape(plane * n_rows, share)

    hq, hk, hv = to_heads(queries), to_heads(keys), to_heads(values)
    turn = here_blk % sharing
    pair_at = turn * pairs + jnp.arange(pairs)
    seq_of = pair_at // (held * heads)
    held_of = (pair_at // heads) % held
    which = (here_blk // sharing) * held + held_of
    own_lengths = lengths[seq_of, which]
    first = own_lengths[:, 0:1]
    second = first + own_lengths[:, 1:2]
    position = jnp.arange(length, dtype=jnp.int32)[None]
    doc = (position >= first).astype(jnp.int32) + (position >= second).astype(jnp.int32)
    allowed = (doc[:, :, None] == doc[:, None, :]) & (
        position[:, None, :] <= position[:, :, None]
    )

    def head_forward(args):
        q, k, v, ok = args
        scores = jnp.where(ok, against(q, k), NEGATIVE)
        top = jnp.max(scores, axis=1, keepdims=True)
        powered = jnp.exp(scores - top)
        total = jnp.sum(powered, axis=1, keepdims=True)
        result = product(powered.astype(BF), v) / total
        return result, top + jnp.log(total)

    attended, log_total = lax.map(head_forward, (hq, hk, hv, allowed))
    attended_low = from_heads(attended.astype(BF))
    hidden, normed_two = hidden_gather(
        attended_low, out_part, tokens, bias_out, gain_two, shift_two, plane, order
    )
    normed_two = normed_two.reshape(plane * n_rows, width)
    inner = product(normed_two, fc) + bias_fc
    gelu_value, gelu_back = jax.vjp(gelu_tanh, inner)
    active = gelu_value.astype(BF)
    grad_w_proj = lax.psum_scatter(
        transposed(active, grad_all).astype(BF), "blk", scatter_dimension=0, tiled=True
    ).astype(F32)
    grad_inner = gelu_back(against(grad_all, proj))[0].astype(BF)
    grad_b_fc = jnp.sum(grad_inner.astype(F32), axis=0)
    grad_fc = lax.psum_scatter(
        transposed(normed_two, grad_inner).astype(BF), "blk", scatter_dimension=0, tiled=True
    )
    grad_hidden, sums_two, branch_all = branch_gather(
        grad_inner, fc, hidden, grad_out, gain_two, plane, order
    )
    branch_all = branch_all.reshape(plane * n_rows, width)
    result = result_return(active, proj, hidden, bias_proj, n_blk)
    grad_w_out = transposed(attended_low, branch_all).astype(BF)
    grad_w_out = grad_w_out.reshape(n_blk // n_uly, n_uly, rows, width).transpose(1, 0, 2, 3)
    grad_w_out = lax.all_to_all(grad_w_out, "uly", split_axis=0, concat_axis=0, tiled=True)
    grad_w_out = lax.psum_scatter(
        grad_w_out.reshape(n_blk * rows, width), "blk", scatter_dimension=0, tiled=True
    ).astype(F32)
    grad_heads = to_heads(against(branch_all, out_part).astype(BF))

    def head_backward(args):
        q, k, v, ok, grad, kept, logs = args
        dots = jnp.sum(grad.astype(F32) * kept, axis=1, keepdims=True)
        scores = jnp.where(ok, against(q, k), NEGATIVE)
        chances = jnp.exp(scores - logs)
        grad_v = transposed(chances.astype(BF), grad)
        grad_scores = (chances * (against(grad, v) - dots)).astype(BF)
        grad_q = product(grad_scores, k) * scale
        grad_k = transposed(grad_scores, q)
        return grad_q.astype(BF), grad_k.astype(BF), grad_v.astype(BF)

    backs = lax.map(head_backward, (hq, hk, hv, allowed, grad_heads, attended, log_total))
    backs = jnp.concatenate([from_heads(b) for b in backs], axis=1)
    grad_bias = jnp.sum(backs.astype(F32), axis=0)
    grad_qkv = lax.psum_scatter(
        transposed(normed, backs).astype(BF), "blk", scatter_dimension=0, tiled=True
    )
    sums_one, grad_inputs = inputs_return(
        backs, qkv, tokens, grad_hidden, gain_one, n_blk, order
    )

    def widened(vector):
        return lax.dynamic_update_slice(jnp.zeros((width,), F32), vector, (here * share,))

    parts = (
        sums_one[0],
        sums_one[1],
        widened(grad_bias[:share]),
        widened(grad_bias[2 * share :]),
        sums_two[2],
        sums_two[0],
        sums_two[1],
        sums_two[3],
    )
    wide_fc = lax.dynamic_update_slice(
        jnp.zeros((n_seq, n_blk, n_uly, hidden_rows), F32),
        grad_b_fc.reshape(1, n_blk, 1, hidden_rows),
        (here_seq, 0, here_uly, 0),
    )
    sums = jnp.concatenate(
        [p.reshape(n_seq, n_blk, n_uly, rows) for p in parts] + [wide_fc], axis=3
    )
    used = sums.shape[3]
    end_lanes = -(-used // 1024) * 8
    sums = jnp.pad(sums, ((0, 0),) * 3 + ((0, end_lanes * 128 - used),))
    sums = sums.transpose(0, 2, 1, 3).reshape(plane, n_blk, end_lanes, 128)
    grad_qkv, grad_fc, sums = finish(
        grad_qkv.reshape(plane, rows, 3 * share), grad_fc.reshape(plane, rows, ff_share), sums
    )
    sums = sums.reshape(-1)
    each = [sums[i * rows : (i + 1) * rows] for i in range(8)]
    grad_qkv = grad_qkv.reshape(plane, rows, 3, share).transpose(2, 1, 0, 3)
    grad_qkv = grad_qkv.reshape(3, rows, width).astype(F32)
    grad_fc = grad_fc.reshape(n_seq, n_uly, rows, n_blk, hidden_rows)
    grad_fc = grad_fc.transpose(2, 0, 3, 1, 4).reshape(rows, -1).astype(F32)
    return (
        from_plane(result),
        from_plane(grad_inputs),
        each[0],
        each[1],
        grad_qkv[0],
        each[2],
        grad_qkv[1],
        grad_qkv[2],
        each[3],
        grad_w_out,
        each[4],
        each[5],
        each[6],
        grad_fc,
        sums[8 * rows : used],
        grad_w_proj,
        each[7],
    )


def solution(mesh):
    tokens = P("seq", ("blk", "uly"), None)
    vector = P(ALL)
    matrix = P(ALL, None)
    return jax.shard_map(
        on_device,
        mesh=mesh,
        in_specs=(
            tokens, P("seq", None), vector, vector, matrix, vector, matrix, matrix, vector,
            matrix, vector, vector, vector, matrix, vector, matrix, vector, tokens,
        ),
        out_specs=(
            tokens, tokens, vector, vector, matrix, vector, matrix, matrix, vector,
            matrix, vector, vector, vector, matrix, vector, matrix, vector,
        ),
        check_vma=False,
    )
```

```python
import functools
import math

import jax
import jax.numpy as jnp
from jax import lax
from jax.experimental import pallas as pl
from jax.experimental.pallas import tpu as pltpu
from jax.sharding import PartitionSpec as P

HD = 128
EPS = 1e-05
NEGATIVE = -1e30
ALL = ("seq", "blk", "uly")
PLANE = ("seq", "uly")
BF = jnp.bfloat16
F32 = jnp.float32
MESH = pl.DeviceIdType.MESH
ANY = pl.BlockSpec(memory_space=pl.ANY)
VMEM = pl.BlockSpec(memory_space=pltpu.VMEM)
MIB = 2**20
CHUNK = 16
TILE = 512


def gelu_tanh(values):
    return jax.nn.gelu(values, approximate=True)


def product(left_side, right_side):
    return jnp.dot(left_side, right_side, preferred_element_type=F32)


def transposed(left_side, right_side):
    return lax.dot_general(
        left_side, right_side, (((0,), (0,)), ((), ())), preferred_element_type=F32
    )


def against(left_side, right_side):
    return lax.dot_general(
        left_side, right_side, (((1,), (1,)), ((), ())), preferred_element_type=F32
    )


def meet(peers):
    barrier = pltpu.get_barrier_semaphore()
    for peer in peers:
        pl.semaphore_signal(barrier, inc=1, device_id=peer, device_id_type=MESH)
    pl.semaphore_wait(barrier, len(peers))


def sender(send, recv):
    def copy(i, source, target, device):
        made = pltpu.make_async_remote_copy(
            src_ref=source,
            dst_ref=target,
            send_sem=send.at[i],
            recv_sem=recv.at[i],
            device_id=device,
            device_id_type=MESH,
        )
        made.start()
        return made

    return copy


def place():
    s, b, u = (lax.axis_index(a) for a in ALL)
    a, c = u // 2, u % 2
    beside = (s, b, 2 * (1 - a) + c)
    across = (1 - s, b, u)
    twin = (s, b, 2 * a + 1 - c)

    def blocks(core):
        own = 4 * s + 2 * a + core
        on_x = 4 * s + 2 * (1 - a) + core
        on_y = 4 * (1 - s) + 2 * a + core
        diagonal = 4 * (1 - s) + 2 * (1 - a) + core
        return diagonal, on_x, on_y, own

    return (s, b, u), (beside, across, twin), blocks(c), blocks(1 - c)


def spread(own, out, send, recv, local):
    _, (beside, across, twin), (diag, on_x, on_y, me), _ = place()
    half = own.shape[0] // 2
    parts = (pl.ds(0, half), pl.ds(half, half))
    copy = sender(send, recv)
    x0 = copy(0, own.at[parts[0]], out.at[me, parts[0]], beside)
    y1 = copy(1, own.at[parts[1]], out.at[me, parts[1]], across)
    x1 = copy(2, own.at[parts[1]], out.at[me, parts[1]], beside)
    y0 = copy(3, own.at[parts[0]], out.at[me, parts[0]], across)
    started = [x0, y1, x1, y0, copy(4, own, out.at[me], twin)]
    kept = pltpu.make_async_copy(own, out.at[me], local)
    kept.start()

    def pass_on(i, block, part, device):
        made = copy(i, out.at[block, parts[part]], out.at[block, parts[part]], device)
        started.append(made)
        return made

    yield
    x0.wait_recv()
    d0 = pass_on(5, on_x, 0, across)
    pass_on(6, on_x, 0, twin)
    y1.wait_recv()
    d1 = pass_on(7, on_y, 1, beside)
    pass_on(8, on_y, 1, twin)
    yield
    x1.wait_recv()
    pass_on(9, on_x, 1, twin)
    y0.wait_recv()
    pass_on(10, on_y, 0, twin)
    yield
    d0.wait_recv()
    pass_on(11, diag, 0, twin)
    d1.wait_recv()
    pass_on(12, diag, 1, twin)
    for i in (4, 6, 8, 9, 10, 11, 12):
        started[i].wait_recv()
    for made in started:
        made.wait_send()
    kept.wait()


def run(steps):
    for _ in steps:
        pass


SPREAD = 13


def collect(multiply, total, to_twin, from_twin, mine, in_x, in_y, send, recv):
    _, (beside, across, twin), here, other = place()
    rows, width = total.shape
    half = rows // 2
    parts = (pl.ds(0, half), pl.ds(half, half))
    copy = sender(send, recv)
    tiles = width // TILE

    def each_tile(body):
        def step(t, carry):
            body(pl.ds(pl.multiple_of(t * TILE, TILE), TILE))
            return carry

        lax.fori_loop(0, tiles, step, 0)

    to_twins = []

    def for_twin(k):
        def term(cols):
            to_twin[k, :, cols] = multiply(other[k], cols).astype(BF)

        each_tile(term)
        to_twins.append(copy(k, to_twin.at[k], from_twin.at[k], twin))

    def for_here(k):
        to_twins[k].wait_recv()

        def term(cols):
            both = multiply(here[k], cols) + from_twin[k, :, cols].astype(F32)
            if k < 3:
                mine[k, :, cols] = both.astype(BF)
            else:
                total[:, cols] = both

        each_tile(term)

    started = []
    for_twin(0)
    for_twin(1)
    for_here(0)
    dx = copy(4, mine.at[0, parts[0]], in_x.at[0], beside)
    dy = copy(5, mine.at[0, parts[1]], in_y.at[0], across)
    for_twin(2)
    for_here(1)
    started.append(copy(6, mine.at[1, parts[0]], in_x.at[1], beside))
    for_twin(3)
    for_here(2)
    started.append(copy(7, mine.at[2, parts[1]], in_y.at[1], across))
    for_here(3)
    yield

    def add(k, part, arrived):
        def step(t, carry):
            at = pl.ds(pl.multiple_of(t * CHUNK, CHUNK), CHUNK)
            to = pl.ds(pl.multiple_of(part * half + t * CHUNK, CHUNK), CHUNK)
            mine[k, to] = (mine[k, to].astype(F32) + arrived[0, at].astype(F32)).astype(BF)
            return carry

        lax.fori_loop(0, half // CHUNK, step, 0)

    dy.wait_recv()
    add(1, 1, in_y)
    started.append(copy(8, mine.at[1, parts[1]], in_x.at[2], beside))
    dx.wait_recv()
    add(2, 0, in_x)
    started.append(copy(9, mine.at[2, parts[0]], in_y.at[2], across))
    yield
    for made in started:
        made.wait_recv()

    def finish(t, carry):
        at = pl.ds(pl.multiple_of(t * CHUNK, CHUNK), CHUNK)
        low = pl.ds(pl.multiple_of(half + t * CHUNK, CHUNK), CHUNK)
        total[at] += in_x[1, at].astype(F32) + in_y[2, at].astype(F32)
        total[low] += in_x[2, at].astype(F32) + in_y[1, at].astype(F32)
        return carry

    lax.fori_loop(0, half // CHUNK, finish, 0)
    for made in to_twins + started + [dx, dy]:
        made.wait_send()


COLLECT = 10


def collect_scratch(rows, width):
    return [
        pltpu.VMEM((rows, width), F32),
        pltpu.VMEM((4, rows, width), BF),
        pltpu.VMEM((4, rows, width), BF),
        pltpu.VMEM((3, rows, width), BF),
        pltpu.VMEM((3, rows // 2, width), BF),
        pltpu.VMEM((3, rows // 2, width), BF),
        pltpu.SemaphoreType.DMA((COLLECT,)),
        pltpu.SemaphoreType.DMA((COLLECT,)),
    ]


def reorder(values, outer, inner, lanes):
    return jnp.concatenate(
        [
            values[:, (o * inner + i) * lanes : (o * inner + i + 1) * lanes]
            for i in range(inner)
            for o in range(outer)
        ],
        axis=1,
    )


def norm_parts(values):
    average = jnp.mean(values, axis=-1, keepdims=True)
    centred = values - average
    variance = jnp.mean(centred * centred, axis=-1, keepdims=True)
    spread_back = lax.rsqrt(variance + EPS)
    return centred * spread_back, spread_back


def norm_back(grad, values, gain):
    unit, spread_back = norm_parts(values)
    scaled = grad * gain
    back = spread_back * (
        scaled
        - jnp.mean(scaled, axis=-1, keepdims=True)
        - unit * jnp.mean(scaled * unit, axis=-1, keepdims=True)
    )
    return back, grad * unit


def each_chunk(rows, body):
    def step(t, carry):
        body(pl.ds(pl.multiple_of(t * CHUNK, CHUNK), CHUNK))
        return carry

    lax.fori_loop(0, rows // CHUNK, step, 0)


def row_sum(values):
    return jnp.sum(values, axis=0, keepdims=True)


def return_rows(block, out, n_blk, send, recv, local):
    (s, b, u), _, _, _ = place()
    count = block.shape[0] // n_blk
    copy = sender(send, recv)
    started = []
    for j in range(1, n_blk):
        to = (b + j) % n_blk
        rows = pl.ds(pl.multiple_of(to * count, count), count)
        started.append(copy(j - 1, block.at[rows], out.at[b], (s, to, u)))
    rows = pl.ds(pl.multiple_of(b * count, count), count)
    kept = pltpu.make_async_copy(block.at[rows], out.at[b], local)
    kept.start()
    for made in started:
        made.wait()
    kept.wait()


def blk_peers(n_blk):
    (s, b, u), _, _, _ = place()
    return [(s, (b + j) % n_blk, u) for j in range(1, n_blk)]


def entry_kernel(
    n_blk, x_ref, qkv_ref, fc_ref, small_ref, tok, qkv, fc, small,
    blk_send, blk_recv, plane_send, plane_recv, local,
):
    (s, b, u), _, (_, _, _, me), _ = place()
    plane = qkv_ref.shape[0]
    n_uly = plane // 2
    others = [(me + j) % plane for j in range(1, plane)]
    friends = [(p // n_uly, b, p % n_uly) for p in others]
    column = blk_peers(n_blk)
    meet(friends + column)
    by_blk = sender(blk_send, blk_recv)
    by_plane = sender(plane_send, plane_recv)
    kept = [
        pltpu.make_async_copy(small_ref, small.at[me, b], local.at[0]),
        pltpu.make_async_copy(x_ref.at[b], tok.at[b], local.at[1]),
        pltpu.make_async_copy(qkv_ref.at[me], qkv.at[me], local.at[2]),
        pltpu.make_async_copy(fc_ref.at[me], fc.at[me], local.at[3]),
    ]
    for made in kept:
        made.start()
    vectors, started = [], []
    for j, peer in enumerate(column):
        vectors.append(by_blk(j, small_ref, small.at[me, b], peer))
    for j, peer in enumerate(column):
        started.append(by_blk(n_blk - 1 + j, x_ref.at[peer[1]], tok.at[b], peer))
    for j, (p, peer) in enumerate(zip(others, friends)):
        started.append(by_plane(3 * j, qkv_ref.at[p], qkv.at[me], peer))
        started.append(by_plane(3 * j + 1, fc_ref.at[p], fc.at[me], peer))
    kept[0].wait()
    for made in vectors:
        made.wait()
    for j, peer in enumerate(friends):
        started.append(by_plane(3 * j + 2, small.at[me], small.at[me], peer))
    for made in kept[1:] + started:
        made.wait()


def enter(x, qkv, fc, small, n_blk):
    plane = qkv.shape[0]
    return pl.pallas_call(
        functools.partial(entry_kernel, n_blk),
        name="enter",
        out_shape=(
            jax.ShapeDtypeStruct(x.shape, x.dtype),
            jax.ShapeDtypeStruct(qkv.shape, qkv.dtype),
            jax.ShapeDtypeStruct(fc.shape, fc.dtype),
            jax.ShapeDtypeStruct((plane, n_blk) + small.shape, small.dtype),
        ),
        in_specs=[ANY] * 4,
        out_specs=(ANY,) * 4,
        scratch_shapes=[
            pltpu.SemaphoreType.DMA((2 * (n_blk - 1),)),
            pltpu.SemaphoreType.DMA((2 * (n_blk - 1),)),
            pltpu.SemaphoreType.DMA((3 * (plane - 1),)),
            pltpu.SemaphoreType.DMA((3 * (plane - 1),)),
            pltpu.SemaphoreType.DMA((4,)),
        ],
        compiler_params=pltpu.CompilerParams(collective_id=0, has_side_effects=True),
        cost_estimate=pl.CostEstimate(flops=0, bytes_accessed=60 * MIB, transcendentals=0),
    )(x, qkv, fc, small)


def norm_kernel(order, tok, gain, shift, out, own, send, recv, local):
    _, near, _, _ = place()

    def chunk(at):
        unit, _ = norm_parts(tok[at].astype(F32))
        own[at] = reorder(unit * gain[...] + shift[...], *order).astype(BF)

    each_chunk(own.shape[0], chunk)
    meet(near)
    run(spread(own, out, send, recv, local))


def norm_gather(tok, gain, shift, plane, order):
    rows, width = tok.shape
    return pl.pallas_call(
        functools.partial(norm_kernel, order),
        name="norm_gather",
        out_shape=jax.ShapeDtypeStruct((plane, rows, width), BF),
        in_specs=[VMEM] * 3,
        out_specs=ANY,
        scratch_shapes=[
            pltpu.VMEM((rows, width), BF),
            pltpu.SemaphoreType.DMA((SPREAD,)),
            pltpu.SemaphoreType.DMA((SPREAD,)),
            pltpu.SemaphoreType.DMA,
        ],
        compiler_params=pltpu.CompilerParams(
            collective_id=1, has_side_effects=True, vmem_limit_bytes=16 * MIB
        ),
        cost_estimate=pl.CostEstimate(flops=0, bytes_accessed=100 * MIB, transcendentals=0),
    )(tok, gain, shift)


BLOCK = 256


def document_start(bounds, s, position):
    first, second = bounds[2 * s], bounds[2 * s + 1]
    return jnp.where(position >= second, second, jnp.where(position >= first, first, 0))


def chunks_of(layout):
    n_seq, n_uly, n_blk, part, _ = layout
    for s in range(n_seq):
        for b in range(n_blk):
            for u in range(n_uly):
                yield ((s * n_uly + u) * n_blk + b) * part, s, (b * n_uly + u) * part


def attend_kernel(
    layout, bounds, qkv, cot, low, natural, attended, logs, out, send, recv, local,
):
    _, near, _, _ = place()
    _, _, _, part, heads = layout
    meet(near)
    moving = spread(cot, out, send, recv, local)
    next(moving)
    share = heads * HD
    pairs, length = natural.shape[1:3]
    for row, s, position in chunks_of(layout):
        for kind in range(3):
            for h in range(heads):
                lane = kind * share + h * HD
                natural[kind, s * heads + h, position : position + part] = qkv[
                    row : row + part, lane : lane + HD
                ]

    def pair(p, carry):
        for start in range(0, length, BLOCK):
            stop = start + BLOCK
            scores = against(natural[0, p, start:stop], natural[1, p, :stop])
            row = start + lax.broadcasted_iota(jnp.int32, (BLOCK, 1), 0)
            key = lax.broadcasted_iota(jnp.int32, (BLOCK, stop), 1)
            allowed = (key >= document_start(bounds, p // heads, row)) & (key <= row)
            scores = jnp.where(allowed, scores, NEGATIVE)
            top = jnp.max(scores, axis=1, keepdims=True)
            powered = jnp.exp(scores - top)
            total = jnp.sum(powered, axis=1, keepdims=True)
            made = product(powered.astype(BF), natural[2, p, :stop])
            attended[p, start:stop] = made / total
            log_total = jnp.broadcast_to(top + jnp.log(total), (BLOCK, HD))
            logs[p, :, start:stop] = log_total.T[:8]
        return carry

    cut = (pairs + 1) // 2
    lax.fori_loop(0, cut, pair, 0)
    next(moving)
    lax.fori_loop(cut, pairs, pair, 0)
    next(moving)
    for row, s, position in chunks_of(layout):
        for h in range(heads):
            low[row : row + part, h * HD : (h + 1) * HD] = attended[
                s * heads + h, position : position + part
            ].astype(BF)
    run(moving)


def attend(bounds, qkv, cot, plane, layout):
    n_seq, n_uly, n_blk, part, heads = layout
    rows, width = cot.shape
    pairs, length = n_seq * heads, n_uly * n_blk * part
    return pl.pallas_call(
        functools.partial(attend_kernel, layout),
        name="attend",
        out_shape=(
            jax.ShapeDtypeStruct((qkv.shape[0], heads * HD), BF),
            jax.ShapeDtypeStruct((3, pairs, length, HD), BF),
            jax.ShapeDtypeStruct((pairs, length, HD), F32),
            jax.ShapeDtypeStruct((pairs, 8, length), F32),
            jax.ShapeDtypeStruct((plane, rows, width), BF),
        ),
        in_specs=[pl.BlockSpec(memory_space=pltpu.SMEM), VMEM, ANY],
        out_specs=(VMEM, VMEM, VMEM, VMEM, ANY),
        scratch_shapes=[
            pltpu.SemaphoreType.DMA((SPREAD,)),
            pltpu.SemaphoreType.DMA((SPREAD,)),
            pltpu.SemaphoreType.DMA,
        ],
        compiler_params=pltpu.CompilerParams(
            collective_id=2, has_side_effects=True, vmem_limit_bytes=40 * MIB
        ),
        cost_estimate=pl.CostEstimate(flops=0, bytes_accessed=150 * MIB, transcendentals=0),
    )(bounds, qkv, cot)


def attend_back_kernel(
    layout, scale, bounds, grad, natural, attended, logs, act, weight, hid, bias, back, out,
    grads, grads_back, key_grad, value_grad,
    total, to_twin, from_twin, mine, in_x, in_y, c_send, c_recv,
):
    _, near, _, _ = place()
    rows = total.shape[0]
    _, _, _, part, heads = layout
    share = heads * HD
    meet(near)

    def multiply(block, cols):
        return product(rows_of(act, block, rows), weight[:, cols])

    moving = collect(multiply, total, to_twin, from_twin, mine, in_x, in_y, c_send, c_recv)
    next(moving)
    pairs, length = natural.shape[1:3]
    for row, s, position in chunks_of(layout):
        for h in range(heads):
            grads[s * heads + h, position : position + part] = grad[
                row : row + part, h * HD : (h + 1) * HD
            ]

    def pair(p, carry):
        for start in reversed(range(0, length, BLOCK)):
            stop = start + BLOCK
            query, key, value = (
                natural[0, p, start:stop], natural[1, p, :stop], natural[2, p, :stop]
            )
            above = grads[p, start:stop]
            row = start + lax.broadcasted_iota(jnp.int32, (1, BLOCK), 1)
            at = lax.broadcasted_iota(jnp.int32, (stop, BLOCK), 0)
            allowed = (at >= document_start(bounds, p // heads, row)) & (at <= row)
            scores = jnp.where(allowed, against(key, query), NEGATIVE)
            chances = jnp.exp(scores - logs[p, 0:1, start:stop])
            dots = (above.astype(F32) * attended[p, start:stop]).T
            dots = jnp.sum(dots, axis=0, keepdims=True)
            by_value = product(chances.astype(BF), above)
            scored = (chances * (against(value, above) - dots)).astype(BF)
            by_key = product(scored, query)
            grads_back[p, start:stop] = (transposed(scored, key) * scale).astype(BF)
            if stop == length:
                key_grad[...] = by_key
                value_grad[...] = by_value
            else:
                key_grad[:stop] += by_key
                value_grad[:stop] += by_value
        grads_back[pairs + p] = key_grad[...].astype(BF)
        grads_back[2 * pairs + p] = value_grad[...].astype(BF)
        return carry

    cut = (pairs + 1) // 2
    lax.fori_loop(0, cut, pair, 0)
    next(moving)
    lax.fori_loop(cut, pairs, pair, 0)
    for row, s, position in chunks_of(layout):
        for kind in range(3):
            for h in range(heads):
                lane = kind * share + h * HD
                back[row : row + part, lane : lane + HD] = grads_back[
                    kind * pairs + s * heads + h, position : position + part
                ]
    run(moving)

    def chunk(at):
        out[at] = (total[at] + hid[at] + bias[...]).astype(BF)

    each_chunk(rows, chunk)


def attend_back(bounds, grad, natural, attended, logs, act, weight, hid, bias, layout, scale):
    rows, width = hid.shape
    pairs, length = natural.shape[1:3]
    return pl.pallas_call(
        functools.partial(attend_back_kernel, layout, scale),
        name="attend_back",
        out_shape=(
            jax.ShapeDtypeStruct((grad.shape[0], 3 * grad.shape[1]), BF),
            jax.ShapeDtypeStruct((rows, width), BF),
        ),
        in_specs=[pl.BlockSpec(memory_space=pltpu.SMEM)] + [VMEM] * 8,
        out_specs=(VMEM, VMEM),
        scratch_shapes=[
            pltpu.VMEM((pairs, length, HD), BF),
            pltpu.VMEM((3 * pairs, length, HD), BF),
            pltpu.VMEM((length, HD), F32),
            pltpu.VMEM((length, HD), F32),
        ]
        + collect_scratch(rows, width),
        compiler_params=pltpu.CompilerParams(
            collective_id=5, has_side_effects=True, vmem_limit_bytes=60 * MIB
        ),
        cost_estimate=pl.CostEstimate(flops=0, bytes_accessed=200 * MIB, transcendentals=0),
    )(bounds, grad, natural, attended, logs, act, weight, hid, bias)


def rows_of(ref, block, rows):
    return ref[pl.ds(pl.multiple_of(block * rows, rows), rows), :]


def hidden_kernel(
    order, act, weight, tok, bias, gain, shift, hidden, out,
    total, to_twin, from_twin, mine, in_x, in_y, c_send, c_recv, own, send, recv, local,
):
    _, near, _, _ = place()
    rows = total.shape[0]
    meet(near)

    def multiply(block, cols):
        return product(rows_of(act, block, rows), weight[:, cols])

    run(collect(multiply, total, to_twin, from_twin, mine, in_x, in_y, c_send, c_recv))

    def chunk(at):
        values = total[at] + tok[at].astype(F32) + bias[...]
        hidden[at] = values
        unit, _ = norm_parts(values)
        own[at] = reorder(unit * gain[...] + shift[...], *order).astype(BF)

    each_chunk(rows, chunk)
    run(spread(own, out, send, recv, local))


def hidden_gather(act, weight, tok, bias, gain, shift, plane, order):
    rows, width = tok.shape
    return pl.pallas_call(
        functools.partial(hidden_kernel, order),
        name="hidden_gather",
        out_shape=(
            jax.ShapeDtypeStruct((rows, width), F32),
            jax.ShapeDtypeStruct((plane, rows, width), BF),
        ),
        in_specs=[VMEM] * 6,
        out_specs=(VMEM, ANY),
        scratch_shapes=collect_scratch(rows, width)
        + [
            pltpu.VMEM((rows, width), BF),
            pltpu.SemaphoreType.DMA((SPREAD,)),
            pltpu.SemaphoreType.DMA((SPREAD,)),
            pltpu.SemaphoreType.DMA,
        ],
        compiler_params=pltpu.CompilerParams(
            collective_id=3, has_side_effects=True, vmem_limit_bytes=40 * MIB
        ),
        cost_estimate=pl.CostEstimate(flops=0, bytes_accessed=250 * MIB, transcendentals=0),
    )(act, weight, tok, bias, gain, shift)


def branch_kernel(
    order, act, weight, hid, cot, gain, grad_hidden, sums, out,
    total, to_twin, from_twin, mine, in_x, in_y, c_send, c_recv, own, send, recv, local,
):
    _, near, _, _ = place()
    rows = total.shape[0]
    meet(near)

    def multiply(block, cols):
        return against(rows_of(act, block, rows), weight[cols, :])

    run(collect(multiply, total, to_twin, from_twin, mine, in_x, in_y, c_send, c_recv))
    sums[...] = jnp.zeros_like(sums)
    inner, outer, lanes = order[1], order[0], order[2]

    def chunk(at):
        grad = reorder(total[at], inner, outer, lanes)
        back, by_gain = norm_back(grad, hid[at], gain[...])
        passed = cot[at].astype(F32)
        back = back + passed
        grad_hidden[at] = back
        low = back.astype(BF)
        own[at] = low
        sums[0:1] += row_sum(by_gain)
        sums[1:2] += row_sum(grad)
        sums[2:3] += row_sum(low.astype(F32))
        sums[3:4] += row_sum(passed)

    each_chunk(rows, chunk)
    run(spread(own, out, send, recv, local))


def branch_gather(act, weight, hid, cot, gain, plane, order):
    rows, width = cot.shape
    return pl.pallas_call(
        functools.partial(branch_kernel, order),
        name="branch_gather",
        out_shape=(
            jax.ShapeDtypeStruct((rows, width), F32),
            jax.ShapeDtypeStruct((8, width), F32),
            jax.ShapeDtypeStruct((plane, rows, width), BF),
        ),
        in_specs=[VMEM] * 5,
        out_specs=(VMEM, VMEM, ANY),
        scratch_shapes=collect_scratch(rows, width)
        + [
            pltpu.VMEM((rows, width), BF),
            pltpu.SemaphoreType.DMA((SPREAD,)),
            pltpu.SemaphoreType.DMA((SPREAD,)),
            pltpu.SemaphoreType.DMA,
        ],
        compiler_params=pltpu.CompilerParams(
            collective_id=4, has_side_effects=True, vmem_limit_bytes=48 * MIB
        ),
        cost_estimate=pl.CostEstimate(flops=0, bytes_accessed=250 * MIB, transcendentals=0),
    )(act, weight, hid, cot, gain)


def inputs_kernel(
    n_blk, order, act, weight, tok, grad_hidden, gain, sums, out,
    total, to_twin, from_twin, mine, in_x, in_y, c_send, c_recv, own, send, recv, local,
):
    _, near, _, _ = place()
    rows = total.shape[0]
    meet(list(near) + blk_peers(n_blk))

    def multiply(block, cols):
        return against(rows_of(act, block, rows), weight[cols, :])

    run(collect(multiply, total, to_twin, from_twin, mine, in_x, in_y, c_send, c_recv))
    sums[...] = jnp.zeros_like(sums)
    inner, outer, lanes = order[1], order[0], order[2]

    def chunk(at):
        grad = reorder(total[at], inner, outer, lanes)
        back, by_gain = norm_back(grad, tok[at].astype(F32), gain[...])
        own[at] = (grad_hidden[at] + back).astype(BF)
        sums[0:1] += row_sum(by_gain)
        sums[1:2] += row_sum(grad)

    each_chunk(rows, chunk)
    return_rows(own, out, n_blk, send, recv, local)


def inputs_return(act, weight, tok, grad_hidden, gain, n_blk, order):
    rows, width = tok.shape
    return pl.pallas_call(
        functools.partial(inputs_kernel, n_blk, order),
        name="inputs_return",
        out_shape=(
            jax.ShapeDtypeStruct((8, width), F32),
            jax.ShapeDtypeStruct((n_blk, rows // n_blk, width), BF),
        ),
        in_specs=[VMEM] * 5,
        out_specs=(VMEM, ANY),
        scratch_shapes=collect_scratch(rows, width)
        + [
            pltpu.VMEM((rows, width), BF),
            pltpu.SemaphoreType.DMA((n_blk - 1,)),
            pltpu.SemaphoreType.DMA((n_blk - 1,)),
            pltpu.SemaphoreType.DMA,
        ],
        compiler_params=pltpu.CompilerParams(
            collective_id=6, has_side_effects=True, vmem_limit_bytes=40 * MIB
        ),
        cost_estimate=pl.CostEstimate(flops=0, bytes_accessed=180 * MIB, transcendentals=0),
    )(act, weight, tok, grad_hidden, gain)


def end_kernel(
    n_blk, qkv_ref, fc_ref, small_ref, qkv, fc, small, gathered, partial, arrived,
    blk_send, blk_recv, plane_send, plane_recv, local,
):
    (s, b, u), _, (_, _, _, me), _ = place()
    plane = qkv_ref.shape[0]
    n_uly = plane // 2
    others = [(me + j) % plane for j in range(1, plane)]
    friends = [(p // n_uly, b, p % n_uly) for p in others]
    column = blk_peers(n_blk)
    meet(friends + column)
    by_blk = sender(blk_send, blk_recv)
    by_plane = sender(plane_send, plane_recv)
    kept = [
        pltpu.make_async_copy(small_ref.at[me], gathered.at[me], local.at[0]),
        pltpu.make_async_copy(qkv_ref.at[me], qkv.at[me], local.at[1]),
        pltpu.make_async_copy(fc_ref.at[me], fc.at[me], local.at[2]),
    ]
    for made in kept:
        made.start()
    vectors, started = [], []
    for j, (p, peer) in enumerate(zip(others, friends)):
        vectors.append(by_plane(3 * j, small_ref.at[p], gathered.at[me], peer))
    for j, (p, peer) in enumerate(zip(others, friends)):
        started.append(by_plane(3 * j + 1, qkv_ref.at[p], qkv.at[me], peer))
        started.append(by_plane(3 * j + 2, fc_ref.at[p], fc.at[me], peer))
    kept[0].wait()
    for made in vectors:
        made.wait()
    partial[...] = jnp.sum(gathered[...], axis=0)
    own = pltpu.make_async_copy(partial.at[b], arrived.at[b], local.at[3])
    own.start()
    sent = [
        by_blk(j, partial.at[peer[1]], arrived.at[b], peer) for j, peer in enumerate(column)
    ]
    own.wait()
    for made in sent:
        made.wait()
    small[...] = jnp.sum(arrived[...], axis=0)
    for made in kept[1:] + started:
        made.wait()


def finish(qkv, fc, small):
    plane, n_blk = small.shape[:2]
    tail = small.shape[2:]
    return pl.pallas_call(
        functools.partial(end_kernel, n_blk),
        name="finish",
        out_shape=(
            jax.ShapeDtypeStruct(qkv.shape, qkv.dtype),
            jax.ShapeDtypeStruct(fc.shape, fc.dtype),
            jax.ShapeDtypeStruct(tail, small.dtype),
        ),
        in_specs=[ANY, ANY, ANY],
        out_specs=(ANY, ANY, VMEM),
        scratch_shapes=[
            pltpu.VMEM((plane, n_blk) + tail, F32),
            pltpu.VMEM((n_blk,) + tail, F32),
            pltpu.VMEM((n_blk,) + tail, F32),
            pltpu.SemaphoreType.DMA((n_blk - 1,)),
            pltpu.SemaphoreType.DMA((n_blk - 1,)),
            pltpu.SemaphoreType.DMA((3 * (plane - 1),)),
            pltpu.SemaphoreType.DMA((3 * (plane - 1),)),
            pltpu.SemaphoreType.DMA((4,)),
        ],
        compiler_params=pltpu.CompilerParams(
            collective_id=7, has_side_effects=True, vmem_limit_bytes=16 * MIB
        ),
        cost_estimate=pl.CostEstimate(flops=0, bytes_accessed=60 * MIB, transcendentals=0),
    )(qkv, fc, small)


def on_device(
    inputs,
    doc_lengths,
    ln1_gain,
    ln1_shift,
    w_query,
    b_query,
    w_key,
    w_value,
    b_value,
    w_out,
    b_out,
    ln2_gain,
    ln2_shift,
    w_fc,
    b_fc,
    w_proj,
    b_proj,
    cotangent,
):
    seqs, tok, width = inputs.shape
    n_seq, n_blk, n_uly = (lax.axis_size(a) for a in ALL)
    plane = n_seq * n_uly
    here_seq, here_blk, here_uly = (lax.axis_index(a) for a in ALL)
    here = here_seq * n_uly + here_uly
    scale = 1.0 / math.sqrt(HD)
    rows = w_query.shape[0]
    hidden_rows = w_proj.shape[0]
    share = width // plane
    heads = share // HD
    ff_share = hidden_rows * n_blk
    sharing = max(1, n_blk // seqs)
    held = seqs * sharing // n_blk
    part = tok // sharing
    n_rows = n_blk * held * part
    order = (n_seq, n_blk, n_uly * rows)

    def by_plane(block):
        block = block.reshape(n_blk // sharing, held, sharing, part, width)
        return block.transpose(0, 2, 1, 3, 4).reshape(n_blk, held * part, width)

    def from_plane(block):
        block = block.reshape(n_blk // sharing, sharing, held, part, width)
        return block.transpose(0, 2, 1, 3, 4).reshape(seqs, tok, width)

    def over(block):
        return lax.all_to_all(block, "blk", split_axis=0, concat_axis=0, tiled=True)

    vectors = (ln1_gain, ln1_shift, b_query, b_value, b_out, ln2_gain, ln2_shift, b_proj)
    small = jnp.concatenate(
        [v.astype(F32) for v in vectors + (b_fc, doc_lengths.reshape(-1))]
    )
    lanes = -(-small.size // 1024) * 8
    small = jnp.pad(small, (0, lanes * 128 - small.size)).reshape(lanes, 128)
    qkv = jnp.stack([w.reshape(rows, plane, share) for w in (w_query, w_key, w_value)], axis=2)
    qkv = qkv.transpose(1, 0, 2, 3).reshape(plane, rows, 3 * share)
    fc = w_fc.reshape(rows, n_seq, n_blk, n_uly, hidden_rows).transpose(1, 3, 0, 2, 4)
    fc = fc.reshape(plane, rows, ff_share)
    tokens, qkv, fc, small = enter(by_plane(inputs), qkv, fc, small, n_blk)
    tokens = tokens.reshape(n_rows, width)

    def over_blk(matrix):
        return lax.all_gather(matrix, "blk", axis=0, tiled=True)

    qkv = over_blk(qkv.reshape(plane * rows, 3 * share))
    out_part = over_blk(w_out).reshape(n_uly, n_blk // n_uly, rows, width)
    out_part = lax.all_to_all(out_part, "uly", split_axis=0, concat_axis=0, tiled=True)
    out_part = out_part.transpose(1, 0, 2, 3).reshape(share, width)
    fc = over_blk(fc.reshape(plane * rows, ff_share))
    proj = over_blk(w_proj)

    small = small.reshape(n_seq, n_uly, n_blk, lanes * 128)
    flat = small.transpose(0, 2, 1, 3).reshape(n_seq * n_blk * n_uly, lanes * 128)
    whole = [flat[:, i * rows : (i + 1) * rows].reshape(1, width) for i in range(8)]
    at = 8 * rows
    bias_fc = lax.dynamic_slice(
        small, (here_seq, here_uly, 0, at), (1, 1, n_blk, hidden_rows)
    ).reshape(1, ff_share)
    at += hidden_rows
    lengths = small[:, 0, 0, at : at + doc_lengths.size].astype(jnp.int32)
    lengths = lengths.reshape(n_seq, *doc_lengths.shape)
    gain_one, shift_one, bias_q, bias_v, bias_out, gain_two, shift_two, bias_proj = whole
    mine = lambda v: lax.dynamic_slice(v, (0, here * share), (1, share))
    bias_q, bias_v = mine(bias_q), mine(bias_v)

    normed = norm_gather(tokens, gain_one, shift_one, plane, order)
    normed = normed.reshape(plane * n_rows, width)
    grad_out = over(by_plane(cotangent)).reshape(n_rows, width)

    made = product(normed, qkv)
    bias_all = jnp.concatenate([bias_q, jnp.zeros_like(bias_q), bias_v], axis=1)
    scales = jnp.repeat(jnp.array([[scale, 1.0, 1.0]], F32), share, axis=1)
    made = ((made + bias_all) * scales).astype(BF)

    groups = [
        [g * sharing + i for i in range(sharing)] for g in range(n_blk // sharing)
    ]
    pairs = n_seq * held * heads // sharing
    length = n_blk * n_uly * tok
    if sharing == held == 1:
        layout = (n_seq, n_uly, n_blk, part, heads)
    else:
        layout = (pairs, 1, 1, length, 1)

    def to_heads(matrix, kinds):
        if sharing == held == 1:
            return matrix
        matrix = matrix.reshape(n_seq, n_uly, n_blk, held, part, kinds, heads, HD)
        matrix = matrix.transpose(0, 3, 6, 2, 1, 4, 5, 7)
        matrix = matrix.reshape(n_seq * held * heads, n_blk, n_uly, 1, part, kinds * HD)
        if sharing > 1:
            matrix = lax.all_to_all(
                matrix, "blk", split_axis=0, concat_axis=3, axis_index_groups=groups, tiled=True
            )
        return matrix.reshape(pairs * length, kinds * HD)

    def from_heads(matrix, kinds):
        if sharing == held == 1:
            return matrix
        matrix = matrix.reshape(pairs, n_blk, n_uly, sharing, part, kinds * HD)
        if sharing > 1:
            matrix = lax.all_to_all(
                matrix, "blk", split_axis=3, concat_axis=0, axis_index_groups=groups, tiled=True
            )
        matrix = matrix.reshape(n_seq, held, heads, n_blk, n_uly, part, kinds, HD)
        matrix = matrix.transpose(0, 4, 3, 1, 5, 6, 2, 7)
        return matrix.reshape(plane * n_rows, kinds * share)

    turn = here_blk % sharing
    pair_at = turn * pairs + jnp.arange(layout[0]) * layout[4]
    seq_of = pair_at // (held * heads)
    held_of = (pair_at // heads) % held
    which = (here_blk // sharing) * held + held_of
    own_lengths = lengths[seq_of, which]
    first = own_lengths[:, 0:1]
    bounds = jnp.concatenate([first, first + own_lengths[:, 1:2]], axis=1).reshape(-1)

    attended_low, natural, attended, logs, grad_all = attend(
        bounds, to_heads(made, 3), grad_out, plane, layout
    )
    grad_all = grad_all.reshape(plane * n_rows, width)
    attended_low = from_heads(attended_low, 1)
    hidden, normed_two = hidden_gather(
        attended_low, out_part, tokens, bias_out, gain_two, shift_two, plane, order
    )
    normed_two = normed_two.reshape(plane * n_rows, width)
    inner = product(normed_two, fc) + bias_fc
    gelu_value, gelu_back = jax.vjp(gelu_tanh, inner)
    active = gelu_value.astype(BF)
    grad_w_proj = lax.psum_scatter(
        transposed(active, grad_all).astype(BF), "blk", scatter_dimension=0, tiled=True
    ).astype(F32)
    grad_inner = gelu_back(against(grad_all, proj))[0].astype(BF)
    grad_b_fc = jnp.sum(grad_inner.astype(F32), axis=0)
    grad_fc = lax.psum_scatter(
        transposed(normed_two, grad_inner).astype(BF), "blk", scatter_dimension=0, tiled=True
    )
    grad_hidden, sums_two, branch_all = branch_gather(
        grad_inner, fc, hidden, grad_out, gain_two, plane, order
    )
    branch_all = branch_all.reshape(plane * n_rows, width)
    grad_w_out = transposed(attended_low, branch_all).astype(BF)
    grad_w_out = grad_w_out.reshape(n_blk // n_uly, n_uly, rows, width).transpose(1, 0, 2, 3)
    grad_w_out = lax.all_to_all(grad_w_out, "uly", split_axis=0, concat_axis=0, tiled=True)
    grad_w_out = lax.psum_scatter(
        grad_w_out.reshape(n_blk * rows, width), "blk", scatter_dimension=0, tiled=True
    ).astype(F32)
    grad_heads = to_heads(against(branch_all, out_part).astype(BF), 1)
    backs, result = attend_back(
        bounds, grad_heads, natural, attended, logs, active, proj, hidden, bias_proj, layout, scale
    )
    result = over(result.reshape(n_blk, held * part, width))
    backs = from_heads(backs, 3)
    grad_bias = jnp.sum(backs.astype(F32), axis=0)
    grad_qkv = lax.psum_scatter(
        transposed(normed, backs).astype(BF), "blk", scatter_dimension=0, tiled=True
    )
    sums_one, grad_inputs = inputs_return(
        backs, qkv, tokens, grad_hidden, gain_one, n_blk, order
    )

    def widened(vector):
        return lax.dynamic_update_slice(jnp.zeros((width,), F32), vector, (here * share,))

    parts = (
        sums_one[0],
        sums_one[1],
        widened(grad_bias[:share]),
        widened(grad_bias[2 * share :]),
        sums_two[2],
        sums_two[0],
        sums_two[1],
        sums_two[3],
    )
    wide_fc = lax.dynamic_update_slice(
        jnp.zeros((n_seq, n_blk, n_uly, hidden_rows), F32),
        grad_b_fc.reshape(1, n_blk, 1, hidden_rows),
        (here_seq, 0, here_uly, 0),
    )
    sums = jnp.concatenate(
        [p.reshape(n_seq, n_blk, n_uly, rows) for p in parts] + [wide_fc], axis=3
    )
    used = sums.shape[3]
    end_lanes = -(-used // 1024) * 8
    sums = jnp.pad(sums, ((0, 0),) * 3 + ((0, end_lanes * 128 - used),))
    sums = sums.transpose(0, 2, 1, 3).reshape(plane, n_blk, end_lanes, 128)
    grad_qkv, grad_fc, sums = finish(
        grad_qkv.reshape(plane, rows, 3 * share), grad_fc.reshape(plane, rows, ff_share), sums
    )
    sums = sums.reshape(-1)
    each = [sums[i * rows : (i + 1) * rows] for i in range(8)]
    grad_qkv = grad_qkv.reshape(plane, rows, 3, share).transpose(2, 1, 0, 3)
    grad_qkv = grad_qkv.reshape(3, rows, width).astype(F32)
    grad_fc = grad_fc.reshape(n_seq, n_uly, rows, n_blk, hidden_rows)
    grad_fc = grad_fc.transpose(2, 0, 3, 1, 4).reshape(rows, -1).astype(F32)
    return (
        from_plane(result),
        from_plane(grad_inputs),
        each[0],
        each[1],
        grad_qkv[0],
        each[2],
        grad_qkv[1],
        grad_qkv[2],
        each[3],
        grad_w_out,
        each[4],
        each[5],
        each[6],
        grad_fc,
        sums[8 * rows : used],
        grad_w_proj,
        each[7],
    )


def solution(mesh):
    tokens = P("seq", ("blk", "uly"), None)
    vector = P(ALL)
    matrix = P(ALL, None)
    return jax.shard_map(
        on_device,
        mesh=mesh,
        in_specs=(
            tokens, P("seq", None), vector, vector, matrix, vector, matrix, matrix, vector,
            matrix, vector, vector, vector, matrix, vector, matrix, vector, tokens,
        ),
        out_specs=(
            tokens, tokens, vector, vector, matrix, vector, matrix, matrix, vector,
            matrix, vector, vector, vector, matrix, vector, matrix, vector,
        ),
        check_vma=False,
    )
```

```python
import functools
import math

import jax
import jax.numpy as jnp
from jax import lax
from jax.experimental import pallas as pl
from jax.experimental.pallas import tpu as pltpu
from jax.sharding import PartitionSpec as P

HD = 128
EPS = 1e-05
NEGATIVE = -1e30
ALL = ("seq", "blk", "uly")
PLANE = ("seq", "uly")
BF = jnp.bfloat16
F32 = jnp.float32
MESH = pl.DeviceIdType.MESH
ANY = pl.BlockSpec(memory_space=pl.ANY)
VMEM = pl.BlockSpec(memory_space=pltpu.VMEM)
MIB = 2**20
CHUNK = 16
TILE = 2048


def gelu_tanh(values):
    return jax.nn.gelu(values, approximate=True)


def product(left_side, right_side):
    return jnp.dot(left_side, right_side, preferred_element_type=F32)


def transposed(left_side, right_side):
    return lax.dot_general(
        left_side, right_side, (((0,), (0,)), ((), ())), preferred_element_type=F32
    )


def against(left_side, right_side):
    return lax.dot_general(
        left_side, right_side, (((1,), (1,)), ((), ())), preferred_element_type=F32
    )


def meet(peers):
    barrier = pltpu.get_barrier_semaphore()
    for peer in peers:
        pl.semaphore_signal(barrier, inc=1, device_id=peer, device_id_type=MESH)
    pl.semaphore_wait(barrier, len(peers))


def sender(send, recv):
    def copy(i, source, target, device):
        made = pltpu.make_async_remote_copy(
            src_ref=source,
            dst_ref=target,
            send_sem=send.at[i],
            recv_sem=recv.at[i],
            device_id=device,
            device_id_type=MESH,
        )
        made.start()
        return made

    return copy


def place():
    s, b, u = (lax.axis_index(a) for a in ALL)
    a, c = u // 2, u % 2
    beside = (s, b, 2 * (1 - a) + c)
    across = (1 - s, b, u)
    twin = (s, b, 2 * a + 1 - c)

    def blocks(core):
        own = 4 * s + 2 * a + core
        on_x = 4 * s + 2 * (1 - a) + core
        on_y = 4 * (1 - s) + 2 * a + core
        diagonal = 4 * (1 - s) + 2 * (1 - a) + core
        return diagonal, on_x, on_y, own

    return (s, b, u), (beside, across, twin), blocks(c), blocks(1 - c)


class Spread:
    def __init__(self, own, out, send, recv, local):
        _, self.near_by, self.blocks, self.twins = place()
        beside, across, twin = self.near_by
        me = self.blocks[3]
        half = own.shape[0] // 2
        self.out, self.parts = out, (pl.ds(0, half), pl.ds(half, half))
        self.copy = copy = sender(send, recv)
        p0, p1 = self.parts
        self.x0 = copy(0, own.at[p0], out.at[me, p0], beside)
        self.y1 = copy(1, own.at[p1], out.at[me, p1], across)
        self.x1 = copy(2, own.at[p1], out.at[me, p1], beside)
        self.y0 = copy(3, own.at[p0], out.at[me, p0], across)
        self.own_twin = copy(4, own, out.at[me], twin)
        self.started = [self.x0, self.y1, self.x1, self.y0, self.own_twin]
        self.kept = pltpu.make_async_copy(own, out.at[me], local)
        self.kept.start()

    def pass_on(self, i, block, part, device):
        at = self.out.at[block, self.parts[part]]
        made = self.copy(i, at, at, device)
        self.started.append(made)
        return made

    def own_blocks(self):
        self.kept.wait()
        self.own_twin.wait_recv()

    def first_halves(self):
        beside, across, twin = self.near_by
        _, on_x, on_y, _ = self.blocks
        self.x0.wait_recv()
        self.d0 = self.pass_on(5, on_x, 0, across)
        self.t0 = self.pass_on(6, on_x, 0, twin)
        self.y1.wait_recv()
        self.d1 = self.pass_on(7, on_y, 1, beside)
        self.t1 = self.pass_on(8, on_y, 1, twin)

    def second_halves(self):
        _, _, twin = self.near_by
        _, on_x, on_y, _ = self.blocks
        self.x1.wait_recv()
        self.t2 = self.pass_on(9, on_x, 1, twin)
        self.y0.wait_recv()
        self.t3 = self.pass_on(10, on_y, 0, twin)

    def twin_sides(self):
        for made in (self.t0, self.t1, self.t2, self.t3):
            made.wait_recv()

    def diagonals(self):
        _, _, twin = self.near_by
        diag = self.blocks[0]
        self.d0.wait_recv()
        t4 = self.pass_on(11, diag, 0, twin)
        self.d1.wait_recv()
        t5 = self.pass_on(12, diag, 1, twin)
        t4.wait_recv()
        t5.wait_recv()

    def close(self):
        for made in self.started:
            made.wait_send()


def spread(own, out, send, recv, local):
    moving = Spread(own, out, send, recv, local)
    yield
    moving.first_halves()
    yield
    moving.second_halves()
    yield
    moving.own_blocks()
    moving.twin_sides()
    moving.diagonals()
    moving.close()


def run(steps):
    for _ in steps:
        pass


SPREAD = 13


def collect(
    multiply, total, to_twin, from_twin, mine, in_x, in_y, send, recv, prepare=lambda block: None
):
    _, (beside, across, twin), here, other = place()
    rows, width = total.shape
    half = rows // 2
    parts = (pl.ds(0, half), pl.ds(half, half))
    copy = sender(send, recv)
    tiles = width // TILE

    def each_tile(body):
        def step(t, carry):
            body(pl.ds(pl.multiple_of(t * TILE, TILE), TILE))
            return carry

        lax.fori_loop(0, tiles, step, 0)

    to_twins = []

    def for_twin(k):
        def term(cols):
            to_twin[k, :, cols] = multiply(other[k], cols).astype(BF)

        prepare(other[k])
        each_tile(term)
        to_twins.append(copy(k, to_twin.at[k], from_twin.at[k], twin))

    def for_here(k):
        prepare(here[k])
        to_twins[k].wait_recv()

        def term(cols):
            both = multiply(here[k], cols) + from_twin[k, :, cols].astype(F32)
            if k < 3:
                mine[k, :, cols] = both.astype(BF)
            else:
                total[:, cols] = both

        each_tile(term)

    started = []
    for_twin(0)
    for_twin(1)
    for_here(0)
    dx = copy(4, mine.at[0, parts[0]], in_x.at[0], beside)
    dy = copy(5, mine.at[0, parts[1]], in_y.at[0], across)
    for_twin(2)
    for_here(1)
    started.append(copy(6, mine.at[1, parts[0]], in_x.at[1], beside))
    for_twin(3)
    for_here(2)
    started.append(copy(7, mine.at[2, parts[1]], in_y.at[1], across))
    for_here(3)
    yield

    def add(k, part, arrived):
        def step(t, carry):
            at = pl.ds(pl.multiple_of(t * CHUNK, CHUNK), CHUNK)
            to = pl.ds(pl.multiple_of(part * half + t * CHUNK, CHUNK), CHUNK)
            mine[k, to] = (mine[k, to].astype(F32) + arrived[0, at].astype(F32)).astype(BF)
            return carry

        lax.fori_loop(0, half // CHUNK, step, 0)

    dy.wait_recv()
    add(1, 1, in_y)
    started.append(copy(8, mine.at[1, parts[1]], in_x.at[2], beside))
    dx.wait_recv()
    add(2, 0, in_x)
    started.append(copy(9, mine.at[2, parts[0]], in_y.at[2], across))
    yield
    for made in started:
        made.wait_recv()

    def finish(t, carry):
        at = pl.ds(pl.multiple_of(t * CHUNK, CHUNK), CHUNK)
        low = pl.ds(pl.multiple_of(half + t * CHUNK, CHUNK), CHUNK)
        total[at] += in_x[1, at].astype(F32) + in_y[2, at].astype(F32)
        total[low] += in_x[2, at].astype(F32) + in_y[1, at].astype(F32)
        return carry

    lax.fori_loop(0, half // CHUNK, finish, 0)
    for made in to_twins + started + [dx, dy]:
        made.wait_send()


COLLECT = 10


def collect_scratch(rows, width):
    return [
        pltpu.VMEM((rows, width), F32),
        pltpu.VMEM((4, rows, width), BF),
        pltpu.VMEM((4, rows, width), BF),
        pltpu.VMEM((3, rows, width), BF),
        pltpu.VMEM((3, rows // 2, width), BF),
        pltpu.VMEM((3, rows // 2, width), BF),
        pltpu.SemaphoreType.DMA((COLLECT,)),
        pltpu.SemaphoreType.DMA((COLLECT,)),
    ]


def reorder(values, outer, inner, lanes):
    return jnp.concatenate(
        [
            values[:, (o * inner + i) * lanes : (o * inner + i + 1) * lanes]
            for i in range(inner)
            for o in range(outer)
        ],
        axis=1,
    )


def norm_parts(values):
    average = jnp.mean(values, axis=-1, keepdims=True)
    centred = values - average
    variance = jnp.mean(centred * centred, axis=-1, keepdims=True)
    spread_back = lax.rsqrt(variance + EPS)
    return centred * spread_back, spread_back


def norm_back(grad, values, gain):
    unit, spread_back = norm_parts(values)
    scaled = grad * gain
    back = spread_back * (
        scaled
        - jnp.mean(scaled, axis=-1, keepdims=True)
        - unit * jnp.mean(scaled * unit, axis=-1, keepdims=True)
    )
    return back, grad * unit


def each_chunk(rows, body):
    def step(t, carry):
        body(pl.ds(pl.multiple_of(t * CHUNK, CHUNK), CHUNK))
        return carry

    lax.fori_loop(0, rows // CHUNK, step, 0)


def row_sum(values):
    return jnp.sum(values, axis=0, keepdims=True)


def return_rows(block, out, n_blk, send, recv, local):
    (s, b, u), _, _, _ = place()
    count = block.shape[0] // n_blk
    copy = sender(send, recv)
    started = []
    for j in range(1, n_blk):
        to = (b + j) % n_blk
        rows = pl.ds(pl.multiple_of(to * count, count), count)
        started.append(copy(j - 1, block.at[rows], out.at[b], (s, to, u)))
    rows = pl.ds(pl.multiple_of(b * count, count), count)
    kept = pltpu.make_async_copy(block.at[rows], out.at[b], local)
    kept.start()
    return started + [kept]


def blk_peers(n_blk):
    (s, b, u), _, _, _ = place()
    return [(s, (b + j) % n_blk, u) for j in range(1, n_blk)]


def exchange_columns(copy, first, whole, cut, p, me, device, sizes, gather):
    n_seq, _, n_uly, runs = sizes
    plane = n_seq * n_uly
    owner = p if gather else me
    share = whole[0].shape[1] // plane
    run_share = whole[3].shape[1] // (plane * runs)
    spans = []
    for i in range(3):
        at = pl.ds(pl.multiple_of(owner * share, share), share)
        spans.append((whole[i], at, cut[0], pl.ds(i * share, share)))
    for r in range(runs):
        at = ((owner // n_uly) * runs + r) * n_uly + owner % n_uly
        at = pl.ds(pl.multiple_of(at * run_share, run_share), run_share)
        spans.append((whole[3], at, cut[1], pl.ds(r * run_share, run_share)))
    started = []
    for i, (matrix, at, part, inside) in enumerate(spans):
        if gather:
            source, target = matrix.at[:, at], part.at[me, :, inside]
        else:
            source, target = part.at[p, :, inside], matrix.at[:, at]
        started.append(copy(first + i, source, target, device))
    return started


def entry_kernel(
    sizes, x_ref, wq_ref, wk_ref, wv_ref, fc_ref, *refs
):
    vectors, (bias_ref, lengths_ref), refs = refs[:8], refs[8:10], refs[10:]
    enter_body(sizes, x_ref, wq_ref, wk_ref, wv_ref, fc_ref, vectors, bias_ref, lengths_ref, *refs)


def enter_body(
    sizes, x_ref, wq_ref, wk_ref, wv_ref, fc_ref, short, bias_ref, lengths_ref, tok, qkv, fc, small,
    small_ref, blk_send, blk_recv, plane_send, plane_recv, local,
):
    n_seq, n_blk, n_uly, runs = sizes
    (s, b, u), _, (_, _, _, me), _ = place()
    plane = n_seq * n_uly
    pieces = 3 + runs
    small_ref[...] = jnp.zeros_like(small_ref)
    for i, ref in enumerate(short):
        small_ref[i : i + 1, : ref.shape[1]] = ref[...].astype(F32)
    lanes = min(128, bias_ref.shape[1])
    for i in range(bias_ref.shape[1] // lanes):
        part = bias_ref[:, i * lanes : (i + 1) * lanes].astype(F32)
        small_ref[8 + i : 9 + i, :lanes] = part
    small_ref[SMALL - 1 :, : lengths_ref.shape[1]] = lengths_ref[...].astype(F32)
    others = [(me + j) % plane for j in range(1, plane)]
    friends = [(p // n_uly, b, p % n_uly) for p in others]
    column = blk_peers(n_blk)
    meet(friends + column)
    by_blk = sender(blk_send, blk_recv)
    by_plane = sender(plane_send, plane_recv)

    def at_home(i, source, target, _):
        made = pltpu.make_async_copy(source, target, local.at[i])
        made.start()
        return made

    sources, targets = (wq_ref, wk_ref, wv_ref, fc_ref), (qkv, fc)
    first = at_home(0, small_ref, small.at[me, b], None)
    vectors, started = [], []
    for j, peer in enumerate(column):
        vectors.append(by_blk(j, small_ref, small.at[me, b], peer))
    for j, peer in enumerate(column):
        started.append(by_blk(n_blk - 1 + j, x_ref.at[peer[1]], tok.at[b], peer))
    for j, (p, peer) in enumerate(zip(others, friends)):
        started += exchange_columns(
            by_plane, pieces * j, sources, targets, p, me, peer, sizes, True
        )
    started.append(at_home(1, x_ref.at[b], tok.at[b], None))
    started += exchange_columns(at_home, 2, sources, targets, me, me, None, sizes, True)
    first.wait()
    for made in vectors:
        made.wait()
    for j, peer in enumerate(friends):
        at = small.at[me]
        started.append(by_plane(pieces * (plane - 1) + j, at, at, peer))
    for made in started:
        made.wait()


SMALL = 16


def enter(x, weights, fc, short, sizes):
    n_seq, n_blk, n_uly, runs = sizes
    plane = n_seq * n_uly
    rows, width = weights[0].shape
    pieces = (4 + runs) * (plane - 1)
    return pl.pallas_call(
        functools.partial(entry_kernel, sizes),
        name="enter",
        out_shape=(
            jax.ShapeDtypeStruct(x.shape, x.dtype),
            jax.ShapeDtypeStruct((plane, rows, 3 * width // plane), BF),
            jax.ShapeDtypeStruct((plane, rows, fc.shape[1] // plane), BF),
            jax.ShapeDtypeStruct((plane, n_blk, SMALL, 128), F32),
        ),
        in_specs=[ANY] * 5 + [VMEM] * len(short),
        out_specs=(ANY,) * 4,
        scratch_shapes=[
            pltpu.VMEM((SMALL, 128), F32),
            pltpu.SemaphoreType.DMA((2 * (n_blk - 1),)),
            pltpu.SemaphoreType.DMA((2 * (n_blk - 1),)),
            pltpu.SemaphoreType.DMA((pieces,)),
            pltpu.SemaphoreType.DMA((pieces,)),
            pltpu.SemaphoreType.DMA((5 + runs,)),
        ],
        compiler_params=pltpu.CompilerParams(collective_id=0, has_side_effects=True),
        cost_estimate=pl.CostEstimate(flops=0, bytes_accessed=MIB, transcendentals=0),
    )(x, *weights, fc, *short)


def norm_kernel(
    order, n_blk, tok, gain, shift, cot_ref, out, cot, own, send, recv, local, g_send, g_recv, kept
):
    (s, b, u), near, _, _ = place()
    column = blk_peers(n_blk)
    meet(list(near) + column)
    copy = sender(g_send, g_recv)
    count = cot_ref.shape[1]
    rows = pl.ds(pl.multiple_of(b * count, count), count)
    started = [copy(j, cot_ref.at[peer[1]], cot.at[rows], peer) for j, peer in enumerate(column)]
    started.append(pltpu.make_async_copy(cot_ref.at[b], cot.at[rows], kept))
    started[-1].start()

    def chunk(at):
        unit, _ = norm_parts(tok[at].astype(F32))
        own[at] = reorder(unit * gain[...] + shift[...], *order).astype(BF)

    each_chunk(own.shape[0], chunk)
    run(spread(own, out, send, recv, local))
    for made in started:
        made.wait()


def norm_gather(tok, gain, shift, cot, plane, order):
    rows, width = tok.shape
    n_blk = cot.shape[0]
    return pl.pallas_call(
        functools.partial(norm_kernel, order, n_blk),
        name="norm_gather",
        out_shape=(
            jax.ShapeDtypeStruct((plane, rows, width), BF),
            jax.ShapeDtypeStruct((rows, width), BF),
        ),
        in_specs=[VMEM] * 3 + [ANY],
        out_specs=(ANY, ANY),
        scratch_shapes=[pltpu.VMEM((rows, width), BF)]
        + spread_scratch()
        + [
            pltpu.SemaphoreType.DMA((n_blk - 1,)),
            pltpu.SemaphoreType.DMA((n_blk - 1,)),
            pltpu.SemaphoreType.DMA,
        ],
        compiler_params=pltpu.CompilerParams(
            collective_id=1, has_side_effects=True, vmem_limit_bytes=16 * MIB
        ),
        cost_estimate=pl.CostEstimate(flops=0, bytes_accessed=MIB, transcendentals=0),
    )(tok, gain, shift, cot)


BLOCK = 256


def document_start(bounds, s, position):
    first, second = bounds[2 * s], bounds[2 * s + 1]
    return jnp.where(position >= second, second, jnp.where(position >= first, first, 0))


def chunks_of(layout):
    n_seq, n_uly, n_blk, part, _ = layout
    for s in range(n_seq):
        for b in range(n_blk):
            for u in range(n_uly):
                yield ((s * n_uly + u) * n_blk + b) * part, s, (b * n_uly + u) * part


def attend_kernel(
    layout, bounds, qkv, cot, low, natural, attended, logs, out, send, recv, local,
):
    _, near, _, _ = place()
    _, _, _, part, heads = layout
    meet(near)
    moving = spread(cot, out, send, recv, local)
    next(moving)
    share = heads * HD
    pairs, length = natural.shape[1:3]
    for row, s, position in chunks_of(layout):
        for kind in range(3):
            for h in range(heads):
                lane = kind * share + h * HD
                natural[kind, s * heads + h, position : position + part] = qkv[
                    row : row + part, lane : lane + HD
                ]

    def pair(p, carry):
        for start in range(0, length, BLOCK):
            stop = start + BLOCK
            scores = against(natural[0, p, start:stop], natural[1, p, :stop])
            row = start + lax.broadcasted_iota(jnp.int32, (BLOCK, 1), 0)
            key = lax.broadcasted_iota(jnp.int32, (BLOCK, stop), 1)
            allowed = (key >= document_start(bounds, p // heads, row)) & (key <= row)
            scores = jnp.where(allowed, scores, NEGATIVE)
            top = jnp.max(scores, axis=1, keepdims=True)
            powered = jnp.exp(scores - top)
            total = jnp.sum(powered, axis=1, keepdims=True)
            made = product(powered.astype(BF), natural[2, p, :stop])
            attended[p, start:stop] = made / total
            log_total = jnp.broadcast_to(top + jnp.log(total), (BLOCK, HD))
            logs[p, :, start:stop] = log_total.T[:8]
        return carry

    cut = (pairs + 1) // 2
    lax.fori_loop(0, cut, pair, 0)
    next(moving)
    lax.fori_loop(cut, pairs, pair, 0)
    next(moving)
    for row, s, position in chunks_of(layout):
        for h in range(heads):
            low[row : row + part, h * HD : (h + 1) * HD] = attended[
                s * heads + h, position : position + part
            ].astype(BF)
    run(moving)


def attend(bounds, qkv, cot, plane, layout):
    n_seq, n_uly, n_blk, part, heads = layout
    rows, width = cot.shape
    pairs, length = n_seq * heads, n_uly * n_blk * part
    return pl.pallas_call(
        functools.partial(attend_kernel, layout),
        name="attend",
        out_shape=(
            jax.ShapeDtypeStruct((qkv.shape[0], heads * HD), BF),
            jax.ShapeDtypeStruct((3, pairs, length, HD), BF),
            jax.ShapeDtypeStruct((pairs, length, HD), F32),
            jax.ShapeDtypeStruct((pairs, 8, length), F32),
            jax.ShapeDtypeStruct((plane, rows, width), BF),
        ),
        in_specs=[pl.BlockSpec(memory_space=pltpu.SMEM), VMEM, ANY],
        out_specs=(VMEM, VMEM, VMEM, VMEM, ANY),
        scratch_shapes=[
            pltpu.SemaphoreType.DMA((SPREAD,)),
            pltpu.SemaphoreType.DMA((SPREAD,)),
            pltpu.SemaphoreType.DMA,
        ],
        compiler_params=pltpu.CompilerParams(
            collective_id=2, has_side_effects=True, vmem_limit_bytes=40 * MIB
        ),
        cost_estimate=pl.CostEstimate(flops=0, bytes_accessed=MIB, transcendentals=0),
    )(bounds, qkv, cot)


def attend_back_kernel(
    layout, scale, bounds, grad, natural, attended, logs, act, weight, hid, bias, mixed,
    back, out, mixed_out, grads, grads_back, key_grad, value_grad,
    total, to_twin, from_twin, mine, in_x, in_y, c_send, c_recv, u_send, u_recv, local,
):
    (s, b, u), near, _, _ = place()
    rows = total.shape[0]
    _, _, _, part, heads = layout
    share = heads * HD
    n_uly = mixed.shape[0]
    in_row = [(s, b, (u + j) % n_uly) for j in range(1, n_uly)]
    meet([near[1]] + in_row)
    copy = sender(u_send, u_recv)
    mixing = [copy(j, mixed.at[to[2]], mixed_out.at[u], to) for j, to in enumerate(in_row)]
    mixing.append(pltpu.make_async_copy(mixed.at[u], mixed_out.at[u], local))
    mixing[-1].start()

    def multiply(block, cols):
        return product(rows_of(act, block, rows), weight[:, cols])

    moving = collect(multiply, total, to_twin, from_twin, mine, in_x, in_y, c_send, c_recv)
    next(moving)
    pairs, length = natural.shape[1:3]
    for row, s, position in chunks_of(layout):
        for h in range(heads):
            grads[s * heads + h, position : position + part] = grad[
                row : row + part, h * HD : (h + 1) * HD
            ]

    def pair(p, carry):
        for start in reversed(range(0, length, BLOCK)):
            stop = start + BLOCK
            query, key, value = (
                natural[0, p, start:stop], natural[1, p, :stop], natural[2, p, :stop]
            )
            above = grads[p, start:stop]
            row = start + lax.broadcasted_iota(jnp.int32, (1, BLOCK), 1)
            at = lax.broadcasted_iota(jnp.int32, (stop, BLOCK), 0)
            allowed = (at >= document_start(bounds, p // heads, row)) & (at <= row)
            scores = jnp.where(allowed, against(key, query), NEGATIVE)
            chances = jnp.exp(scores - logs[p, 0:1, start:stop])
            dots = (above.astype(F32) * attended[p, start:stop]).T
            dots = jnp.sum(dots, axis=0, keepdims=True)
            by_value = product(chances.astype(BF), above)
            scored = (chances * (against(value, above) - dots)).astype(BF)
            by_key = product(scored, query)
            grads_back[p, start:stop] = (transposed(scored, key) * scale).astype(BF)
            if stop == length:
                key_grad[...] = by_key
                value_grad[...] = by_value
            else:
                key_grad[:stop] += by_key
                value_grad[:stop] += by_value
        grads_back[pairs + p] = key_grad[...].astype(BF)
        grads_back[2 * pairs + p] = value_grad[...].astype(BF)
        return carry

    cut = (pairs + 1) // 2
    lax.fori_loop(0, cut, pair, 0)
    next(moving)
    lax.fori_loop(cut, pairs, pair, 0)
    for row, s, position in chunks_of(layout):
        for kind in range(3):
            for h in range(heads):
                lane = kind * share + h * HD
                back[row : row + part, lane : lane + HD] = grads_back[
                    kind * pairs + s * heads + h, position : position + part
                ]
    run(moving)

    def chunk(at):
        out[at] = (total[at] + hid[at] + bias[...]).astype(BF)

    each_chunk(rows, chunk)
    for made in mixing:
        made.wait()


def attend_back(
    bounds, grad, natural, attended, logs, act, weight, hid, bias, mixed, layout, scale
):
    rows, width = hid.shape
    pairs, length = natural.shape[1:3]
    return pl.pallas_call(
        functools.partial(attend_back_kernel, layout, scale),
        name="attend_back",
        out_shape=(
            jax.ShapeDtypeStruct((grad.shape[0], 3 * grad.shape[1]), BF),
            jax.ShapeDtypeStruct((rows, width), BF),
            jax.ShapeDtypeStruct(mixed.shape, BF),
        ),
        in_specs=[pl.BlockSpec(memory_space=pltpu.SMEM)] + [VMEM] * 8 + [ANY],
        out_specs=(VMEM, VMEM, ANY),
        scratch_shapes=[
            pltpu.VMEM((pairs, length, HD), BF),
            pltpu.VMEM((3 * pairs, length, HD), BF),
            pltpu.VMEM((length, HD), F32),
            pltpu.VMEM((length, HD), F32),
        ]
        + collect_scratch(rows, width)
        + [
            pltpu.SemaphoreType.DMA((mixed.shape[0] - 1,)),
            pltpu.SemaphoreType.DMA((mixed.shape[0] - 1,)),
            pltpu.SemaphoreType.DMA,
        ],
        compiler_params=pltpu.CompilerParams(
            collective_id=5, has_side_effects=True, vmem_limit_bytes=60 * MIB
        ),
        cost_estimate=pl.CostEstimate(flops=0, bytes_accessed=MIB, transcendentals=0),
    )(bounds, grad, natural, attended, logs, act, weight, hid, bias, mixed)


def rows_of(ref, block, rows):
    return ref[pl.ds(pl.multiple_of(block * rows, rows), rows), :]


def hidden_kernel(
    order, act, weight, tok, bias, gain, shift, hidden, own,
    total, to_twin, from_twin, mine, in_x, in_y, c_send, c_recv,
):
    _, near, _, _ = place()
    rows = total.shape[0]
    meet(near)

    def multiply(block, cols):
        return product(rows_of(act, block, rows), weight[:, cols])

    run(collect(multiply, total, to_twin, from_twin, mine, in_x, in_y, c_send, c_recv))

    def chunk(at):
        values = total[at] + tok[at].astype(F32) + bias[...]
        hidden[at] = values
        unit, _ = norm_parts(values)
        own[at] = reorder(unit * gain[...] + shift[...], *order).astype(BF)

    each_chunk(rows, chunk)


def hidden_norm(act, weight, tok, bias, gain, shift, order):
    rows, width = tok.shape
    return pl.pallas_call(
        functools.partial(hidden_kernel, order),
        name="hidden_norm",
        out_shape=(
            jax.ShapeDtypeStruct((rows, width), F32),
            jax.ShapeDtypeStruct((rows, width), BF),
        ),
        in_specs=[VMEM] * 6,
        out_specs=(VMEM, VMEM),
        scratch_shapes=collect_scratch(rows, width),
        compiler_params=pltpu.CompilerParams(
            collective_id=3, has_side_effects=True, vmem_limit_bytes=40 * MIB
        ),
        cost_estimate=pl.CostEstimate(flops=0, bytes_accessed=MIB, transcendentals=0),
    )(act, weight, tok, bias, gain, shift)


def spread_scratch():
    return [
        pltpu.SemaphoreType.DMA((SPREAD,)),
        pltpu.SemaphoreType.DMA((SPREAD,)),
        pltpu.SemaphoreType.DMA,
    ]


def block_rows(block, rows):
    return pl.ds(pl.multiple_of(block * rows, rows), rows)


def fetch(sources, targets, sems):
    made = [
        pltpu.make_async_copy(source, target, sems.at[i])
        for i, (source, target) in enumerate(zip(sources, targets))
    ]
    for copy in made:
        copy.start()
    return made


def pairs_of(moving):
    diag, on_x, on_y, me = moving.blocks
    twin_diag, twin_x, twin_y, twin = moving.twins
    moving.own_blocks()
    yield me, twin
    moving.first_halves()
    moving.second_halves()
    yield on_x, on_y
    moving.twin_sides()
    yield twin_x, twin_y
    moving.diagonals()
    yield diag, twin_diag
    moving.close()


FF_TILE = 1024
FC_TILE = 256


def feed_kernel(
    own, weight_ref, bias, cots, out, active, slope, grad,
    weight, rows_in, cots_in, low_out, steep_out, acc, w_sem, sems, out_sems, send, recv, local,
):
    _, near, _, _ = place()
    rows, width = own.shape
    ff = weight.shape[1]
    loading = pltpu.make_async_copy(weight_ref, weight, w_sem)
    loading.start()
    halves = (pl.ds(0, rows), pl.ds(rows, rows))
    meet(near)
    moving = Spread(own, out, send, recv, local)
    diag, on_x, on_y, me = moving.blocks
    twin_diag, twin_x, twin_y, twin = moving.twins
    plan = [(me, twin), (on_x, on_y), (twin_x, twin_y), (diag, twin_diag)]

    def cots_of(i):
        return fetch(
            [cots.at[p] for p in plan[i]], [cots_in.at[i % 2, h] for h in halves], sems.at[i % 2]
        )

    arriving = cots_of(0)
    leaving = {}
    for i, (left, right) in enumerate(pairs_of(moving)):
        fetched = fetch([out.at[left], out.at[right]], [rows_in.at[h] for h in halves], sems.at[2])
        for made in fetched + arriving:
            made.wait()
        if i == 0:
            loading.wait()
        if i < 3:
            arriving = cots_of(i + 1)
        for made in leaving.pop(i - 2, []):
            made.wait()

        def tile(t, carry, i=i):
            at = pl.ds(pl.multiple_of(t * FF_TILE, FF_TILE), FF_TILE)
            inner = product(rows_in[...], weight[:, at]) + bias[:, at]
            bent = math.sqrt(2 / math.pi) * (inner + 0.044715 * (inner * inner * inner))
            curve = jnp.tanh(bent)
            low = (0.5 * inner * (1.0 + curve)).astype(BF)
            steep = math.sqrt(2 / math.pi) * (1.0 + 3 * 0.044715 * (inner * inner))
            steep = 0.5 * (1.0 + curve) + 0.5 * inner * (1.0 - curve * curve) * steep
            low_out[i % 2, :, at] = low
            steep_out[i % 2, :, at] = steep.astype(BF)
            for cut in range(0, width, 1024):
                cols = pl.ds(cut, 1024)
                term = transposed(low, cots_in[i % 2, :, cols])
                if i == 0:
                    acc[at, cols] = term
                elif i < 3:
                    acc[at, cols] += term
                else:
                    grad[at, cols] = (acc[at, cols] + term).astype(BF)
            return carry

        lax.fori_loop(0, ff // FF_TILE, tile, 0)
        places = [block_rows(left, rows), block_rows(right, rows)]
        leaving[i] = fetch(
            [held.at[i % 2, h] for held in (low_out, steep_out) for h in halves],
            [kept.at[p] for kept in (active, slope) for p in places],
            out_sems.at[i % 2],
        )
    for group in leaving.values():
        for made in group:
            made.wait()


def feed(own, weight, bias, cots):
    rows, width = own.shape
    plane, ff = cots.shape[0], weight.shape[1]
    return pl.pallas_call(
        feed_kernel,
        name="feed",
        out_shape=(
            jax.ShapeDtypeStruct((plane, rows, width), BF),
            jax.ShapeDtypeStruct((plane * rows, ff), BF),
            jax.ShapeDtypeStruct((plane * rows, ff), BF),
            jax.ShapeDtypeStruct((ff, width), BF),
        ),
        in_specs=[VMEM, ANY, VMEM, ANY],
        out_specs=(ANY, ANY, ANY, VMEM),
        scratch_shapes=[
            pltpu.VMEM(weight.shape, BF),
            pltpu.VMEM((2 * rows, width), BF),
            pltpu.VMEM((2, 2 * rows, width), BF),
            pltpu.VMEM((2, 2 * rows, ff), BF),
            pltpu.VMEM((2, 2 * rows, ff), BF),
            pltpu.VMEM((ff, width), F32),
            pltpu.SemaphoreType.DMA,
            pltpu.SemaphoreType.DMA((3, 2)),
            pltpu.SemaphoreType.DMA((2, 4)),
        ]
        + spread_scratch(),
        compiler_params=pltpu.CompilerParams(
            collective_id=8, has_side_effects=True, vmem_limit_bytes=56 * MIB
        ),
        cost_estimate=pl.CostEstimate(flops=0, bytes_accessed=MIB, transcendentals=0),
    )(own, weight, bias, cots)


def back_feed_kernel(
    order, cots, slope, proj, weight, hid, cot, gain, inner_grad, grad_hidden, own, sums, bias,
    cots_in, slope_in, sems,
    total, to_twin, from_twin, mine, in_x, in_y, c_send, c_recv,
):
    _, near, here, other = place()
    rows, width = total.shape
    ff = weight.shape[1]
    plan = [other[0], other[1], here[0], other[2], here[1], other[3], here[2], here[3]]

    def load(i):
        at = i % 2
        return fetch(
            (cots.at[plan[i]], slope.at[block_rows(plan[i], rows)]),
            (cots_in.at[at], slope_in.at[at]),
            sems.at[at],
        )

    loads = [load(0)]
    sums[...] = jnp.zeros_like(sums)
    bias[...] = jnp.zeros_like(bias)
    meet(near)

    def prepare(block):
        i = len(loads) - 1
        for made in loads[i]:
            made.wait()
        loads.append(load(i + 1) if i + 1 < len(plan) else [])

        def tile(t, carry):
            at = pl.ds(pl.multiple_of(t * FF_TILE, FF_TILE), FF_TILE)
            made = against(cots_in[i % 2], proj[at, :]) * slope_in[i % 2, :, at].astype(F32)
            low = made.astype(BF)
            inner_grad[block_rows(block, rows), at] = low
            bias[0:1, at] += row_sum(low.astype(F32))
            return carry

        lax.fori_loop(0, ff // FF_TILE, tile, 0)

    def multiply(block, cols):
        return against(rows_of(inner_grad, block, rows), weight[cols, :])

    run(
        collect(
            multiply, total, to_twin, from_twin, mine, in_x, in_y, c_send, c_recv, prepare
        )
    )
    inner, outer, lanes = order[1], order[0], order[2]

    def chunk(at):
        grad = reorder(total[at], inner, outer, lanes)
        back, by_gain = norm_back(grad, hid[at], gain[...])
        passed = cot[at].astype(F32)
        back = back + passed
        grad_hidden[at] = back
        low = back.astype(BF)
        own[at] = low
        sums[0:1] += row_sum(by_gain)
        sums[1:2] += row_sum(grad)
        sums[2:3] += row_sum(low.astype(F32))
        sums[3:4] += row_sum(passed)

    each_chunk(rows, chunk)


def back_feed(cots, slope, proj, weight, hid, cot, gain, order):
    rows, width = cot.shape
    ff = weight.shape[1]
    return pl.pallas_call(
        functools.partial(back_feed_kernel, order),
        name="back_feed",
        out_shape=(
            jax.ShapeDtypeStruct((slope.shape[0], ff), BF),
            jax.ShapeDtypeStruct((rows, width), F32),
            jax.ShapeDtypeStruct((rows, width), BF),
            jax.ShapeDtypeStruct((8, width), F32),
            jax.ShapeDtypeStruct((8, ff), F32),
        ),
        in_specs=[ANY, ANY] + [VMEM] * 5,
        out_specs=(VMEM,) * 5,
        scratch_shapes=[
            pltpu.VMEM((2, rows, width), BF),
            pltpu.VMEM((2, rows, ff), BF),
            pltpu.SemaphoreType.DMA((2, 2)),
        ]
        + collect_scratch(rows, width),
        compiler_params=pltpu.CompilerParams(
            collective_id=4, has_side_effects=True, vmem_limit_bytes=56 * MIB
        ),
        cost_estimate=pl.CostEstimate(flops=0, bytes_accessed=MIB, transcendentals=0),
    )(cots, slope, proj, weight, hid, cot, gain)


def branch_kernel(
    own, weight, low, normed, inner_grad, out, heads_grad, weight_grad, fc_grad,
    rows_in, acc, sems, send, recv, local,
):
    _, near, _, _ = place()
    rows, width = own.shape
    meet(near)
    moving = Spread(own, out, send, recv, local)
    tiles = width // FC_TILE

    def fc_tile(t, carry):
        at = pl.ds(pl.multiple_of(t * FC_TILE, FC_TILE), FC_TILE)
        fc_grad[at, :] = transposed(normed[:, at], inner_grad[...]).astype(BF)
        return carry

    done = 0
    for i, (left, right) in enumerate(pairs_of(moving)):
        fetched = fetch(
            (out.at[left], out.at[right]),
            (rows_in.at[pl.ds(0, rows)], rows_in.at[pl.ds(rows, rows)]),
            sems,
        )
        for made in fetched:
            made.wait()
        grads = against(rows_in[...], weight[...]).astype(BF)
        heads_grad[block_rows(left, rows)] = grads[:rows]
        heads_grad[block_rows(right, rows)] = grads[rows:]
        kept = jnp.concatenate(
            [low[block_rows(left, rows), :], low[block_rows(right, rows), :]], axis=0
        )
        for cut in range(0, width, 1024):
            cols = pl.ds(cut, 1024)
            term = transposed(kept, rows_in[:, cols])
            if i == 0:
                acc[:, cols] = term
            elif i < 3:
                acc[:, cols] += term
            else:
                weight_grad[:, cols] = (acc[:, cols] + term).astype(BF)
        more = (3 * tiles // 8, 3 * tiles // 4, tiles, tiles)[i]
        lax.fori_loop(done, more, fc_tile, 0)
        done = more


def branch_spread(own, weight, low, normed, inner_grad, plane):
    rows, width = own.shape
    share, ff = weight.shape[0], inner_grad.shape[1]
    return pl.pallas_call(
        branch_kernel,
        name="branch_spread",
        out_shape=(
            jax.ShapeDtypeStruct((plane, rows, width), BF),
            jax.ShapeDtypeStruct((plane * rows, share), BF),
            jax.ShapeDtypeStruct((share, width), BF),
            jax.ShapeDtypeStruct((width, ff), BF),
        ),
        in_specs=[VMEM] * 5,
        out_specs=(ANY, VMEM, VMEM, VMEM),
        scratch_shapes=[
            pltpu.VMEM((2 * rows, width), BF),
            pltpu.VMEM((share, width), F32),
            pltpu.SemaphoreType.DMA((2,)),
        ]
        + spread_scratch(),
        compiler_params=pltpu.CompilerParams(
            collective_id=9, has_side_effects=True, vmem_limit_bytes=56 * MIB
        ),
        cost_estimate=pl.CostEstimate(flops=0, bytes_accessed=MIB, transcendentals=0),
    )(own, weight, low, normed, inner_grad)


def inputs_kernel(
    n_blk, order, act, weight, tok, grad_hidden, gain, result, sums, out, result_out,
    total, to_twin, from_twin, mine, in_x, in_y, c_send, c_recv, own,
    send, recv, local, r_send, r_recv, r_local,
):
    _, near, _, _ = place()
    rows = total.shape[0]
    meet(list(near) + blk_peers(n_blk))
    leaving = return_rows(result, result_out, n_blk, r_send, r_recv, r_local)

    def multiply(block, cols):
        return against(rows_of(act, block, rows), weight[cols, :])

    run(collect(multiply, total, to_twin, from_twin, mine, in_x, in_y, c_send, c_recv))
    sums[...] = jnp.zeros_like(sums)
    inner, outer, lanes = order[1], order[0], order[2]

    def chunk(at):
        grad = reorder(total[at], inner, outer, lanes)
        back, by_gain = norm_back(grad, tok[at].astype(F32), gain[...])
        own[at] = (grad_hidden[at] + back).astype(BF)
        sums[0:1] += row_sum(by_gain)
        sums[1:2] += row_sum(grad)

    each_chunk(rows, chunk)
    leaving += return_rows(own, out, n_blk, send, recv, local)
    for made in leaving:
        made.wait()


def inputs_return(act, weight, tok, grad_hidden, gain, result, n_blk, order):
    rows, width = tok.shape
    back = jax.ShapeDtypeStruct((n_blk, rows // n_blk, width), BF)
    moves = [
        pltpu.SemaphoreType.DMA((n_blk - 1,)),
        pltpu.SemaphoreType.DMA((n_blk - 1,)),
        pltpu.SemaphoreType.DMA,
    ]
    return pl.pallas_call(
        functools.partial(inputs_kernel, n_blk, order),
        name="inputs_return",
        out_shape=(jax.ShapeDtypeStruct((8, width), F32), back, back),
        in_specs=[VMEM] * 5 + [ANY],
        out_specs=(VMEM, ANY, ANY),
        scratch_shapes=collect_scratch(rows, width) + [pltpu.VMEM((rows, width), BF)] + moves * 2,
        compiler_params=pltpu.CompilerParams(
            collective_id=6, has_side_effects=True, vmem_limit_bytes=40 * MIB
        ),
        cost_estimate=pl.CostEstimate(flops=0, bytes_accessed=MIB, transcendentals=0),
    )(act, weight, tok, grad_hidden, gain, result)


def weight_kernel(left, right, mixed, out):
    wide = right.shape[1]
    share = out.shape[1] - wide
    pieces = left.shape[1] // share
    rows = mixed.shape[1]

    def tile(t, carry):
        at = pl.ds(pl.multiple_of(t * FC_TILE, FC_TILE), FC_TILE)
        out[at, :wide] = transposed(left[:, at], right[...]).astype(BF)
        return carry

    lax.fori_loop(0, out.shape[0] // FC_TILE, tile, 0)
    for b in range(mixed.shape[0]):
        for j in range(pieces):
            at = (b * pieces + j) * rows
            out[at : at + rows, wide:] = mixed[b, :, j * share : (j + 1) * share]


def weight_grad(left, right, mixed):
    width = left.shape[1]
    return pl.pallas_call(
        weight_kernel,
        name="weight_grad",
        out_shape=jax.ShapeDtypeStruct((width, 4 * right.shape[1] // 3), BF),
        in_specs=[VMEM] * 3,
        out_specs=VMEM,
        compiler_params=pltpu.CompilerParams(vmem_limit_bytes=32 * MIB),
        cost_estimate=pl.CostEstimate(flops=0, bytes_accessed=MIB, transcendentals=0),
    )(left, right, mixed)


def end_kernel(
    sizes, qkv_ref, fc_ref, small_ref, gq, gk, gv, fc, small,
    gathered, partial, arrived, blk_send, blk_recv, plane_send, plane_recv, local,
):
    n_seq, n_blk, n_uly, runs = sizes
    (s, b, u), _, (_, _, _, me), _ = place()
    plane = n_seq * n_uly
    pieces = 3 + runs
    others = [(me + j) % plane for j in range(1, plane)]
    friends = [(p // n_uly, b, p % n_uly) for p in others]
    column = blk_peers(n_blk)
    meet(friends + column)
    by_blk = sender(blk_send, blk_recv)
    by_plane = sender(plane_send, plane_recv)

    def at_home(i, source, target, _):
        made = pltpu.make_async_copy(source, target, local.at[i])
        made.start()
        return made

    sources, targets = (qkv_ref, fc_ref), (gq, gk, gv, fc)
    first = at_home(0, small_ref.at[me], gathered.at[me], None)
    vectors, started = [], []
    for j, (p, peer) in enumerate(zip(others, friends)):
        slot = pieces * (plane - 1) + j
        vectors.append(by_plane(slot, small_ref.at[p], gathered.at[me], peer))
    for j, (p, peer) in enumerate(zip(others, friends)):
        started += exchange_columns(
            by_plane, pieces * j, targets, sources, p, me, peer, sizes, False
        )
    started += exchange_columns(at_home, 2, targets, sources, me, me, None, sizes, False)
    first.wait()
    for made in vectors:
        made.wait()
    partial[...] = jnp.sum(gathered[...], axis=0)
    own = at_home(1, partial.at[b], arrived.at[b], None)
    sent = [
        by_blk(j, partial.at[peer[1]], arrived.at[b], peer) for j, peer in enumerate(column)
    ]
    own.wait()
    for made in sent:
        made.wait()
    small[...] = jnp.sum(arrived[...], axis=0)
    for made in started:
        made.wait()


def finish(qkv, fc, small, sizes):
    n_seq, n_blk, n_uly, runs = sizes
    plane = n_seq * n_uly
    rows, share = qkv.shape[1], qkv.shape[2] // 4
    tail = small.shape[2:]
    pieces = (4 + runs) * (plane - 1)
    whole = jax.ShapeDtypeStruct((rows, plane * share), BF)
    return pl.pallas_call(
        functools.partial(end_kernel, sizes),
        name="finish",
        out_shape=(
            whole,
            whole,
            whole,
            jax.ShapeDtypeStruct((rows, plane * fc.shape[2]), BF),
            jax.ShapeDtypeStruct(tail, small.dtype),
        ),
        in_specs=[ANY] * 3,
        out_specs=(ANY, ANY, ANY, ANY, VMEM),
        scratch_shapes=[
            pltpu.VMEM((plane, n_blk) + tail, F32),
            pltpu.VMEM((n_blk,) + tail, F32),
            pltpu.VMEM((n_blk,) + tail, F32),
            pltpu.SemaphoreType.DMA((n_blk - 1,)),
            pltpu.SemaphoreType.DMA((n_blk - 1,)),
            pltpu.SemaphoreType.DMA((pieces,)),
            pltpu.SemaphoreType.DMA((pieces,)),
            pltpu.SemaphoreType.DMA((5 + runs,)),
        ],
        compiler_params=pltpu.CompilerParams(
            collective_id=7, has_side_effects=True, vmem_limit_bytes=16 * MIB
        ),
        cost_estimate=pl.CostEstimate(flops=0, bytes_accessed=MIB, transcendentals=0),
    )(qkv, fc, small)


def on_device(
    inputs,
    doc_lengths,
    ln1_gain,
    ln1_shift,
    w_query,
    b_query,
    w_key,
    w_value,
    b_value,
    w_out,
    b_out,
    ln2_gain,
    ln2_shift,
    w_fc,
    b_fc,
    w_proj,
    b_proj,
    cotangent,
):
    seqs, tok, width = inputs.shape
    n_seq, n_blk, n_uly = (lax.axis_size(a) for a in ALL)
    plane = n_seq * n_uly
    here_seq, here_blk, here_uly = (lax.axis_index(a) for a in ALL)
    here = here_seq * n_uly + here_uly
    scale = 1.0 / math.sqrt(HD)
    rows = w_query.shape[0]
    hidden_rows = w_proj.shape[0]
    share = width // plane
    heads = share // HD
    ff_share = hidden_rows * n_blk
    sharing = max(1, n_blk // seqs)
    held = seqs * sharing // n_blk
    part = tok // sharing
    n_rows = n_blk * held * part
    order = (n_seq, n_blk, n_uly * rows)

    def by_plane(block):
        block = block.reshape(n_blk // sharing, held, sharing, part, width)
        return block.transpose(0, 2, 1, 3, 4).reshape(n_blk, held * part, width)

    def from_plane(block):
        block = block.reshape(n_blk // sharing, sharing, held, part, width)
        return block.transpose(0, 2, 1, 3, 4).reshape(seqs, tok, width)

    vectors = (ln1_gain, ln1_shift, b_query, b_value, b_out, ln2_gain, ln2_shift, b_proj)
    vectors += (b_fc, doc_lengths.reshape(-1))
    runs = n_blk if hidden_rows % 128 == 0 else 1
    sizes = (n_seq, n_blk, n_uly, runs)
    by_block = (rows, n_seq, n_blk, n_uly, hidden_rows)
    by_device = (rows, n_seq, n_uly, n_blk, hidden_rows)
    if runs == 1:
        w_fc = w_fc.reshape(by_block).transpose(0, 1, 3, 2, 4).reshape(rows, -1)
    tokens, qkv, fc, small = enter(
        by_plane(inputs), (w_query, w_key, w_value), w_fc, [v.reshape(1, -1) for v in vectors], sizes
    )
    tokens = tokens.reshape(n_rows, width)

    def over_blk(matrix):
        return lax.all_gather(matrix, "blk", axis=0, tiled=True)

    qkv = over_blk(qkv.reshape(plane * rows, 3 * share))
    small = small.reshape(n_seq, n_uly, n_blk, SMALL, 128)
    flat = small[:, :, :, :8, :rows].transpose(3, 0, 2, 1, 4).reshape(8, 1, width)
    whole = [flat[i] for i in range(8)]
    lanes = min(128, hidden_rows)
    bias_fc = lax.dynamic_slice(
        small, (here_seq, here_uly, 0, 8, 0), (1, 1, n_blk, hidden_rows // lanes, lanes)
    ).reshape(1, ff_share)
    lengths = small[:, 0, 0, SMALL - 1, : doc_lengths.size].astype(jnp.int32)
    lengths = lengths.reshape(n_seq, *doc_lengths.shape)
    gain_one, shift_one, bias_q, bias_v, bias_out, gain_two, shift_two, bias_proj = whole
    mine = lambda v: lax.dynamic_slice(v, (0, here * share), (1, share))
    bias_q, bias_v = mine(bias_q), mine(bias_v)

    normed, grad_out = norm_gather(
        tokens, gain_one, shift_one, by_plane(cotangent), plane, order
    )
    normed, w_out, fc = lax.optimization_barrier((normed, w_out, fc))
    out_part = over_blk(w_out)
    out_part = out_part.reshape(n_uly, n_blk // n_uly, rows, width)
    out_part = lax.all_to_all(out_part, "uly", split_axis=0, concat_axis=0, tiled=True)
    out_part = out_part.transpose(1, 0, 2, 3).reshape(share, width)
    fc = over_blk(fc.reshape(plane * rows, ff_share))
    normed = normed.reshape(plane * n_rows, width)
    made = product(normed, qkv)
    bias_all = jnp.concatenate([bias_q, jnp.zeros_like(bias_q), bias_v], axis=1)
    scales = jnp.repeat(jnp.array([[scale, 1.0, 1.0]], F32), share, axis=1)
    made = ((made + bias_all) * scales).astype(BF)

    made, w_proj = lax.optimization_barrier((made, w_proj))
    proj = over_blk(w_proj)

    groups = [
        [g * sharing + i for i in range(sharing)] for g in range(n_blk // sharing)
    ]
    pairs = n_seq * held * heads // sharing
    length = n_blk * n_uly * tok
    if sharing == held == 1:
        layout = (n_seq, n_uly, n_blk, part, heads)
    else:
        layout = (pairs, 1, 1, length, 1)

    def to_heads(matrix, kinds):
        if sharing == held == 1:
            return matrix
        matrix = matrix.reshape(n_seq, n_uly, n_blk, held, part, kinds, heads, HD)
        matrix = matrix.transpose(0, 3, 6, 2, 1, 4, 5, 7)
        matrix = matrix.reshape(n_seq * held * heads, n_blk, n_uly, 1, part, kinds * HD)
        if sharing > 1:
            matrix = lax.all_to_all(
                matrix, "blk", split_axis=0, concat_axis=3, axis_index_groups=groups, tiled=True
            )
        return matrix.reshape(pairs * length, kinds * HD)

    def from_heads(matrix, kinds):
        if sharing == held == 1:
            return matrix
        matrix = matrix.reshape(pairs, n_blk, n_uly, sharing, part, kinds * HD)
        if sharing > 1:
            matrix = lax.all_to_all(
                matrix, "blk", split_axis=3, concat_axis=0, axis_index_groups=groups, tiled=True
            )
        matrix = matrix.reshape(n_seq, held, heads, n_blk, n_uly, part, kinds, HD)
        matrix = matrix.transpose(0, 4, 3, 1, 5, 6, 2, 7)
        return matrix.reshape(plane * n_rows, kinds * share)

    turn = here_blk % sharing
    pair_at = turn * pairs + jnp.arange(layout[0]) * layout[4]
    seq_of = pair_at // (held * heads)
    held_of = (pair_at // heads) % held
    which = (here_blk // sharing) * held + held_of
    own_lengths = lengths[seq_of, which]
    first = own_lengths[:, 0:1]
    bounds = jnp.concatenate([first, first + own_lengths[:, 1:2]], axis=1).reshape(-1)

    attended_low, natural, attended, logs, grad_all = attend(
        bounds, to_heads(made, 3), grad_out, plane, layout
    )
    attended_low = from_heads(attended_low, 1)
    hidden, own_two = hidden_norm(
        attended_low, out_part, tokens, bias_out, gain_two, shift_two, order
    )
    normed_two, active, slope, grad_proj = feed(own_two, fc, bias_fc, grad_all)

    def sum_blk(matrix):
        return lax.psum_scatter(matrix, "blk", scatter_dimension=0, tiled=True)

    grad_w_proj = sum_blk(grad_proj).astype(F32)
    inner_grad, grad_hidden, branch, sums_two, sums_fc = back_feed(
        grad_all, slope, proj, fc, hidden, grad_out, gain_two, order
    )
    _, grad_heads, grad_w_out, grad_fc = branch_spread(
        branch, out_part, attended_low, normed_two.reshape(plane * n_rows, width), inner_grad, plane
    )
    grad_b_fc = sums_fc[0]
    grad_fc = sum_blk(grad_fc)
    grad_w_out = grad_w_out.reshape(n_blk // n_uly, n_uly, rows, width).transpose(1, 0, 2, 3)
    grad_w_out = grad_w_out.reshape(n_uly, n_blk // n_uly * rows, width)
    grad_heads, grad_w_proj = lax.optimization_barrier((grad_heads, grad_w_proj))
    grad_heads = to_heads(grad_heads, 1)
    backs, result, grad_w_out = attend_back(
        bounds,
        grad_heads,
        natural,
        attended,
        logs,
        active,
        proj,
        hidden,
        bias_proj,
        grad_w_out,
        layout,
        scale,
    )
    backs = from_heads(backs, 3)
    grad_bias = jnp.sum(backs.astype(F32), axis=0)
    grads = weight_grad(normed, backs, grad_w_out.reshape(n_blk, rows, width))
    grads = sum_blk(grads).reshape(plane, rows, 4 * share)
    grad_w_out = grads[:, :, 3 * share :].transpose(1, 0, 2).reshape(rows, width).astype(F32)
    last, grad_fc = lax.optimization_barrier((backs, grad_fc))
    sums_one, grad_inputs, result = inputs_return(
        last, qkv, tokens, grad_hidden, gain_one, result, n_blk, order
    )

    def widened(vector):
        return lax.dynamic_update_slice(jnp.zeros((width,), F32), vector, (here * share,))

    parts = (
        sums_one[0],
        sums_one[1],
        widened(grad_bias[:share]),
        widened(grad_bias[2 * share :]),
        sums_two[2],
        sums_two[0],
        sums_two[1],
        sums_two[3],
    )
    wide_fc = lax.dynamic_update_slice(
        jnp.zeros((n_seq, n_blk, n_uly, hidden_rows), F32),
        grad_b_fc.reshape(1, n_blk, 1, hidden_rows),
        (here_seq, 0, here_uly, 0),
    )
    sums = jnp.concatenate(
        [p.reshape(n_seq, n_blk, n_uly, rows) for p in parts] + [wide_fc], axis=3
    )
    used = sums.shape[3]
    end_lanes = -(-used // 1024) * 8
    sums = jnp.pad(sums, ((0, 0),) * 3 + ((0, end_lanes * 128 - used),))
    sums = sums.transpose(0, 2, 1, 3).reshape(plane, n_blk, end_lanes, 128)
    *grad_qkv, grad_fc, sums = finish(
        grads,
        grad_fc.reshape(plane, rows, ff_share),
        sums,
        sizes,
    )
    grad_qkv = [g.astype(F32) for g in grad_qkv]
    if runs == 1:
        grad_fc = grad_fc.reshape(by_device).transpose(0, 1, 3, 2, 4).reshape(rows, -1)
    grad_fc = grad_fc.astype(F32)
    sums = sums.reshape(-1)
    each = [sums[i * rows : (i + 1) * rows] for i in range(8)]
    return (
        from_plane(result),
        from_plane(grad_inputs),
        each[0],
        each[1],
        grad_qkv[0],
        each[2],
        grad_qkv[1],
        grad_qkv[2],
        each[3],
        grad_w_out,
        each[4],
        each[5],
        each[6],
        grad_fc,
        sums[8 * rows : used],
        grad_w_proj,
        each[7],
    )


def solution(mesh):
    tokens = P("seq", ("blk", "uly"), None)
    vector = P(ALL)
    matrix = P(ALL, None)
    return jax.shard_map(
        on_device,
        mesh=mesh,
        in_specs=(
            tokens, P("seq", None), vector, vector, matrix, vector, matrix, matrix, vector,
            matrix, vector, vector, vector, matrix, vector, matrix, vector, tokens,
        ),
        out_specs=(
            tokens, tokens, vector, vector, matrix, vector, matrix, matrix, vector,
            matrix, vector, vector, vector, matrix, vector, matrix, vector,
        ),
        check_vma=False,
    )
```

```python
import functools
import math

import jax
import jax.numpy as jnp
from jax import lax
from jax.experimental import pallas as pl
from jax.experimental.pallas import tpu as pltpu
from jax.sharding import PartitionSpec as P

HD = 128
EPS = 1e-05
NEGATIVE = -1e30
ALL = ("seq", "blk", "uly")
PLANE = ("seq", "uly")
BF = jnp.bfloat16
F32 = jnp.float32
MESH = pl.DeviceIdType.MESH
ANY = pl.BlockSpec(memory_space=pl.ANY)
VMEM = pl.BlockSpec(memory_space=pltpu.VMEM)
MIB = 2**20
GRANT = 60 * MIB
CHUNK = 16
TILE = 2048


def gelu_tanh(values):
    return jax.nn.gelu(values, approximate=True)


def product(left_side, right_side):
    return jnp.dot(left_side, right_side, preferred_element_type=F32)


def transposed(left_side, right_side):
    return lax.dot_general(
        left_side, right_side, (((0,), (0,)), ((), ())), preferred_element_type=F32
    )


def against(left_side, right_side):
    return lax.dot_general(
        left_side, right_side, (((1,), (1,)), ((), ())), preferred_element_type=F32
    )


def meet(peers):
    barrier = pltpu.get_barrier_semaphore()
    for peer in peers:
        pl.semaphore_signal(barrier, inc=1, device_id=peer, device_id_type=MESH)
    pl.semaphore_wait(barrier, len(peers))


def sender(send, recv):
    def copy(i, source, target, device):
        made = pltpu.make_async_remote_copy(
            src_ref=source,
            dst_ref=target,
            send_sem=send.at[i],
            recv_sem=recv.at[i],
            device_id=device,
            device_id_type=MESH,
        )
        made.start()
        return made

    return copy


def place():
    s, b, u = (lax.axis_index(a) for a in ALL)
    a, c = u // 2, u % 2
    beside = (s, b, 2 * (1 - a) + c)
    across = (1 - s, b, u)
    twin = (s, b, 2 * a + 1 - c)

    def blocks(core):
        own = 4 * s + 2 * a + core
        on_x = 4 * s + 2 * (1 - a) + core
        on_y = 4 * (1 - s) + 2 * a + core
        diagonal = 4 * (1 - s) + 2 * (1 - a) + core
        return diagonal, on_x, on_y, own

    return (s, b, u), (beside, across, twin), blocks(c), blocks(1 - c)


class Spread:
    def __init__(self, own, out, send, recv, local):
        _, self.near_by, self.blocks, self.twins = place()
        beside, across, twin = self.near_by
        me = self.blocks[3]
        half = own.shape[0] // 2
        self.out, self.parts = out, (pl.ds(0, half), pl.ds(half, half))
        self.copy = copy = sender(send, recv)
        p0, p1 = self.parts
        self.x0 = copy(0, own.at[p0], out.at[me, p0], beside)
        self.y1 = copy(1, own.at[p1], out.at[me, p1], across)
        self.x1 = copy(2, own.at[p1], out.at[me, p1], beside)
        self.y0 = copy(3, own.at[p0], out.at[me, p0], across)
        self.own_twin = copy(4, own, out.at[me], twin)
        self.started = [self.x0, self.y1, self.x1, self.y0, self.own_twin]
        self.kept = pltpu.make_async_copy(own, out.at[me], local)
        self.kept.start()

    def pass_on(self, i, block, part, device):
        at = self.out.at[block, self.parts[part]]
        made = self.copy(i, at, at, device)
        self.started.append(made)
        return made

    def own_blocks(self):
        self.kept.wait()
        self.own_twin.wait_recv()

    def first_halves(self):
        beside, across, twin = self.near_by
        _, on_x, on_y, _ = self.blocks
        self.x0.wait_recv()
        self.d0 = self.pass_on(5, on_x, 0, across)
        self.t0 = self.pass_on(6, on_x, 0, twin)
        self.y1.wait_recv()
        self.d1 = self.pass_on(7, on_y, 1, beside)
        self.t1 = self.pass_on(8, on_y, 1, twin)

    def second_halves(self):
        _, _, twin = self.near_by
        _, on_x, on_y, _ = self.blocks
        self.x1.wait_recv()
        self.t2 = self.pass_on(9, on_x, 1, twin)
        self.y0.wait_recv()
        self.t3 = self.pass_on(10, on_y, 0, twin)

    def twin_sides(self):
        for made in (self.t0, self.t1, self.t2, self.t3):
            made.wait_recv()

    def diagonals(self):
        _, _, twin = self.near_by
        diag = self.blocks[0]
        self.d0.wait_recv()
        t4 = self.pass_on(11, diag, 0, twin)
        self.d1.wait_recv()
        t5 = self.pass_on(12, diag, 1, twin)
        t4.wait_recv()
        t5.wait_recv()

    def close(self):
        for made in self.started:
            made.wait_send()


def spread(own, out, send, recv, local):
    moving = Spread(own, out, send, recv, local)
    yield
    moving.first_halves()
    yield
    moving.second_halves()
    yield
    moving.own_blocks()
    moving.twin_sides()
    moving.diagonals()
    moving.close()


def run(steps):
    for _ in steps:
        pass


SPREAD = 13


class ChipSums:
    def __init__(self, multiply, total, to_twin, from_twin, mine, send, recv, prepare=None):
        _, (_, _, self.twin), self.here, self.other = place()
        self.multiply, self.prepare = multiply, prepare or (lambda block: None)
        self.total, self.mine = total, mine
        self.to_twin, self.from_twin = to_twin, from_twin
        self.copy = sender(send, recv)
        self.sent = []

    def each_tile(self, body):
        def step(t, carry):
            body(pl.ds(pl.multiple_of(t * TILE, TILE), TILE))
            return carry

        lax.fori_loop(0, self.total.shape[1] // TILE, step, 0)

    def for_twin(self, k):
        def term(cols):
            self.to_twin[k, :, cols] = self.multiply(self.other[k], cols).astype(BF)

        self.prepare(self.other[k])
        self.each_tile(term)
        self.sent.append(self.copy(k, self.to_twin.at[k], self.from_twin.at[k], self.twin))

    def for_here(self, k):
        def term(cols):
            both = self.multiply(self.here[k], cols) + self.from_twin[k, :, cols].astype(F32)
            if k < 3:
                self.mine[k, :, cols] = both.astype(BF)
            else:
                self.total[:, cols] = both

        self.prepare(self.here[k])
        self.sent[k].wait_recv()
        self.each_tile(term)

    def close(self):
        for made in self.sent:
            made.wait_send()


class Cross:
    def __init__(self, total, mine, in_x, in_y, send, recv, cut=None):
        _, (self.beside, self.across, _), _, _ = place()
        self.total, self.mine, self.in_x, self.in_y = total, mine, in_x, in_y
        rows = total.shape[0]
        self.cut = cut or rows // 2
        self.rest = rows - self.cut
        self.parts = (pl.ds(0, self.cut), pl.ds(self.cut, self.rest))
        self.copy = sender(send, recv)
        self.started = []

    def to_x(self, i, k, part, slot):
        rows = (self.cut, self.rest)[part]
        target = self.in_x.at[slot, pl.ds(0, rows)]
        return self.copy(i, self.mine.at[k, self.parts[part]], target, self.beside)

    def to_y(self, i, k, part, slot):
        rows = (self.cut, self.rest)[part]
        target = self.in_y.at[slot, pl.ds(0, rows)]
        return self.copy(i, self.mine.at[k, self.parts[part]], target, self.across)

    def begin(self, k):
        if k == 0:
            self.dx = self.to_x(4, 0, 0, 0)
            self.dy = self.to_y(5, 0, 1, 0)
        elif k == 1:
            self.started.append(self.to_x(6, 1, 0, 1))
        else:
            self.started.append(self.to_y(7, 2, 1, 1))

    def add(self, k, first, rows, arrived):
        def step(t, carry):
            at = pl.ds(pl.multiple_of(t * CHUNK, CHUNK), CHUNK)
            to = pl.ds(pl.multiple_of(first + t * CHUNK, CHUNK), CHUNK)
            both = self.mine[k, to].astype(F32) + arrived[0, at].astype(F32)
            self.mine[k, to] = both.astype(BF)
            return carry

        lax.fori_loop(0, rows // CHUNK, step, 0)

    def diagonals(self):
        self.dy.wait_recv()
        self.add(1, self.cut, self.rest, self.in_y)
        self.started.append(self.to_x(8, 1, 1, 2))
        self.dx.wait_recv()
        self.add(2, 0, self.cut, self.in_x)
        self.started.append(self.to_y(9, 2, 0, 2))

    def finish(self):
        total, in_x, in_y = self.total, self.in_x, self.in_y
        for made in self.started:
            made.wait_recv()

        def add(first, rows, x_slot, y_slot):
            def step(t, carry):
                at = pl.ds(pl.multiple_of(t * CHUNK, CHUNK), CHUNK)
                to = pl.ds(pl.multiple_of(first + t * CHUNK, CHUNK), CHUNK)
                total[to] += in_x[x_slot, at].astype(F32) + in_y[y_slot, at].astype(F32)
                return carry

            lax.fori_loop(0, rows // CHUNK, step, 0)

        add(0, self.cut, 1, 2)
        add(self.cut, self.rest, 2, 1)
        for made in self.started + [self.dx, self.dy]:
            made.wait_send()


def collect(
    multiply, total, to_twin, from_twin, mine, in_x, in_y, send, recv, prepare=None
):
    chip = ChipSums(multiply, total, to_twin, from_twin, mine, send, recv, prepare)
    cross = Cross(total, mine, in_x, in_y, send, recv)
    chip.for_twin(0)
    for k in range(4):
        if k < 3:
            chip.for_twin(k + 1)
        chip.for_here(k)
        if k < 3:
            cross.begin(k)
    yield
    cross.diagonals()
    yield
    cross.finish()
    chip.close()


COLLECT = 10


def chip_scratch(rows, width):
    return [pltpu.VMEM((4, rows, width), BF)] * 2


def cross_scratch(rows, width, cut=None):
    cut = cut or rows // 2
    return [
        pltpu.VMEM((3, rows, width), BF),
        pltpu.VMEM((3, rows - cut, width), BF),
        pltpu.VMEM((3, rows - cut, width), BF),
        pltpu.SemaphoreType.DMA((COLLECT,)),
        pltpu.SemaphoreType.DMA((COLLECT,)),
    ]


def collect_scratch(rows, width):
    return [pltpu.VMEM((rows, width), F32)] + chip_scratch(rows, width) + cross_scratch(rows, width)


def reorder(values, outer, inner, lanes):
    return jnp.concatenate(
        [
            values[:, (o * inner + i) * lanes : (o * inner + i + 1) * lanes]
            for i in range(inner)
            for o in range(outer)
        ],
        axis=1,
    )


def norm_parts(values):
    average = jnp.mean(values, axis=-1, keepdims=True)
    centred = values - average
    variance = jnp.mean(centred * centred, axis=-1, keepdims=True)
    spread_back = lax.rsqrt(variance + EPS)
    return centred * spread_back, spread_back


def norm_back(grad, values, gain):
    unit, spread_back = norm_parts(values)
    scaled = grad * gain
    back = spread_back * (
        scaled
        - jnp.mean(scaled, axis=-1, keepdims=True)
        - unit * jnp.mean(scaled * unit, axis=-1, keepdims=True)
    )
    return back, grad * unit


def each_chunk(rows, body):
    def step(t, carry):
        body(pl.ds(pl.multiple_of(t * CHUNK, CHUNK), CHUNK))
        return carry

    lax.fori_loop(0, rows // CHUNK, step, 0)


def row_sum(values):
    return jnp.sum(values, axis=0, keepdims=True)


def return_rows(block, out, n_blk, send, recv, local):
    (s, b, u), _, _, _ = place()
    count = block.shape[0] // n_blk
    copy = sender(send, recv)
    started = []
    for j in range(1, n_blk):
        to = (b + j) % n_blk
        rows = pl.ds(pl.multiple_of(to * count, count), count)
        started.append(copy(j - 1, block.at[rows], out.at[b], (s, to, u)))
    rows = pl.ds(pl.multiple_of(b * count, count), count)
    kept = pltpu.make_async_copy(block.at[rows], out.at[b], local)
    kept.start()
    return started + [kept]


def blk_peers(n_blk):
    (s, b, u), _, _, _ = place()
    return [(s, (b + j) % n_blk, u) for j in range(1, n_blk)]


def projection_spans(whole, cut, owner, sizes):
    plane = sizes[0] * sizes[2]
    share = whole[0].shape[1] // plane
    at = pl.ds(pl.multiple_of(owner * share, share), share)
    return [(matrix, at, cut, pl.ds(i * share, share)) for i, matrix in enumerate(whole)]


def feed_spans(matrix, cut, owner, sizes):
    n_seq, _, n_uly, runs = sizes
    share = matrix.shape[1] // (n_seq * n_uly * runs)
    spans = []
    for r in range(runs):
        at = ((owner // n_uly) * runs + r) * n_uly + owner % n_uly
        at = pl.ds(pl.multiple_of(at * share, share), share)
        spans.append((matrix, at, cut, pl.ds(r * share, share)))
    return spans


def gather_columns(copy, first, spans, me, device):
    return [
        copy(first + i, matrix.at[:, at], cut.at[me, :, inside], device)
        for i, (matrix, at, cut, inside) in enumerate(spans)
    ]


def return_columns(copy, first, spans, p, device):
    return [
        copy(first + i, cut.at[p, :, inside], matrix.at[:, at], device)
        for i, (matrix, at, cut, inside) in enumerate(spans)
    ]


def plane_peers(plane):
    (s, b, u), _, (_, _, _, me), _ = place()
    n_uly = plane // 2
    others = [(me + j) % plane for j in range(1, plane)]
    return me, [(p, (p // n_uly, b, p % n_uly)) for p in others]


def home(local):
    def copy(i, source, target, _):
        made = pltpu.make_async_copy(source, target, local.at[i])
        made.start()
        return made

    return copy


def entry_kernel(
    sizes, x_ref, wq_ref, wk_ref, wv_ref, fc_ref, *refs
):
    vectors, (bias_ref, lengths_ref), refs = refs[:8], refs[8:10], refs[10:]
    matrices = (wq_ref, wk_ref, wv_ref)
    enter_body(sizes, x_ref, matrices, fc_ref, vectors, bias_ref, lengths_ref, *refs)


def enter_body(
    sizes, x_ref, matrices, fc_ref, short, bias_ref, lengths_ref, tok, qkv, fc, small,
    small_ref, blk_send, blk_recv, plane_send, plane_recv, local,
):
    n_seq, n_blk, n_uly, runs = sizes
    (s, b, u), _, (_, _, _, me), _ = place()
    plane = n_seq * n_uly
    pieces = 3 + runs
    small_ref[...] = jnp.zeros_like(small_ref)
    for i, ref in enumerate(short):
        small_ref[i : i + 1, : ref.shape[1]] = ref[...].astype(F32)
    lanes = min(128, bias_ref.shape[1])
    for i in range(bias_ref.shape[1] // lanes):
        part = bias_ref[:, i * lanes : (i + 1) * lanes].astype(F32)
        small_ref[8 + i : 9 + i, :lanes] = part
    small_ref[SMALL - 1 :, : lengths_ref.shape[1]] = lengths_ref[...].astype(F32)
    me, friends = plane_peers(plane)
    column = blk_peers(n_blk)
    meet([peer for _, peer in friends] + column)
    by_blk = sender(blk_send, blk_recv)
    by_plane = sender(plane_send, plane_recv)
    at_home = home(local)

    def spans(owner):
        return projection_spans(matrices, qkv, owner, sizes) + feed_spans(fc_ref, fc, owner, sizes)

    first = at_home(0, small_ref, small.at[me, b], None)
    vectors, started = [], []
    for j, peer in enumerate(column):
        vectors.append(by_blk(j, small_ref, small.at[me, b], peer))
    for j, peer in enumerate(column):
        started.append(by_blk(n_blk - 1 + j, x_ref.at[peer[1]], tok.at[b], peer))
    for j, (p, peer) in enumerate(friends):
        started += gather_columns(by_plane, pieces * j, spans(p), me, peer)
    started.append(at_home(1, x_ref.at[b], tok.at[b], None))
    started += gather_columns(at_home, 2, spans(me), me, None)
    first.wait()
    for made in vectors:
        made.wait()
    for j, (_, peer) in enumerate(friends):
        at = small.at[me]
        started.append(by_plane(pieces * (plane - 1) + j, at, at, peer))
    for made in started:
        made.wait()


SMALL = 16


def enter(x, weights, fc, short, sizes):
    n_seq, n_blk, n_uly, runs = sizes
    plane = n_seq * n_uly
    rows, width = weights[0].shape
    pieces = (4 + runs) * (plane - 1)
    return pl.pallas_call(
        functools.partial(entry_kernel, sizes),
        name="enter",
        out_shape=(
            jax.ShapeDtypeStruct(x.shape, x.dtype),
            jax.ShapeDtypeStruct((plane, rows, 3 * width // plane), BF),
            jax.ShapeDtypeStruct((plane, rows, fc.shape[1] // plane), BF),
            jax.ShapeDtypeStruct((plane, n_blk, SMALL, 128), F32),
        ),
        in_specs=[ANY] * 5 + [VMEM] * len(short),
        out_specs=(ANY,) * 4,
        scratch_shapes=[
            pltpu.VMEM((SMALL, 128), F32),
            pltpu.SemaphoreType.DMA((2 * (n_blk - 1),)),
            pltpu.SemaphoreType.DMA((2 * (n_blk - 1),)),
            pltpu.SemaphoreType.DMA((pieces,)),
            pltpu.SemaphoreType.DMA((pieces,)),
            pltpu.SemaphoreType.DMA((5 + runs,)),
        ],
        compiler_params=pltpu.CompilerParams(
            collective_id=0, has_side_effects=True, vmem_limit_bytes=GRANT
        ),
        cost_estimate=pl.CostEstimate(flops=0, bytes_accessed=MIB, transcendentals=0),
    )(x, *weights, fc, *short)


def norm_kernel(
    order, n_blk, tok, gain, shift, cot_ref, out, cot, cots,
    own, send, recv, local, c_send, c_recv, c_local, g_send, g_recv, kept,
):
    (s, b, u), near, _, _ = place()
    column = blk_peers(n_blk)
    meet(list(near) + column)
    copy = sender(g_send, g_recv)
    count = cot_ref.shape[1]
    rows = pl.ds(pl.multiple_of(b * count, count), count)
    exchanged = [copy(j, cot_ref.at[peer[1]], cot.at[rows], peer) for j, peer in enumerate(column)]
    exchanged.append(home(kept)(0, cot_ref.at[b], cot.at[rows], None))

    def chunk(at):
        unit, _ = norm_parts(tok[at].astype(F32))
        own[at] = reorder(unit * gain[...] + shift[...], *order).astype(BF)

    each_chunk(own.shape[0], chunk)
    run(spread(own, out, send, recv, local))
    for made in exchanged:
        made.wait()
    run(spread(cot, cots, c_send, c_recv, c_local))


def norm_gather(tok, gain, shift, cot, plane, order):
    rows, width = tok.shape
    n_blk = cot.shape[0]
    return pl.pallas_call(
        functools.partial(norm_kernel, order, n_blk),
        name="norm_gather",
        out_shape=(
            jax.ShapeDtypeStruct((plane, rows, width), BF),
            jax.ShapeDtypeStruct((rows, width), BF),
            jax.ShapeDtypeStruct((plane, rows, width), BF),
        ),
        in_specs=[VMEM] * 3 + [ANY],
        out_specs=(ANY, ANY, ANY),
        scratch_shapes=[pltpu.VMEM((rows, width), BF)]
        + spread_scratch() * 2
        + [
            pltpu.SemaphoreType.DMA((n_blk - 1,)),
            pltpu.SemaphoreType.DMA((n_blk - 1,)),
            pltpu.SemaphoreType.DMA((1,)),
        ],
        compiler_params=pltpu.CompilerParams(
            collective_id=1, has_side_effects=True, vmem_limit_bytes=GRANT
        ),
        cost_estimate=pl.CostEstimate(flops=0, bytes_accessed=MIB, transcendentals=0),
    )(tok, gain, shift, cot)


BLOCK = 256


def document_start(bounds, s, position):
    first, second = bounds[2 * s], bounds[2 * s + 1]
    return jnp.where(position >= second, second, jnp.where(position >= first, first, 0))


def chunks_of(layout):
    n_seq, n_uly, n_blk, part, _ = layout
    for s in range(n_seq):
        for b in range(n_blk):
            for u in range(n_uly):
                yield ((s * n_uly + u) * n_blk + b) * part, s, (b * n_uly + u) * part


def attend_kernel(
    layout, bounds, qkv, mixed, low, natural, attended, logs, mixed_out, u_send, u_recv, u_local
):
    _, _, _, part, heads = layout
    meet(row_peers(mixed.shape[0]))
    mixing = mix_row(mixed, mixed_out, u_send, u_recv, u_local)
    share = heads * HD
    pairs, length = natural.shape[1:3]
    for row, s, position in chunks_of(layout):
        for kind in range(3):
            for h in range(heads):
                lane = kind * share + h * HD
                natural[kind, s * heads + h, position : position + part] = qkv[
                    row : row + part, lane : lane + HD
                ]

    def pair(p, carry):
        for start in range(0, length, BLOCK):
            stop = start + BLOCK
            scores = against(natural[0, p, start:stop], natural[1, p, :stop])
            row = start + lax.broadcasted_iota(jnp.int32, (BLOCK, 1), 0)
            key = lax.broadcasted_iota(jnp.int32, (BLOCK, stop), 1)
            allowed = (key >= document_start(bounds, p // heads, row)) & (key <= row)
            scores = jnp.where(allowed, scores, NEGATIVE)
            top = jnp.max(scores, axis=1, keepdims=True)
            powered = jnp.exp(scores - top)
            total = jnp.sum(powered, axis=1, keepdims=True)
            made = product(powered.astype(BF), natural[2, p, :stop])
            attended[p, start:stop] = made / total
            log_total = jnp.broadcast_to(top + jnp.log(total), (BLOCK, HD))
            logs[p, :, start:stop] = log_total.T[:8]
        return carry

    lax.fori_loop(0, pairs, pair, 0)
    for row, s, position in chunks_of(layout):
        for h in range(heads):
            low[row : row + part, h * HD : (h + 1) * HD] = attended[
                s * heads + h, position : position + part
            ].astype(BF)
    for made in mixing:
        made.wait()


def attend(bounds, qkv, mixed, layout):
    n_seq, n_uly, n_blk, part, heads = layout
    pairs, length = n_seq * heads, n_uly * n_blk * part
    return pl.pallas_call(
        functools.partial(attend_kernel, layout),
        name="attend",
        out_shape=(
            jax.ShapeDtypeStruct((qkv.shape[0], heads * HD), BF),
            jax.ShapeDtypeStruct((3, pairs, length, HD), BF),
            jax.ShapeDtypeStruct((pairs, length, HD), F32),
            jax.ShapeDtypeStruct((pairs, 8, length), F32),
            jax.ShapeDtypeStruct(mixed.shape, BF),
        ),
        in_specs=[pl.BlockSpec(memory_space=pltpu.SMEM), VMEM, ANY],
        out_specs=(VMEM, VMEM, VMEM, VMEM, ANY),
        scratch_shapes=mix_scratch(mixed.shape[0]),
        compiler_params=pltpu.CompilerParams(
            collective_id=2, has_side_effects=True, vmem_limit_bytes=GRANT
        ),
        cost_estimate=pl.CostEstimate(flops=0, bytes_accessed=MIB, transcendentals=0),
    )(bounds, qkv, mixed)


def attend_back_kernel(
    layout, scale, fused, bounds, grad, natural, attended, logs, mine_ref, own_ref, hid, bias,
    mixed, normed_ref, back, out, mixed_out, *refs
):
    weights, refs = (refs[0], refs[1:]) if fused else (None, refs)
    (
        grads, grads_back, key_grad, value_grad, mixed_in, normed, n_sems,
        total, mine, in_x, in_y, c_send, c_recv, u_send, u_recv, u_local,
    ) = refs
    (s, b, u), near, _, _ = place()
    rows = total.shape[0]
    _, _, _, part, heads = layout
    share = heads * HD
    first = fetch((mine_ref.at[0], mine_ref.at[1], mine_ref.at[2], own_ref),
                  (mine.at[0], mine.at[1], mine.at[2], total), n_sems)
    if fused:
        loading = pltpu.make_async_copy(normed_ref, normed, n_sems.at[4])
        loading.start()
    meet([near[1]] + row_peers(mixed.shape[0]))
    cross = Cross(total, mine, in_x, in_y, c_send, c_recv, rows // 4)
    for k in range(3):
        first[k].wait()
        cross.begin(k)
    target = mixed_in if fused else mixed_out
    mixing = mix_row(mixed, target, u_send, u_recv, u_local)
    pairs, length = natural.shape[1:3]
    for row, s_at, position in chunks_of(layout):
        for h in range(heads):
            grads[s_at * heads + h, position : position + part] = grad[
                row : row + part, h * HD : (h + 1) * HD
            ]

    def pair(p, carry):
        for start in reversed(range(0, length, BLOCK)):
            stop = start + BLOCK
            query, key, value = (
                natural[0, p, start:stop], natural[1, p, :stop], natural[2, p, :stop]
            )
            above = grads[p, start:stop]
            row = start + lax.broadcasted_iota(jnp.int32, (1, BLOCK), 1)
            at = lax.broadcasted_iota(jnp.int32, (stop, BLOCK), 0)
            allowed = (at >= document_start(bounds, p // heads, row)) & (at <= row)
            scores = jnp.where(allowed, against(key, query), NEGATIVE)
            chances = jnp.exp(scores - logs[p, 0:1, start:stop])
            dots = (above.astype(F32) * attended[p, start:stop]).T
            dots = jnp.sum(dots, axis=0, keepdims=True)
            by_value = product(chances.astype(BF), above)
            scored = (chances * (against(value, above) - dots)).astype(BF)
            by_key = product(scored, query)
            grads_back[p, start:stop] = (transposed(scored, key) * scale).astype(BF)
            if stop == length:
                key_grad[...] = by_key
                value_grad[...] = by_value
            else:
                key_grad[:stop] += by_key
                value_grad[:stop] += by_value
        grads_back[pairs + p] = key_grad[...].astype(BF)
        grads_back[2 * pairs + p] = value_grad[...].astype(BF)
        return carry

    cut = (pairs + 1) // 2
    lax.fori_loop(0, cut, pair, 0)
    cross.diagonals()
    lax.fori_loop(cut, pairs, pair, 0)
    for row, s_at, position in chunks_of(layout):
        for kind in range(3):
            for h in range(heads):
                lane = kind * share + h * HD
                back[row : row + part, lane : lane + HD] = grads_back[
                    kind * pairs + s_at * heads + h, position : position + part
                ]
    for made in mixing:
        made.wait()
    if fused:
        loading.wait()
        weight_terms(normed, back, mixed_in, weights)
        mixed_out[...] = jnp.zeros_like(mixed_out)
    first[3].wait()
    cross.finish()

    def chunk(at):
        out[at] = (total[at] + hid[at] + bias[...]).astype(BF)

    each_chunk(rows, chunk)


def attend_back(
    bounds, grad, natural, attended, logs, mine, own, hid, bias, mixed, normed, layout, scale,
    fused,
):
    rows, width = hid.shape
    pairs, length = natural.shape[1:3]
    wide = 3 * grad.shape[1]
    out_shape = (
        jax.ShapeDtypeStruct((grad.shape[0], wide), BF),
        jax.ShapeDtypeStruct((rows, width), BF),
        jax.ShapeDtypeStruct((16, 128) if fused else mixed.shape, BF),
    )
    out_specs = (VMEM, VMEM, VMEM if fused else ANY)
    if fused:
        out_shape += (jax.ShapeDtypeStruct((normed.shape[1], 4 * grad.shape[1]), BF),)
        out_specs += (VMEM,)
    return pl.pallas_call(
        functools.partial(attend_back_kernel, layout, scale, fused),
        name="attend_back",
        out_shape=out_shape,
        in_specs=[pl.BlockSpec(memory_space=pltpu.SMEM)]
        + [VMEM] * 4
        + [ANY] * 2
        + [VMEM] * 2
        + [ANY] * 2,
        out_specs=out_specs,
        scratch_shapes=[
            pltpu.VMEM((pairs, length, HD), BF),
            pltpu.VMEM((3 * pairs, length, HD), BF),
            pltpu.VMEM((length, HD), F32),
            pltpu.VMEM((length, HD), F32),
            pltpu.VMEM(mixed.shape if fused else (16, 128), BF),
            pltpu.VMEM(normed.shape if fused else (16, 128), BF),
            pltpu.SemaphoreType.DMA((5,)),
            pltpu.VMEM((rows, width), F32),
        ]
        + cross_scratch(rows, width, rows // 4)
        + mix_scratch(mixed.shape[0]),
        compiler_params=pltpu.CompilerParams(
            collective_id=5, has_side_effects=True, vmem_limit_bytes=GRANT
        ),
        cost_estimate=pl.CostEstimate(flops=0, bytes_accessed=MIB, transcendentals=0),
    )(bounds, grad, natural, attended, logs, mine, own, hid, bias, mixed, normed)


def mix_row(source, target, send, recv, local):
    (s, b, u), _, _, _ = place()
    copy = sender(send, recv)
    made = [
        copy(j, source.at[to[2]], target.at[u], to)
        for j, to in enumerate(row_peers(source.shape[0]))
    ]
    kept = pltpu.make_async_copy(source.at[u], target.at[u], local)
    kept.start()
    return made + [kept]


def row_peers(n_uly):
    (s, b, u), _, _, _ = place()
    return [(s, b, (u + j) % n_uly) for j in range(1, n_uly)]


def mix_scratch(n_uly):
    return [
        pltpu.SemaphoreType.DMA((n_uly - 1,)),
        pltpu.SemaphoreType.DMA((n_uly - 1,)),
        pltpu.SemaphoreType.DMA,
    ]


def rows_of(ref, block, rows):
    return ref[pl.ds(pl.multiple_of(block * rows, rows), rows), :]


def hidden_kernel(
    order, act, weight, tok, bias, gain, shift, hidden, own,
    total, to_twin, from_twin, mine, in_x, in_y, c_send, c_recv,
):
    _, near, _, _ = place()
    rows = total.shape[0]
    meet(near)

    def multiply(block, cols):
        return product(rows_of(act, block, rows), weight[:, cols])

    run(collect(multiply, total, to_twin, from_twin, mine, in_x, in_y, c_send, c_recv))

    def chunk(at):
        values = total[at] + tok[at].astype(F32) + bias[...]
        hidden[at] = values
        unit, _ = norm_parts(values)
        own[at] = reorder(unit * gain[...] + shift[...], *order).astype(BF)

    each_chunk(rows, chunk)


def hidden_norm(act, weight, tok, bias, gain, shift, order):
    rows, width = tok.shape
    return pl.pallas_call(
        functools.partial(hidden_kernel, order),
        name="hidden_norm",
        out_shape=(
            jax.ShapeDtypeStruct((rows, width), F32),
            jax.ShapeDtypeStruct((rows, width), BF),
        ),
        in_specs=[VMEM] * 6,
        out_specs=(VMEM, VMEM),
        scratch_shapes=collect_scratch(rows, width),
        compiler_params=pltpu.CompilerParams(
            collective_id=3, has_side_effects=True, vmem_limit_bytes=GRANT
        ),
        cost_estimate=pl.CostEstimate(flops=0, bytes_accessed=MIB, transcendentals=0),
    )(act, weight, tok, bias, gain, shift)


def spread_scratch():
    return [
        pltpu.SemaphoreType.DMA((SPREAD,)),
        pltpu.SemaphoreType.DMA((SPREAD,)),
        pltpu.SemaphoreType.DMA,
    ]


def block_rows(block, rows):
    return pl.ds(pl.multiple_of(block * rows, rows), rows)


def fetch(sources, targets, sems):
    made = [
        pltpu.make_async_copy(source, target, sems.at[i])
        for i, (source, target) in enumerate(zip(sources, targets))
    ]
    for copy in made:
        copy.start()
    return made


def pairs_of(moving):
    diag, on_x, on_y, me = moving.blocks
    twin_diag, twin_x, twin_y, twin = moving.twins
    moving.own_blocks()
    yield me, twin
    moving.first_halves()
    moving.second_halves()
    yield on_x, on_y
    moving.twin_sides()
    yield twin_x, twin_y
    moving.diagonals()
    yield diag, twin_diag
    moving.close()


FF_TILE = 1024
FC_TILE = 256


def feed_kernel(
    own, weight_ref, bias, cots, out, active, slope, grad,
    weight, rows_in, cots_in, low_out, steep_out, acc, w_sem, sems, out_sems, send, recv, local,
):
    _, near, _, _ = place()
    rows, width = own.shape
    ff = weight.shape[1]
    loading = pltpu.make_async_copy(weight_ref, weight, w_sem)
    loading.start()
    halves = (pl.ds(0, rows), pl.ds(rows, rows))
    meet(near)
    moving = Spread(own, out, send, recv, local)
    diag, on_x, on_y, me = moving.blocks
    twin_diag, twin_x, twin_y, twin = moving.twins
    plan = [(me, twin), (on_x, on_y), (twin_x, twin_y), (diag, twin_diag)]

    def cots_of(i):
        return fetch(
            [cots.at[p] for p in plan[i]], [cots_in.at[i % 2, h] for h in halves], sems.at[i % 2]
        )

    arriving = cots_of(0)
    leaving = {}
    for i, (left, right) in enumerate(pairs_of(moving)):
        fetched = fetch([out.at[left], out.at[right]], [rows_in.at[h] for h in halves], sems.at[2])
        for made in fetched + arriving:
            made.wait()
        if i == 0:
            loading.wait()
        if i < 3:
            arriving = cots_of(i + 1)
        for made in leaving.pop(i - 2, []):
            made.wait()

        def tile(t, carry, i=i):
            at = pl.ds(pl.multiple_of(t * FF_TILE, FF_TILE), FF_TILE)
            inner = product(rows_in[...], weight[:, at]) + bias[:, at]
            bent = math.sqrt(2 / math.pi) * (inner + 0.044715 * (inner * inner * inner))
            curve = jnp.tanh(bent)
            low = (0.5 * inner * (1.0 + curve)).astype(BF)
            steep = math.sqrt(2 / math.pi) * (1.0 + 3 * 0.044715 * (inner * inner))
            steep = 0.5 * (1.0 + curve) + 0.5 * inner * (1.0 - curve * curve) * steep
            low_out[i % 2, :, at] = low
            steep_out[i % 2, :, at] = steep.astype(BF)
            for cut in range(0, width, 1024):
                cols = pl.ds(cut, 1024)
                term = transposed(low, cots_in[i % 2, :, cols])
                if i == 0:
                    acc[at, cols] = term
                elif i < 3:
                    acc[at, cols] += term
                else:
                    grad[at, cols] = (acc[at, cols] + term).astype(BF)
            return carry

        lax.fori_loop(0, ff // FF_TILE, tile, 0)
        places = [block_rows(left, rows), block_rows(right, rows)]
        leaving[i] = fetch(
            [held.at[i % 2, h] for held in (low_out, steep_out) for h in halves],
            [kept.at[p] for kept in (active, slope) for p in places],
            out_sems.at[i % 2],
        )
    for group in leaving.values():
        for made in group:
            made.wait()


def feed(own, weight, bias, cots):
    rows, width = own.shape
    plane, ff = cots.shape[0], weight.shape[1]
    return pl.pallas_call(
        feed_kernel,
        name="feed",
        out_shape=(
            jax.ShapeDtypeStruct((plane, rows, width), BF),
            jax.ShapeDtypeStruct((plane * rows, ff), BF),
            jax.ShapeDtypeStruct((plane * rows, ff), BF),
            jax.ShapeDtypeStruct((ff, width), BF),
        ),
        in_specs=[VMEM, ANY, VMEM, ANY],
        out_specs=(ANY, ANY, ANY, VMEM),
        scratch_shapes=[
            pltpu.VMEM(weight.shape, BF),
            pltpu.VMEM((2 * rows, width), BF),
            pltpu.VMEM((2, 2 * rows, width), BF),
            pltpu.VMEM((2, 2 * rows, ff), BF),
            pltpu.VMEM((2, 2 * rows, ff), BF),
            pltpu.VMEM((ff, width), F32),
            pltpu.SemaphoreType.DMA,
            pltpu.SemaphoreType.DMA((3, 2)),
            pltpu.SemaphoreType.DMA((2, 4)),
        ]
        + spread_scratch(),
        compiler_params=pltpu.CompilerParams(
            collective_id=8, has_side_effects=True, vmem_limit_bytes=GRANT
        ),
        cost_estimate=pl.CostEstimate(flops=0, bytes_accessed=MIB, transcendentals=0),
    )(own, weight, bias, cots)


def back_feed_kernel(
    order, cots, slope, normed_ref, proj, weight, hid, cot, gain,
    fc_grad, grad_hidden, own, sums, bias,
    inner_grad, normed, cots_in, slope_in, sems, n_sem,
    total, to_twin, from_twin, mine, in_x, in_y, c_send, c_recv,
):
    _, near, here, other = place()
    rows, width = total.shape
    ff = weight.shape[1]
    plan = [other[0], other[1], here[0], other[2], here[1], other[3], here[2], here[3]]

    def load(i):
        at = i % 2
        return fetch(
            (cots.at[plan[i]], slope.at[block_rows(plan[i], rows)]),
            (cots_in.at[at], slope_in.at[at]),
            sems.at[at],
        )

    loads = [load(0)]
    normed_load = pltpu.make_async_copy(normed_ref, normed, n_sem)
    normed_load.start()
    sums[...] = jnp.zeros_like(sums)
    bias[...] = jnp.zeros_like(bias)
    meet(near)

    def prepare(block):
        i = len(loads) - 1
        for made in loads[i]:
            made.wait()
        loads.append(load(i + 1) if i + 1 < len(plan) else [])

        def tile(t, carry):
            at = pl.ds(pl.multiple_of(t * FF_TILE, FF_TILE), FF_TILE)
            made = against(cots_in[i % 2], proj[at, :]) * slope_in[i % 2, :, at].astype(F32)
            low = made.astype(BF)
            inner_grad[block_rows(block, rows), at] = low
            bias[0:1, at] += row_sum(low.astype(F32))
            return carry

        lax.fori_loop(0, ff // FF_TILE, tile, 0)

    def multiply(block, cols):
        return against(rows_of(inner_grad, block, rows), weight[cols, :])

    def fc_tile(t, carry):
        at = pl.ds(pl.multiple_of(t * FC_TILE, FC_TILE), FC_TILE)
        fc_grad[at, :] = transposed(normed[:, at], inner_grad[...]).astype(BF)
        return carry

    moving = collect(
        multiply, total, to_twin, from_twin, mine, in_x, in_y, c_send, c_recv, prepare
    )
    next(moving)
    next(moving)
    normed_load.wait()
    lax.fori_loop(0, width // FC_TILE, fc_tile, 0)
    run(moving)
    inner, outer, lanes = order[1], order[0], order[2]

    def chunk(at):
        grad = reorder(total[at], inner, outer, lanes)
        back, by_gain = norm_back(grad, hid[at], gain[...])
        passed = cot[at].astype(F32)
        back = back + passed
        grad_hidden[at] = back
        low = back.astype(BF)
        own[at] = low
        sums[0:1] += row_sum(by_gain)
        sums[1:2] += row_sum(grad)
        sums[2:3] += row_sum(low.astype(F32))
        sums[3:4] += row_sum(passed)

    each_chunk(rows, chunk)


def back_feed(cots, slope, normed, proj, weight, hid, cot, gain, order):
    rows, width = cot.shape
    ff = weight.shape[1]
    return pl.pallas_call(
        functools.partial(back_feed_kernel, order),
        name="back_feed",
        out_shape=(
            jax.ShapeDtypeStruct((width, ff), BF),
            jax.ShapeDtypeStruct((rows, width), F32),
            jax.ShapeDtypeStruct((rows, width), BF),
            jax.ShapeDtypeStruct((8, width), F32),
            jax.ShapeDtypeStruct((8, ff), F32),
        ),
        in_specs=[ANY] * 3 + [VMEM] * 5,
        out_specs=(VMEM,) * 5,
        scratch_shapes=[
            pltpu.VMEM((slope.shape[0], ff), BF),
            pltpu.VMEM(normed.shape, BF),
            pltpu.VMEM((2, rows, width), BF),
            pltpu.VMEM((2, rows, ff), BF),
            pltpu.SemaphoreType.DMA((2, 2)),
            pltpu.SemaphoreType.DMA,
        ]
        + collect_scratch(rows, width),
        compiler_params=pltpu.CompilerParams(
            collective_id=4, has_side_effects=True, vmem_limit_bytes=GRANT
        ),
        cost_estimate=pl.CostEstimate(flops=0, bytes_accessed=MIB, transcendentals=0),
    )(cots, slope, normed, proj, weight, hid, cot, gain)


def branch_kernel(
    own, weight, low, act_ref, proj_ref, out, heads_grad, weight_grad, mine, total,
    act, proj, rows_in, acc, sems, to_twin, from_twin, c_send, c_recv, a_sems, send, recv, local,
):
    _, near, _, _ = place()
    rows, width = own.shape
    loading = fetch((act_ref, proj_ref), (act, proj), a_sems)
    meet(near)
    moving = Spread(own, out, send, recv, local)

    def multiply(block, cols):
        return product(rows_of(act, block, rows), proj[:, cols])

    chip = ChipSums(multiply, total, to_twin, from_twin, mine, c_send, c_recv)
    for i, (left, right) in enumerate(pairs_of(moving)):
        fetched = fetch(
            (out.at[left], out.at[right]),
            (rows_in.at[pl.ds(0, rows)], rows_in.at[pl.ds(rows, rows)]),
            sems,
        )
        for made in fetched:
            made.wait()
        grads = against(rows_in[...], weight[...]).astype(BF)
        heads_grad[block_rows(left, rows)] = grads[:rows]
        heads_grad[block_rows(right, rows)] = grads[rows:]
        kept = jnp.concatenate(
            [low[block_rows(left, rows), :], low[block_rows(right, rows), :]], axis=0
        )
        for cut in range(0, width, 1024):
            cols = pl.ds(cut, 1024)
            term = transposed(kept, rows_in[:, cols])
            if i == 0:
                acc[:, cols] = term
            elif i < 3:
                acc[:, cols] += term
            else:
                weight_grad[:, cols] = (acc[:, cols] + term).astype(BF)
        if i == 0:
            for made in loading:
                made.wait()
            for k in range(4):
                chip.for_twin(k)
        elif i == 1:
            for k in range(4):
                chip.for_here(k)
    chip.close()


def branch_spread(own, weight, low, act, proj, plane):
    rows, width = own.shape
    share = weight.shape[0]
    return pl.pallas_call(
        branch_kernel,
        name="branch_spread",
        out_shape=(
            jax.ShapeDtypeStruct((plane, rows, width), BF),
            jax.ShapeDtypeStruct((plane * rows, share), BF),
            jax.ShapeDtypeStruct((share, width), BF),
            jax.ShapeDtypeStruct((3, rows, width), BF),
            jax.ShapeDtypeStruct((rows, width), F32),
        ),
        in_specs=[VMEM] * 3 + [ANY] * 2,
        out_specs=(ANY, VMEM, VMEM, VMEM, VMEM),
        scratch_shapes=[
            pltpu.VMEM(act.shape, BF),
            pltpu.VMEM(proj.shape, BF),
            pltpu.VMEM((2 * rows, width), BF),
            pltpu.VMEM((share, width), F32),
            pltpu.SemaphoreType.DMA((2,)),
        ]
        + chip_scratch(rows, width)
        + [pltpu.SemaphoreType.DMA((4,))] * 2
        + [pltpu.SemaphoreType.DMA((2,))]
        + spread_scratch(),
        compiler_params=pltpu.CompilerParams(
            collective_id=9, has_side_effects=True, vmem_limit_bytes=GRANT
        ),
        cost_estimate=pl.CostEstimate(flops=0, bytes_accessed=MIB, transcendentals=0),
    )(own, weight, low, act, proj)


def inputs_kernel(
    sizes, order, act, weight, tok, grad_hidden, gain, fc_ref, sums, out, fc,
    total, to_twin, from_twin, mine, in_x, in_y, c_send, c_recv, own,
    send, recv, local, f_send, f_recv, f_local,
):
    n_seq, n_blk, n_uly, runs = sizes
    rows = total.shape[0]
    me, friends = plane_peers(n_seq * n_uly)
    meet([peer for _, peer in friends] + blk_peers(n_blk))

    def multiply(block, cols):
        return against(rows_of(act, block, rows), weight[cols, :])

    run(collect(multiply, total, to_twin, from_twin, mine, in_x, in_y, c_send, c_recv))
    spans = feed_spans(fc, fc_ref, me, sizes)
    leaving = return_columns(home(f_local), 0, spans, me, None)
    for j, (p, peer) in enumerate(friends):
        leaving += return_columns(sender(f_send, f_recv), runs * j, spans, p, peer)
    sums[...] = jnp.zeros_like(sums)
    inner, outer, lanes = order[1], order[0], order[2]

    def chunk(at):
        grad = reorder(total[at], inner, outer, lanes)
        back, by_gain = norm_back(grad, tok[at].astype(F32), gain[...])
        own[at] = (grad_hidden[at] + back).astype(BF)
        sums[0:1] += row_sum(by_gain)
        sums[1:2] += row_sum(grad)

    each_chunk(rows, chunk)
    leaving += return_rows(own, out, n_blk, send, recv, local)
    for made in leaving:
        made.wait()


def inputs_return(act, weight, tok, grad_hidden, gain, fc, sizes, order):
    rows, width = tok.shape
    n_blk, runs = sizes[1], sizes[3]
    plane = fc.shape[0]
    return pl.pallas_call(
        functools.partial(inputs_kernel, sizes, order),
        name="inputs_return",
        out_shape=(
            jax.ShapeDtypeStruct((8, width), F32),
            jax.ShapeDtypeStruct((n_blk, rows // n_blk, width), BF),
            jax.ShapeDtypeStruct((fc.shape[1], plane * fc.shape[2]), BF),
        ),
        in_specs=[VMEM] * 5 + [ANY],
        out_specs=(VMEM, ANY, ANY),
        scratch_shapes=collect_scratch(rows, width)
        + [pltpu.VMEM((rows, width), BF)]
        + [pltpu.SemaphoreType.DMA((n_blk - 1,))] * 2
        + [pltpu.SemaphoreType.DMA]
        + [pltpu.SemaphoreType.DMA((runs * (plane - 1),))] * 2
        + [pltpu.SemaphoreType.DMA((runs,))],
        compiler_params=pltpu.CompilerParams(
            collective_id=6, has_side_effects=True, vmem_limit_bytes=GRANT
        ),
        cost_estimate=pl.CostEstimate(flops=0, bytes_accessed=MIB, transcendentals=0),
    )(act, weight, tok, grad_hidden, gain, fc)


def weight_terms(left, right, mixed, out):
    wide = right.shape[1]
    share = out.shape[1] - wide
    pieces = left.shape[1] // share
    rows = mixed.shape[1]

    def tile(t, carry):
        at = pl.ds(pl.multiple_of(t * FC_TILE, FC_TILE), FC_TILE)
        out[at, :wide] = transposed(left[:, at], right[...]).astype(BF)
        return carry

    lax.fori_loop(0, out.shape[0] // FC_TILE, tile, 0)
    for at in range(0, mixed.shape[0] * rows, rows):
        b, first = at // rows, at * pieces
        for j in range(pieces):
            to = first + j * rows
            out[to : to + rows, wide:] = mixed[b, :, j * share : (j + 1) * share]


def weight_grad(left, right, mixed):
    width = left.shape[1]
    return pl.pallas_call(
        weight_terms,
        name="weight_grad",
        out_shape=jax.ShapeDtypeStruct((width, 4 * right.shape[1] // 3), BF),
        in_specs=[VMEM] * 3,
        out_specs=VMEM,
        compiler_params=pltpu.CompilerParams(vmem_limit_bytes=GRANT),
        cost_estimate=pl.CostEstimate(flops=0, bytes_accessed=MIB, transcendentals=0),
    )(left, right, mixed)


def end_kernel(
    sizes, qkv_ref, small_ref, result_ref, gq, gk, gv, small, result,
    gathered, partial, arrived,
    blk_send, blk_recv, plane_send, plane_recv, local, r_send, r_recv, r_local,
):
    n_seq, n_blk, n_uly, _ = sizes
    (s, b, u), _, _, _ = place()
    plane = n_seq * n_uly
    me, friends = plane_peers(plane)
    column = blk_peers(n_blk)
    meet([peer for _, peer in friends] + column)
    by_blk = sender(blk_send, blk_recv)
    by_plane = sender(plane_send, plane_recv)
    at_home = home(local)
    spans = projection_spans((gq, gk, gv), qkv_ref, me, sizes)
    first = at_home(0, small_ref.at[me], gathered.at[me], None)
    vectors = [
        by_plane(3 * (plane - 1) + j, small_ref.at[p], gathered.at[me], peer)
        for j, (p, peer) in enumerate(friends)
    ]
    started = return_rows(result_ref, result, n_blk, r_send, r_recv, r_local)
    for j, (p, peer) in enumerate(friends):
        started += return_columns(by_plane, 3 * j, spans, p, peer)
    started += return_columns(at_home, 2, spans, me, None)
    first.wait()
    for made in vectors:
        made.wait()
    partial[...] = jnp.sum(gathered[...], axis=0)
    sent = [at_home(1, partial.at[b], arrived.at[b], None)]
    sent += [
        by_blk(j, partial.at[peer[1]], arrived.at[b], peer) for j, peer in enumerate(column)
    ]
    for made in sent:
        made.wait()
    small[...] = jnp.sum(arrived[...], axis=0)
    for made in started:
        made.wait()


def finish(qkv, small, result, sizes):
    n_seq, n_blk, n_uly, _ = sizes
    plane = n_seq * n_uly
    rows, share = qkv.shape[1], qkv.shape[2] // 4
    tail = small.shape[2:]
    whole = jax.ShapeDtypeStruct((rows, plane * share), BF)
    back = jax.ShapeDtypeStruct((n_blk, result.shape[0] // n_blk, result.shape[1]), BF)
    blk_sems = [pltpu.SemaphoreType.DMA((n_blk - 1,))] * 2
    return pl.pallas_call(
        functools.partial(end_kernel, sizes),
        name="finish",
        out_shape=(whole, whole, whole, jax.ShapeDtypeStruct(tail, small.dtype), back),
        in_specs=[ANY] * 3,
        out_specs=(ANY, ANY, ANY, VMEM, ANY),
        scratch_shapes=[
            pltpu.VMEM((plane, n_blk) + tail, F32),
            pltpu.VMEM((n_blk,) + tail, F32),
            pltpu.VMEM((n_blk,) + tail, F32),
        ]
        + blk_sems
        + [pltpu.SemaphoreType.DMA((4 * (plane - 1),))] * 2
        + [pltpu.SemaphoreType.DMA((5,))]
        + blk_sems
        + [pltpu.SemaphoreType.DMA],
        compiler_params=pltpu.CompilerParams(
            collective_id=7, has_side_effects=True, vmem_limit_bytes=16 * MIB
        ),
        cost_estimate=pl.CostEstimate(flops=0, bytes_accessed=MIB, transcendentals=0),
    )(qkv, small, result)


def on_device(
    inputs,
    doc_lengths,
    ln1_gain,
    ln1_shift,
    w_query,
    b_query,
    w_key,
    w_value,
    b_value,
    w_out,
    b_out,
    ln2_gain,
    ln2_shift,
    w_fc,
    b_fc,
    w_proj,
    b_proj,
    cotangent,
):
    seqs, tok, width = inputs.shape
    n_seq, n_blk, n_uly = (lax.axis_size(a) for a in ALL)
    plane = n_seq * n_uly
    here_seq, here_blk, here_uly = (lax.axis_index(a) for a in ALL)
    here = here_seq * n_uly + here_uly
    scale = 1.0 / math.sqrt(HD)
    rows = w_query.shape[0]
    hidden_rows = w_proj.shape[0]
    share = width // plane
    heads = share // HD
    ff_share = hidden_rows * n_blk
    sharing = max(1, n_blk // seqs)
    held = seqs * sharing // n_blk
    part = tok // sharing
    n_rows = n_blk * held * part
    order = (n_seq, n_blk, n_uly * rows)

    def by_plane(block):
        block = block.reshape(n_blk // sharing, held, sharing, part, width)
        return block.transpose(0, 2, 1, 3, 4).reshape(n_blk, held * part, width)

    def from_plane(block):
        block = block.reshape(n_blk // sharing, sharing, held, part, width)
        return block.transpose(0, 2, 1, 3, 4).reshape(seqs, tok, width)

    vectors = (ln1_gain, ln1_shift, b_query, b_value, b_out, ln2_gain, ln2_shift, b_proj)
    vectors += (b_fc, doc_lengths.reshape(-1))
    runs = n_blk if hidden_rows % 128 == 0 else 1
    sizes = (n_seq, n_blk, n_uly, runs)
    by_block = (rows, n_seq, n_blk, n_uly, hidden_rows)
    by_device = (rows, n_seq, n_uly, n_blk, hidden_rows)
    if runs == 1:
        w_fc = w_fc.reshape(by_block).transpose(0, 1, 3, 2, 4).reshape(rows, -1)
    tokens, qkv, fc, small = enter(
        by_plane(inputs), (w_query, w_key, w_value), w_fc, [v.reshape(1, -1) for v in vectors], sizes
    )
    tokens = tokens.reshape(n_rows, width)

    def over_blk(matrix):
        return lax.all_gather(matrix, "blk", axis=0, tiled=True)

    out_part = over_blk(w_out)
    tokens, out_part = lax.optimization_barrier((tokens, out_part))
    qkv = over_blk(qkv.reshape(plane * rows, 3 * share))
    small = small.reshape(n_seq, n_uly, n_blk, SMALL, 128)
    flat = small[:, :, :, :8, :rows].transpose(3, 0, 2, 1, 4).reshape(8, 1, width)
    whole = [flat[i] for i in range(8)]
    lanes = min(128, hidden_rows)
    bias_fc = lax.dynamic_slice(
        small, (here_seq, here_uly, 0, 8, 0), (1, 1, n_blk, hidden_rows // lanes, lanes)
    ).reshape(1, ff_share)
    lengths = small[:, 0, 0, SMALL - 1, : doc_lengths.size].astype(jnp.int32)
    lengths = lengths.reshape(n_seq, *doc_lengths.shape)
    gain_one, shift_one, bias_q, bias_v, bias_out, gain_two, shift_two, bias_proj = whole
    mine = lambda v: lax.dynamic_slice(v, (0, here * share), (1, share))
    bias_q, bias_v = mine(bias_q), mine(bias_v)

    normed, grad_out, grad_all = norm_gather(
        tokens, gain_one, shift_one, by_plane(cotangent), plane, order
    )
    fc = over_blk(fc.reshape(plane * rows, ff_share))
    normed = normed.reshape(plane * n_rows, width)
    made = product(normed, qkv)
    bias_all = jnp.concatenate([bias_q, jnp.zeros_like(bias_q), bias_v], axis=1)
    scales = jnp.repeat(jnp.array([[scale, 1.0, 1.0]], F32), share, axis=1)
    made = ((made + bias_all) * scales).astype(BF)

    made, w_proj = lax.optimization_barrier((made, w_proj))
    proj = over_blk(w_proj)

    groups = [
        [g * sharing + i for i in range(sharing)] for g in range(n_blk // sharing)
    ]
    pairs = n_seq * held * heads // sharing
    length = n_blk * n_uly * tok
    if sharing == held == 1:
        layout = (n_seq, n_uly, n_blk, part, heads)
    else:
        layout = (pairs, 1, 1, length, 1)

    def to_heads(matrix, kinds):
        if sharing == held == 1:
            return matrix
        matrix = matrix.reshape(n_seq, n_uly, n_blk, held, part, kinds, heads, HD)
        matrix = matrix.transpose(0, 3, 6, 2, 1, 4, 5, 7)
        matrix = matrix.reshape(n_seq * held * heads, n_blk, n_uly, 1, part, kinds * HD)
        if sharing > 1:
            matrix = lax.all_to_all(
                matrix, "blk", split_axis=0, concat_axis=3, axis_index_groups=groups, tiled=True
            )
        return matrix.reshape(pairs * length, kinds * HD)

    def from_heads(matrix, kinds):
        if sharing == held == 1:
            return matrix
        matrix = matrix.reshape(pairs, n_blk, n_uly, sharing, part, kinds * HD)
        if sharing > 1:
            matrix = lax.all_to_all(
                matrix, "blk", split_axis=3, concat_axis=0, axis_index_groups=groups, tiled=True
            )
        matrix = matrix.reshape(n_seq, held, heads, n_blk, n_uly, part, kinds, HD)
        matrix = matrix.transpose(0, 4, 3, 1, 5, 6, 2, 7)
        return matrix.reshape(plane * n_rows, kinds * share)

    turn = here_blk % sharing
    pair_at = turn * pairs + jnp.arange(layout[0]) * layout[4]
    seq_of = pair_at // (held * heads)
    held_of = (pair_at // heads) % held
    which = (here_blk // sharing) * held + held_of
    own_lengths = lengths[seq_of, which]
    first = own_lengths[:, 0:1]
    bounds = jnp.concatenate([first, first + own_lengths[:, 1:2]], axis=1).reshape(-1)

    out_part = out_part.reshape(n_uly, n_blk // n_uly * rows, width)
    attended_low, natural, attended, logs, out_part = attend(
        bounds, to_heads(made, 3), out_part, layout
    )
    out_part = out_part.reshape(n_uly, n_blk // n_uly, rows, width)
    out_part = out_part.transpose(1, 0, 2, 3).reshape(share, width)
    attended_low = from_heads(attended_low, 1)
    hidden, own_two = hidden_norm(
        attended_low, out_part, tokens, bias_out, gain_two, shift_two, order
    )
    normed_two, active, slope, grad_proj = feed(own_two, fc, bias_fc, grad_all)

    def sum_blk(matrix):
        return lax.psum_scatter(matrix, "blk", scatter_dimension=0, tiled=True)

    grad_w_proj = sum_blk(grad_proj)
    grad_fc, grad_hidden, branch, sums_two, sums_fc = back_feed(
        grad_all, slope, normed_two.reshape(plane * n_rows, width), proj, fc, hidden, grad_out, gain_two, order
    )
    _, grad_heads, grad_w_out, chip_sums, own_sum = branch_spread(
        branch, out_part, attended_low, active, proj, plane
    )
    grad_b_fc = sums_fc[0]
    grad_fc = sum_blk(grad_fc)
    grad_w_out = grad_w_out.reshape(n_blk // n_uly, n_uly, rows, width).transpose(1, 0, 2, 3)
    grad_w_out = grad_w_out.reshape(n_uly, n_blk // n_uly * rows, width)
    grad_heads, grad_w_proj = lax.optimization_barrier((grad_heads, grad_w_proj))
    grad_heads = to_heads(grad_heads, 1)
    fused = sharing == held == 1
    backs, result, grad_w_out, *grads = attend_back(
        bounds,
        grad_heads,
        natural,
        attended,
        logs,
        chip_sums,
        own_sum,
        hidden,
        bias_proj,
        grad_w_out,
        normed,
        layout,
        scale,
        fused,
    )
    backs = from_heads(backs, 3)
    if fused:
        grads = grads[0]
    else:
        grads = weight_grad(normed, backs, grad_w_out.reshape(n_blk, rows, width))
    grad_bias = jnp.sum(backs.astype(F32), axis=0)
    grads = sum_blk(grads).reshape(plane, rows, 4 * share)
    grad_w_out = grads[:, :, 3 * share :].transpose(1, 0, 2).reshape(rows, width).astype(F32)
    last, grad_fc = lax.optimization_barrier((backs, grad_fc))
    sums_one, grad_inputs, grad_fc = inputs_return(
        last,
        qkv,
        tokens,
        grad_hidden,
        gain_one,
        grad_fc.reshape(plane, rows, ff_share),
        sizes,
        order,
    )

    def widened(vector):
        return lax.dynamic_update_slice(jnp.zeros((width,), F32), vector, (here * share,))

    parts = (
        sums_one[0],
        sums_one[1],
        widened(grad_bias[:share]),
        widened(grad_bias[2 * share :]),
        sums_two[2],
        sums_two[0],
        sums_two[1],
        sums_two[3],
    )
    wide_fc = lax.dynamic_update_slice(
        jnp.zeros((n_seq, n_blk, n_uly, hidden_rows), F32),
        grad_b_fc.reshape(1, n_blk, 1, hidden_rows),
        (here_seq, 0, here_uly, 0),
    )
    sums = jnp.concatenate(
        [p.reshape(n_seq, n_blk, n_uly, rows) for p in parts] + [wide_fc], axis=3
    )
    used = sums.shape[3]
    end_lanes = -(-used // 1024) * 8
    sums = jnp.pad(sums, ((0, 0),) * 3 + ((0, end_lanes * 128 - used),))
    sums = sums.transpose(0, 2, 1, 3).reshape(plane, n_blk, end_lanes, 128)
    *grad_qkv, sums, result = finish(grads, sums, result, sizes)
    grad_qkv = [g.astype(F32) for g in grad_qkv]
    if runs == 1:
        grad_fc = grad_fc.reshape(by_device).transpose(0, 1, 3, 2, 4).reshape(rows, -1)
    grad_fc = grad_fc.astype(F32)
    grad_w_proj = grad_w_proj.astype(F32)
    sums = sums.reshape(-1)
    each = [sums[i * rows : (i + 1) * rows] for i in range(8)]
    return (
        from_plane(result),
        from_plane(grad_inputs),
        each[0],
        each[1],
        grad_qkv[0],
        each[2],
        grad_qkv[1],
        grad_qkv[2],
        each[3],
        grad_w_out,
        each[4],
        each[5],
        each[6],
        grad_fc,
        sums[8 * rows : used],
        grad_w_proj,
        each[7],
    )


def solution(mesh):
    tokens = P("seq", ("blk", "uly"), None)
    vector = P(ALL)
    matrix = P(ALL, None)
    return jax.shard_map(
        on_device,
        mesh=mesh,
        in_specs=(
            tokens, P("seq", None), vector, vector, matrix, vector, matrix, matrix, vector,
            matrix, vector, vector, vector, matrix, vector, matrix, vector, tokens,
        ),
        out_specs=(
            tokens, tokens, vector, vector, matrix, vector, matrix, matrix, vector,
            matrix, vector, vector, vector, matrix, vector, matrix, vector,
        ),
        check_vma=False,
    )
```

```python
import functools
import math

import jax
import jax.numpy as jnp
from jax import lax
from jax.experimental import pallas as pl
from jax.experimental.pallas import tpu as pltpu
from jax.sharding import PartitionSpec as P

HD = 128
EPS = 1e-05
NEGATIVE = -1e30
ALL = ("seq", "blk", "uly")
PLANE = ("seq", "uly")
BF = jnp.bfloat16
F32 = jnp.float32
MESH = pl.DeviceIdType.MESH
ANY = pl.BlockSpec(memory_space=pl.ANY)
VMEM = pl.BlockSpec(memory_space=pltpu.VMEM)
MIB = 2**20
GRANT = 60 * MIB
CHUNK = 16
TILE = 2048


def gelu_tanh(values):
    return jax.nn.gelu(values, approximate=True)


def product(left_side, right_side):
    return jnp.dot(left_side, right_side, preferred_element_type=F32)


def transposed(left_side, right_side):
    return lax.dot_general(
        left_side, right_side, (((0,), (0,)), ((), ())), preferred_element_type=F32
    )


def against(left_side, right_side):
    return lax.dot_general(
        left_side, right_side, (((1,), (1,)), ((), ())), preferred_element_type=F32
    )


def meet(peers):
    barrier = pltpu.get_barrier_semaphore()
    for peer in peers:
        pl.semaphore_signal(barrier, inc=1, device_id=peer, device_id_type=MESH)
    pl.semaphore_wait(barrier, len(peers))


def sender(send, recv):
    def copy(i, source, target, device):
        made = pltpu.make_async_remote_copy(
            src_ref=source,
            dst_ref=target,
            send_sem=send.at[i],
            recv_sem=recv.at[i],
            device_id=device,
            device_id_type=MESH,
        )
        made.start()
        return made

    return copy


def place():
    s, b, u = (lax.axis_index(a) for a in ALL)
    a, c = u // 2, u % 2
    beside = (s, b, 2 * (1 - a) + c)
    across = (1 - s, b, u)
    twin = (s, b, 2 * a + 1 - c)

    def blocks(core):
        own = 4 * s + 2 * a + core
        on_x = 4 * s + 2 * (1 - a) + core
        on_y = 4 * (1 - s) + 2 * a + core
        diagonal = 4 * (1 - s) + 2 * (1 - a) + core
        return diagonal, on_x, on_y, own

    return (s, b, u), (beside, across, twin), blocks(c), blocks(1 - c)


class Spread:
    def __init__(self, own, out, send, recv, local):
        _, self.near_by, self.blocks, self.twins = place()
        beside, across, twin = self.near_by
        me = self.blocks[3]
        half = own.shape[0] // 2
        self.out, self.parts = out, (pl.ds(0, half), pl.ds(half, half))
        self.copy = copy = sender(send, recv)
        p0, p1 = self.parts
        self.x0 = copy(0, own.at[p0], out.at[me, p0], beside)
        self.y1 = copy(1, own.at[p1], out.at[me, p1], across)
        self.x1 = copy(2, own.at[p1], out.at[me, p1], beside)
        self.y0 = copy(3, own.at[p0], out.at[me, p0], across)
        self.own_twin = copy(4, own, out.at[me], twin)
        self.started = [self.x0, self.y1, self.x1, self.y0, self.own_twin]
        self.kept = pltpu.make_async_copy(own, out.at[me], local)
        self.kept.start()

    def pass_on(self, i, block, part, device):
        at = self.out.at[block, self.parts[part]]
        made = self.copy(i, at, at, device)
        self.started.append(made)
        return made

    def own_blocks(self):
        self.kept.wait()
        self.own_twin.wait_recv()

    def first_halves(self):
        beside, across, twin = self.near_by
        _, on_x, on_y, _ = self.blocks
        self.x0.wait_recv()
        self.d0 = self.pass_on(5, on_x, 0, across)
        self.t0 = self.pass_on(6, on_x, 0, twin)
        self.y1.wait_recv()
        self.d1 = self.pass_on(7, on_y, 1, beside)
        self.t1 = self.pass_on(8, on_y, 1, twin)

    def second_halves(self):
        _, _, twin = self.near_by
        _, on_x, on_y, _ = self.blocks
        self.x1.wait_recv()
        self.t2 = self.pass_on(9, on_x, 1, twin)
        self.y0.wait_recv()
        self.t3 = self.pass_on(10, on_y, 0, twin)

    def twin_sides(self):
        for made in (self.t0, self.t1, self.t2, self.t3):
            made.wait_recv()

    def diagonals(self):
        _, _, twin = self.near_by
        diag = self.blocks[0]
        self.d0.wait_recv()
        t4 = self.pass_on(11, diag, 0, twin)
        self.d1.wait_recv()
        t5 = self.pass_on(12, diag, 1, twin)
        t4.wait_recv()
        t5.wait_recv()

    def close(self):
        for made in self.started:
            made.wait_send()


def spread(own, out, send, recv, local):
    moving = Spread(own, out, send, recv, local)
    yield
    moving.first_halves()
    yield
    moving.second_halves()
    yield
    moving.own_blocks()
    moving.twin_sides()
    moving.diagonals()
    moving.close()


def run(steps):
    for _ in steps:
        pass


SPREAD = 13


class ChipSums:
    def __init__(self, multiply, total, to_twin, from_twin, mine, send, recv, prepare=None):
        _, (_, _, self.twin), self.here, self.other = place()
        self.multiply, self.prepare = multiply, prepare or (lambda block: None)
        self.total, self.mine = total, mine
        self.to_twin, self.from_twin = to_twin, from_twin
        self.copy = sender(send, recv)
        self.sent = []

    def each_tile(self, body):
        def step(t, carry):
            body(pl.ds(pl.multiple_of(t * TILE, TILE), TILE))
            return carry

        lax.fori_loop(0, self.total.shape[1] // TILE, step, 0)

    def for_twin(self, k):
        def term(cols):
            self.to_twin[k, :, cols] = self.multiply(self.other[k], cols).astype(BF)

        self.prepare(self.other[k])
        self.each_tile(term)
        self.sent.append(self.copy(k, self.to_twin.at[k], self.from_twin.at[k], self.twin))

    def for_here(self, k):
        def term(cols):
            both = self.multiply(self.here[k], cols) + self.from_twin[k, :, cols].astype(F32)
            if k < 3:
                self.mine[k, :, cols] = both.astype(BF)
            else:
                self.total[:, cols] = both

        self.prepare(self.here[k])
        self.sent[k].wait_recv()
        self.each_tile(term)

    def close(self):
        for made in self.sent:
            made.wait_send()


class Cross:
    def __init__(self, total, mine, in_x, in_y, send, recv, cut=None):
        _, (self.beside, self.across, _), _, _ = place()
        self.total, self.mine, self.in_x, self.in_y = total, mine, in_x, in_y
        rows = total.shape[0]
        self.cut = cut or rows // 2
        self.rest = rows - self.cut
        self.parts = (pl.ds(0, self.cut), pl.ds(self.cut, self.rest))
        self.copy = sender(send, recv)
        self.started = []

    def to_x(self, i, k, part, slot):
        rows = (self.cut, self.rest)[part]
        target = self.in_x.at[slot, pl.ds(0, rows)]
        return self.copy(i, self.mine.at[k, self.parts[part]], target, self.beside)

    def to_y(self, i, k, part, slot):
        rows = (self.cut, self.rest)[part]
        target = self.in_y.at[slot, pl.ds(0, rows)]
        return self.copy(i, self.mine.at[k, self.parts[part]], target, self.across)

    def begin(self, k):
        if k == 0:
            self.dx = self.to_x(4, 0, 0, 0)
            self.dy = self.to_y(5, 0, 1, 0)
        elif k == 1:
            self.started.append(self.to_x(6, 1, 0, 1))
        else:
            self.started.append(self.to_y(7, 2, 1, 1))

    def add(self, k, first, rows, arrived):
        def step(t, carry):
            at = pl.ds(pl.multiple_of(t * CHUNK, CHUNK), CHUNK)
            to = pl.ds(pl.multiple_of(first + t * CHUNK, CHUNK), CHUNK)
            both = self.mine[k, to].astype(F32) + arrived[0, at].astype(F32)
            self.mine[k, to] = both.astype(BF)
            return carry

        lax.fori_loop(0, rows // CHUNK, step, 0)

    def diagonals(self):
        self.dy.wait_recv()
        self.add(1, self.cut, self.rest, self.in_y)
        self.started.append(self.to_x(8, 1, 1, 2))
        self.dx.wait_recv()
        self.add(2, 0, self.cut, self.in_x)
        self.started.append(self.to_y(9, 2, 0, 2))

    def finish(self):
        total, in_x, in_y = self.total, self.in_x, self.in_y
        for made in self.started:
            made.wait_recv()

        def add(first, rows, x_slot, y_slot):
            def step(t, carry):
                at = pl.ds(pl.multiple_of(t * CHUNK, CHUNK), CHUNK)
                to = pl.ds(pl.multiple_of(first + t * CHUNK, CHUNK), CHUNK)
                total[to] += in_x[x_slot, at].astype(F32) + in_y[y_slot, at].astype(F32)
                return carry

            lax.fori_loop(0, rows // CHUNK, step, 0)

        add(0, self.cut, 1, 2)
        add(self.cut, self.rest, 2, 1)
        for made in self.started + [self.dx, self.dy]:
            made.wait_send()


def collect(
    multiply, total, to_twin, from_twin, mine, in_x, in_y, send, recv, prepare=None
):
    chip = ChipSums(multiply, total, to_twin, from_twin, mine, send, recv, prepare)
    cross = Cross(total, mine, in_x, in_y, send, recv)
    chip.for_twin(0)
    for k in range(4):
        if k < 3:
            chip.for_twin(k + 1)
        chip.for_here(k)
        if k < 3:
            cross.begin(k)
    yield
    cross.diagonals()
    yield
    cross.finish()
    chip.close()


COLLECT = 10


def chip_scratch(rows, width):
    return [pltpu.VMEM((4, rows, width), BF)] * 2


def cross_scratch(rows, width, cut=None):
    cut = cut or rows // 2
    return [
        pltpu.VMEM((3, rows, width), BF),
        pltpu.VMEM((3, rows - cut, width), BF),
        pltpu.VMEM((3, rows - cut, width), BF),
        pltpu.SemaphoreType.DMA((COLLECT,)),
        pltpu.SemaphoreType.DMA((COLLECT,)),
    ]


def collect_scratch(rows, width):
    return [pltpu.VMEM((rows, width), F32)] + chip_scratch(rows, width) + cross_scratch(rows, width)


def reorder(values, outer, inner, lanes):
    return jnp.concatenate(
        [
            values[:, (o * inner + i) * lanes : (o * inner + i + 1) * lanes]
            for i in range(inner)
            for o in range(outer)
        ],
        axis=1,
    )


def norm_parts(values):
    average = jnp.mean(values, axis=-1, keepdims=True)
    centred = values - average
    variance = jnp.mean(centred * centred, axis=-1, keepdims=True)
    spread_back = lax.rsqrt(variance + EPS)
    return centred * spread_back, spread_back


def norm_back(grad, values, gain):
    unit, spread_back = norm_parts(values)
    scaled = grad * gain
    back = spread_back * (
        scaled
        - jnp.mean(scaled, axis=-1, keepdims=True)
        - unit * jnp.mean(scaled * unit, axis=-1, keepdims=True)
    )
    return back, grad * unit


def each_chunk(rows, body):
    def step(t, carry):
        body(pl.ds(pl.multiple_of(t * CHUNK, CHUNK), CHUNK))
        return carry

    lax.fori_loop(0, rows // CHUNK, step, 0)


def row_sum(values):
    return jnp.sum(values, axis=0, keepdims=True)


def return_rows(block, out, n_blk, send, recv, local):
    (s, b, u), _, _, _ = place()
    count = block.shape[0] // n_blk
    copy = sender(send, recv)
    started = []
    for j in range(1, n_blk):
        to = (b + j) % n_blk
        rows = pl.ds(pl.multiple_of(to * count, count), count)
        started.append(copy(j - 1, block.at[rows], out.at[b], (s, to, u)))
    rows = pl.ds(pl.multiple_of(b * count, count), count)
    kept = pltpu.make_async_copy(block.at[rows], out.at[b], local)
    kept.start()
    return started + [kept]


def blk_peers(n_blk):
    (s, b, u), _, _, _ = place()
    return [(s, (b + j) % n_blk, u) for j in range(1, n_blk)]


def projection_spans(whole, cut, owner, sizes):
    plane = sizes[0] * sizes[2]
    share = whole[0].shape[1] // plane
    at = pl.ds(pl.multiple_of(owner * share, share), share)
    return [(matrix, at, cut, pl.ds(i * share, share)) for i, matrix in enumerate(whole)]


def feed_spans(matrix, cut, owner, sizes):
    n_seq, _, n_uly, runs = sizes
    share = matrix.shape[1] // (n_seq * n_uly * runs)
    spans = []
    for r in range(runs):
        at = ((owner // n_uly) * runs + r) * n_uly + owner % n_uly
        at = pl.ds(pl.multiple_of(at * share, share), share)
        spans.append((matrix, at, cut, pl.ds(r * share, share)))
    return spans


def gather_columns(copy, first, spans, me, device):
    return [
        copy(first + i, matrix.at[:, at], cut.at[me, :, inside], device)
        for i, (matrix, at, cut, inside) in enumerate(spans)
    ]


def return_columns(copy, first, spans, p, device):
    return [
        copy(first + i, cut.at[p, :, inside], matrix.at[:, at], device)
        for i, (matrix, at, cut, inside) in enumerate(spans)
    ]


def plane_peers(plane):
    (s, b, u), _, (_, _, _, me), _ = place()
    n_uly = plane // 2
    others = [(me + j) % plane for j in range(1, plane)]
    return me, [(p, (p // n_uly, b, p % n_uly)) for p in others]


def home(local):
    def copy(i, source, target, _):
        made = pltpu.make_async_copy(source, target, local.at[i])
        made.start()
        return made

    return copy


def entry_kernel(
    sizes, x_ref, wq_ref, wk_ref, wv_ref, fc_ref, *refs
):
    vectors, (bias_ref, lengths_ref), refs = refs[:8], refs[8:10], refs[10:]
    matrices = (wq_ref, wk_ref, wv_ref)
    enter_body(sizes, x_ref, matrices, fc_ref, vectors, bias_ref, lengths_ref, *refs)


def enter_body(
    sizes, x_ref, matrices, fc_ref, short, bias_ref, lengths_ref, tok, qkv, fc, small,
    small_ref, blk_send, blk_recv, plane_send, plane_recv, local,
):
    n_seq, n_blk, n_uly, runs = sizes
    (s, b, u), _, (_, _, _, me), _ = place()
    plane = n_seq * n_uly
    pieces = 3 + runs
    small_ref[...] = jnp.zeros_like(small_ref)
    for i, ref in enumerate(short):
        small_ref[i : i + 1, : ref.shape[1]] = ref[...].astype(F32)
    lanes = min(128, bias_ref.shape[1])
    for i in range(bias_ref.shape[1] // lanes):
        part = bias_ref[:, i * lanes : (i + 1) * lanes].astype(F32)
        small_ref[8 + i : 9 + i, :lanes] = part
    small_ref[SMALL - 1 :, : lengths_ref.shape[1]] = lengths_ref[...].astype(F32)
    me, friends = plane_peers(plane)
    column = blk_peers(n_blk)
    meet([peer for _, peer in friends] + column)
    by_blk = sender(blk_send, blk_recv)
    by_plane = sender(plane_send, plane_recv)
    at_home = home(local)

    def spans(owner):
        return projection_spans(matrices, qkv, owner, sizes) + feed_spans(fc_ref, fc, owner, sizes)

    first = at_home(0, small_ref, small.at[me, b], None)
    vectors, started = [], []
    for j, peer in enumerate(column):
        vectors.append(by_blk(j, small_ref, small.at[me, b], peer))
    for j, peer in enumerate(column):
        started.append(by_blk(n_blk - 1 + j, x_ref.at[peer[1]], tok.at[b], peer))
    for j, (p, peer) in enumerate(friends):
        started += gather_columns(by_plane, pieces * j, spans(p), me, peer)
    started.append(at_home(1, x_ref.at[b], tok.at[b], None))
    started += gather_columns(at_home, 2, spans(me), me, None)
    first.wait()
    for made in vectors:
        made.wait()
    for j, (_, peer) in enumerate(friends):
        at = small.at[me]
        started.append(by_plane(pieces * (plane - 1) + j, at, at, peer))
    for made in started:
        made.wait()


SMALL = 16


def enter(x, weights, fc, short, sizes):
    n_seq, n_blk, n_uly, runs = sizes
    plane = n_seq * n_uly
    rows, width = weights[0].shape
    pieces = (4 + runs) * (plane - 1)
    return pl.pallas_call(
        functools.partial(entry_kernel, sizes),
        name="enter",
        out_shape=(
            jax.ShapeDtypeStruct(x.shape, x.dtype),
            jax.ShapeDtypeStruct((plane, rows, 3 * width // plane), BF),
            jax.ShapeDtypeStruct((plane, rows, fc.shape[1] // plane), BF),
            jax.ShapeDtypeStruct((plane, n_blk, SMALL, 128), F32),
        ),
        in_specs=[ANY] * 5 + [VMEM] * len(short),
        out_specs=(ANY,) * 4,
        scratch_shapes=[
            pltpu.VMEM((SMALL, 128), F32),
            pltpu.SemaphoreType.DMA((2 * (n_blk - 1),)),
            pltpu.SemaphoreType.DMA((2 * (n_blk - 1),)),
            pltpu.SemaphoreType.DMA((pieces,)),
            pltpu.SemaphoreType.DMA((pieces,)),
            pltpu.SemaphoreType.DMA((5 + runs,)),
        ],
        compiler_params=pltpu.CompilerParams(
            collective_id=0, has_side_effects=True, vmem_limit_bytes=GRANT
        ),
        cost_estimate=pl.CostEstimate(flops=0, bytes_accessed=MIB, transcendentals=0),
    )(x, *weights, fc, *short)


def norm_kernel(
    order, n_blk, tok, gain, shift, cot_ref, out, cot, cots,
    own, send, recv, local, c_send, c_recv, c_local, g_send, g_recv, kept,
):
    (s, b, u), near, _, _ = place()
    column = blk_peers(n_blk)
    meet(list(near) + column)
    copy = sender(g_send, g_recv)
    count = cot_ref.shape[1]
    rows = pl.ds(pl.multiple_of(b * count, count), count)
    exchanged = [copy(j, cot_ref.at[peer[1]], cot.at[rows], peer) for j, peer in enumerate(column)]
    exchanged.append(home(kept)(0, cot_ref.at[b], cot.at[rows], None))

    def chunk(at):
        unit, _ = norm_parts(tok[at].astype(F32))
        own[at] = reorder(unit * gain[...] + shift[...], *order).astype(BF)

    each_chunk(own.shape[0], chunk)
    run(spread(own, out, send, recv, local))
    for made in exchanged:
        made.wait()
    run(spread(cot, cots, c_send, c_recv, c_local))


def norm_gather(tok, gain, shift, cot, plane, order):
    rows, width = tok.shape
    n_blk = cot.shape[0]
    return pl.pallas_call(
        functools.partial(norm_kernel, order, n_blk),
        name="norm_gather",
        out_shape=(
            jax.ShapeDtypeStruct((plane, rows, width), BF),
            jax.ShapeDtypeStruct((rows, width), BF),
            jax.ShapeDtypeStruct((plane, rows, width), BF),
        ),
        in_specs=[VMEM] * 3 + [ANY],
        out_specs=(ANY, ANY, ANY),
        scratch_shapes=[pltpu.VMEM((rows, width), BF)]
        + spread_scratch() * 2
        + [
            pltpu.SemaphoreType.DMA((n_blk - 1,)),
            pltpu.SemaphoreType.DMA((n_blk - 1,)),
            pltpu.SemaphoreType.DMA((1,)),
        ],
        compiler_params=pltpu.CompilerParams(
            collective_id=1, has_side_effects=True, vmem_limit_bytes=GRANT
        ),
        cost_estimate=pl.CostEstimate(flops=0, bytes_accessed=MIB, transcendentals=0),
    )(tok, gain, shift, cot)


BLOCK = 256


def document_start(bounds, s, position):
    first, second = bounds[2 * s], bounds[2 * s + 1]
    return jnp.where(position >= second, second, jnp.where(position >= first, first, 0))


def chunks_of(layout):
    n_seq, n_uly, n_blk, part, _ = layout
    for s in range(n_seq):
        for b in range(n_blk):
            for u in range(n_uly):
                yield ((s * n_uly + u) * n_blk + b) * part, s, (b * n_uly + u) * part


def attend_kernel(
    layout, bounds, qkv, mixed, low, natural, attended, logs, mixed_out, u_send, u_recv, u_local
):
    _, _, _, part, heads = layout
    meet(row_peers(mixed.shape[0]))
    mixing = mix_row(mixed, mixed_out, u_send, u_recv, u_local)
    share = heads * HD
    pairs, length = natural.shape[1:3]
    for row, s, position in chunks_of(layout):
        for kind in range(3):
            for h in range(heads):
                lane = kind * share + h * HD
                natural[kind, s * heads + h, position : position + part] = qkv[
                    row : row + part, lane : lane + HD
                ]

    def pair(p, carry):
        for start in range(0, length, BLOCK):
            stop = start + BLOCK
            scores = against(natural[0, p, start:stop], natural[1, p, :stop])
            row = start + lax.broadcasted_iota(jnp.int32, (BLOCK, 1), 0)
            key = lax.broadcasted_iota(jnp.int32, (BLOCK, stop), 1)
            allowed = (key >= document_start(bounds, p // heads, row)) & (key <= row)
            scores = jnp.where(allowed, scores, NEGATIVE)
            top = jnp.max(scores, axis=1, keepdims=True)
            powered = jnp.exp(scores - top)
            total = jnp.sum(powered, axis=1, keepdims=True)
            made = product(powered.astype(BF), natural[2, p, :stop])
            attended[p, start:stop] = made / total
            log_total = jnp.broadcast_to(top + jnp.log(total), (BLOCK, HD))
            logs[p, :, start:stop] = log_total.T[:8]
        return carry

    lax.fori_loop(0, pairs, pair, 0)
    for row, s, position in chunks_of(layout):
        for h in range(heads):
            low[row : row + part, h * HD : (h + 1) * HD] = attended[
                s * heads + h, position : position + part
            ].astype(BF)
    for made in mixing:
        made.wait()


def attend(bounds, qkv, mixed, layout):
    n_seq, n_uly, n_blk, part, heads = layout
    pairs, length = n_seq * heads, n_uly * n_blk * part
    return pl.pallas_call(
        functools.partial(attend_kernel, layout),
        name="attend",
        out_shape=(
            jax.ShapeDtypeStruct((qkv.shape[0], heads * HD), BF),
            jax.ShapeDtypeStruct((3, pairs, length, HD), BF),
            jax.ShapeDtypeStruct((pairs, length, HD), F32),
            jax.ShapeDtypeStruct((pairs, 8, length), F32),
            jax.ShapeDtypeStruct(mixed.shape, BF),
        ),
        in_specs=[pl.BlockSpec(memory_space=pltpu.SMEM), VMEM, ANY],
        out_specs=(VMEM, VMEM, VMEM, VMEM, ANY),
        scratch_shapes=mix_scratch(mixed.shape[0]),
        compiler_params=pltpu.CompilerParams(
            collective_id=2, has_side_effects=True, vmem_limit_bytes=GRANT
        ),
        cost_estimate=pl.CostEstimate(flops=0, bytes_accessed=MIB, transcendentals=0),
    )(bounds, qkv, mixed)


def attend_back_kernel(
    layout, scale, fused, bounds, grad, natural, attended, logs, mine_ref, own_ref, hid, bias,
    mixed, normed_ref, back, out, mixed_out, *refs
):
    weights, refs = (refs[0], refs[1:]) if fused else (None, refs)
    (
        grads, grads_back, key_grad, value_grad, mixed_in, normed, n_sems,
        total, mine, in_x, in_y, c_send, c_recv, u_send, u_recv, u_local,
    ) = refs
    (s, b, u), near, _, _ = place()
    rows = total.shape[0]
    _, _, _, part, heads = layout
    share = heads * HD
    first = fetch((mine_ref.at[0], mine_ref.at[1], mine_ref.at[2], own_ref),
                  (mine.at[0], mine.at[1], mine.at[2], total), n_sems)
    if fused:
        loading = pltpu.make_async_copy(normed_ref, normed, n_sems.at[4])
        loading.start()
    meet([near[1]] + row_peers(mixed.shape[0]))
    cross = Cross(total, mine, in_x, in_y, c_send, c_recv, rows // 4)
    for k in range(3):
        first[k].wait()
        cross.begin(k)
    target = mixed_in if fused else mixed_out
    mixing = mix_row(mixed, target, u_send, u_recv, u_local)
    pairs, length = natural.shape[1:3]
    for row, s_at, position in chunks_of(layout):
        for h in range(heads):
            grads[s_at * heads + h, position : position + part] = grad[
                row : row + part, h * HD : (h + 1) * HD
            ]

    def pair(p, carry):
        for start in reversed(range(0, length, BLOCK)):
            stop = start + BLOCK
            query, key, value = (
                natural[0, p, start:stop], natural[1, p, :stop], natural[2, p, :stop]
            )
            above = grads[p, start:stop]
            row = start + lax.broadcasted_iota(jnp.int32, (1, BLOCK), 1)
            at = lax.broadcasted_iota(jnp.int32, (stop, BLOCK), 0)
            allowed = (at >= document_start(bounds, p // heads, row)) & (at <= row)
            scores = jnp.where(allowed, against(key, query), NEGATIVE)
            chances = jnp.exp(scores - logs[p, 0:1, start:stop])
            dots = (above.astype(F32) * attended[p, start:stop]).T
            dots = jnp.sum(dots, axis=0, keepdims=True)
            by_value = product(chances.astype(BF), above)
            scored = (chances * (against(value, above) - dots)).astype(BF)
            by_key = product(scored, query)
            grads_back[p, start:stop] = (transposed(scored, key) * scale).astype(BF)
            if stop == length:
                key_grad[...] = by_key
                value_grad[...] = by_value
            else:
                key_grad[:stop] += by_key
                value_grad[:stop] += by_value
        grads_back[pairs + p] = key_grad[...].astype(BF)
        grads_back[2 * pairs + p] = value_grad[...].astype(BF)
        return carry

    cut = (pairs + 1) // 2
    lax.fori_loop(0, cut, pair, 0)
    cross.diagonals()
    lax.fori_loop(cut, pairs, pair, 0)
    for row, s_at, position in chunks_of(layout):
        for kind in range(3):
            for h in range(heads):
                lane = kind * share + h * HD
                back[row : row + part, lane : lane + HD] = grads_back[
                    kind * pairs + s_at * heads + h, position : position + part
                ]
    for made in mixing:
        made.wait()
    if fused:
        loading.wait()
        weight_terms(normed, back, mixed_in, weights)
        mixed_out[...] = jnp.zeros_like(mixed_out)
    first[3].wait()
    cross.finish()

    def chunk(at):
        out[at] = (total[at] + hid[at] + bias[...]).astype(BF)

    each_chunk(rows, chunk)


def attend_back(
    bounds, grad, natural, attended, logs, mine, own, hid, bias, mixed, normed, layout, scale,
    fused,
):
    rows, width = hid.shape
    pairs, length = natural.shape[1:3]
    wide = 3 * grad.shape[1]
    out_shape = (
        jax.ShapeDtypeStruct((grad.shape[0], wide), BF),
        jax.ShapeDtypeStruct((rows, width), BF),
        jax.ShapeDtypeStruct((16, 128) if fused else mixed.shape, BF),
    )
    out_specs = (VMEM, VMEM, VMEM if fused else ANY)
    if fused:
        out_shape += (jax.ShapeDtypeStruct((normed.shape[1], 4 * grad.shape[1]), BF),)
        out_specs += (VMEM,)
    return pl.pallas_call(
        functools.partial(attend_back_kernel, layout, scale, fused),
        name="attend_back",
        out_shape=out_shape,
        in_specs=[pl.BlockSpec(memory_space=pltpu.SMEM)]
        + [VMEM] * 4
        + [ANY] * 2
        + [VMEM] * 2
        + [ANY] * 2,
        out_specs=out_specs,
        scratch_shapes=[
            pltpu.VMEM((pairs, length, HD), BF),
            pltpu.VMEM((3 * pairs, length, HD), BF),
            pltpu.VMEM((length, HD), F32),
            pltpu.VMEM((length, HD), F32),
            pltpu.VMEM(mixed.shape if fused else (16, 128), BF),
            pltpu.VMEM(normed.shape if fused else (16, 128), BF),
            pltpu.SemaphoreType.DMA((5,)),
            pltpu.VMEM((rows, width), F32),
        ]
        + cross_scratch(rows, width, rows // 4)
        + mix_scratch(mixed.shape[0]),
        compiler_params=pltpu.CompilerParams(
            collective_id=5, has_side_effects=True, vmem_limit_bytes=GRANT
        ),
        cost_estimate=pl.CostEstimate(flops=0, bytes_accessed=MIB, transcendentals=0),
    )(bounds, grad, natural, attended, logs, mine, own, hid, bias, mixed, normed)


def mix_row(source, target, send, recv, local):
    (s, b, u), _, _, _ = place()
    copy = sender(send, recv)
    made = [
        copy(j, source.at[to[2]], target.at[u], to)
        for j, to in enumerate(row_peers(source.shape[0]))
    ]
    kept = pltpu.make_async_copy(source.at[u], target.at[u], local)
    kept.start()
    return made + [kept]


def row_peers(n_uly):
    (s, b, u), _, _, _ = place()
    return [(s, b, (u + j) % n_uly) for j in range(1, n_uly)]


def mix_scratch(n_uly):
    return [
        pltpu.SemaphoreType.DMA((n_uly - 1,)),
        pltpu.SemaphoreType.DMA((n_uly - 1,)),
        pltpu.SemaphoreType.DMA,
    ]


def rows_of(ref, block, rows):
    return ref[pl.ds(pl.multiple_of(block * rows, rows), rows), :]


def hidden_kernel(
    order, act, weight, tok, bias, gain, shift, hidden, own,
    total, to_twin, from_twin, mine, in_x, in_y, c_send, c_recv,
):
    _, near, _, _ = place()
    rows = total.shape[0]
    meet(near)

    def multiply(block, cols):
        return product(rows_of(act, block, rows), weight[:, cols])

    run(collect(multiply, total, to_twin, from_twin, mine, in_x, in_y, c_send, c_recv))

    def chunk(at):
        values = total[at] + tok[at].astype(F32) + bias[...]
        hidden[at] = values
        unit, _ = norm_parts(values)
        own[at] = reorder(unit * gain[...] + shift[...], *order).astype(BF)

    each_chunk(rows, chunk)


def hidden_norm(act, weight, tok, bias, gain, shift, order):
    rows, width = tok.shape
    return pl.pallas_call(
        functools.partial(hidden_kernel, order),
        name="hidden_norm",
        out_shape=(
            jax.ShapeDtypeStruct((rows, width), F32),
            jax.ShapeDtypeStruct((rows, width), BF),
        ),
        in_specs=[VMEM] * 6,
        out_specs=(VMEM, VMEM),
        scratch_shapes=collect_scratch(rows, width),
        compiler_params=pltpu.CompilerParams(
            collective_id=3, has_side_effects=True, vmem_limit_bytes=GRANT
        ),
        cost_estimate=pl.CostEstimate(flops=0, bytes_accessed=MIB, transcendentals=0),
    )(act, weight, tok, bias, gain, shift)


def spread_scratch():
    return [
        pltpu.SemaphoreType.DMA((SPREAD,)),
        pltpu.SemaphoreType.DMA((SPREAD,)),
        pltpu.SemaphoreType.DMA,
    ]


def block_rows(block, rows):
    return pl.ds(pl.multiple_of(block * rows, rows), rows)


def fetch(sources, targets, sems):
    made = [
        pltpu.make_async_copy(source, target, sems.at[i])
        for i, (source, target) in enumerate(zip(sources, targets))
    ]
    for copy in made:
        copy.start()
    return made


def pairs_of(moving):
    diag, on_x, on_y, me = moving.blocks
    twin_diag, twin_x, twin_y, twin = moving.twins
    moving.own_blocks()
    yield me, twin
    moving.first_halves()
    moving.second_halves()
    yield on_x, on_y
    moving.twin_sides()
    yield twin_x, twin_y
    moving.diagonals()
    yield diag, twin_diag
    moving.close()


FF_TILE = 1024
FC_TILE = 256


def feed_kernel(
    own, weight_ref, bias, cots, out, active, slope, grad,
    weight, rows_in, cots_in, low_out, steep_out, acc, w_sem, sems, out_sems, send, recv, local,
):
    _, near, _, _ = place()
    rows, width = own.shape
    ff = weight.shape[1]
    loading = pltpu.make_async_copy(weight_ref, weight, w_sem)
    loading.start()
    halves = (pl.ds(0, rows), pl.ds(rows, rows))
    meet(near)
    moving = Spread(own, out, send, recv, local)
    diag, on_x, on_y, me = moving.blocks
    twin_diag, twin_x, twin_y, twin = moving.twins
    plan = [(me, twin), (on_x, on_y), (twin_x, twin_y), (diag, twin_diag)]

    def cots_of(i):
        return fetch(
            [cots.at[p] for p in plan[i]], [cots_in.at[i % 2, h] for h in halves], sems.at[i % 2]
        )

    arriving = cots_of(0)
    leaving = {}
    for i, (left, right) in enumerate(pairs_of(moving)):
        fetched = fetch([out.at[left], out.at[right]], [rows_in.at[h] for h in halves], sems.at[2])
        for made in fetched + arriving:
            made.wait()
        if i == 0:
            loading.wait()
        if i < 3:
            arriving = cots_of(i + 1)
        for made in leaving.pop(i - 2, []):
            made.wait()

        def tile(t, carry, i=i):
            at = pl.ds(pl.multiple_of(t * FF_TILE, FF_TILE), FF_TILE)
            inner = product(rows_in[...], weight[:, at]) + bias[:, at]
            bent = math.sqrt(2 / math.pi) * (inner + 0.044715 * (inner * inner * inner))
            curve = jnp.tanh(bent)
            low = (0.5 * inner * (1.0 + curve)).astype(BF)
            steep = math.sqrt(2 / math.pi) * (1.0 + 3 * 0.044715 * (inner * inner))
            steep = 0.5 * (1.0 + curve) + 0.5 * inner * (1.0 - curve * curve) * steep
            low_out[i % 2, :, at] = low
            steep_out[i % 2, :, at] = steep.astype(BF)
            for cut in range(0, width, 1024):
                cols = pl.ds(cut, 1024)
                term = transposed(low, cots_in[i % 2, :, cols])
                if i == 0:
                    acc[at, cols] = term
                elif i < 3:
                    acc[at, cols] += term
                else:
                    grad[at, cols] = (acc[at, cols] + term).astype(BF)
            return carry

        lax.fori_loop(0, ff // FF_TILE, tile, 0)
        places = [block_rows(left, rows), block_rows(right, rows)]
        leaving[i] = fetch(
            [held.at[i % 2, h] for held in (low_out, steep_out) for h in halves],
            [kept.at[p] for kept in (active, slope) for p in places],
            out_sems.at[i % 2],
        )
    for group in leaving.values():
        for made in group:
            made.wait()


def feed(own, weight, bias, cots):
    rows, width = own.shape
    plane, ff = cots.shape[0], weight.shape[1]
    return pl.pallas_call(
        feed_kernel,
        name="feed",
        out_shape=(
            jax.ShapeDtypeStruct((plane, rows, width), BF),
            jax.ShapeDtypeStruct((plane * rows, ff), BF),
            jax.ShapeDtypeStruct((plane * rows, ff), BF),
            jax.ShapeDtypeStruct((ff, width), BF),
        ),
        in_specs=[VMEM, ANY, VMEM, ANY],
        out_specs=(ANY, ANY, ANY, VMEM),
        scratch_shapes=[
            pltpu.VMEM(weight.shape, BF),
            pltpu.VMEM((2 * rows, width), BF),
            pltpu.VMEM((2, 2 * rows, width), BF),
            pltpu.VMEM((2, 2 * rows, ff), BF),
            pltpu.VMEM((2, 2 * rows, ff), BF),
            pltpu.VMEM((ff, width), F32),
            pltpu.SemaphoreType.DMA,
            pltpu.SemaphoreType.DMA((3, 2)),
            pltpu.SemaphoreType.DMA((2, 4)),
        ]
        + spread_scratch(),
        compiler_params=pltpu.CompilerParams(
            collective_id=8, has_side_effects=True, vmem_limit_bytes=GRANT
        ),
        cost_estimate=pl.CostEstimate(flops=0, bytes_accessed=MIB, transcendentals=0),
    )(own, weight, bias, cots)


def back_feed_kernel(
    order, cots, slope, normed_ref, proj, weight, hid, cot, gain,
    fc_grad, grad_hidden, own, sums, bias,
    inner_grad, normed, cots_in, slope_in, sems, n_sem,
    total, to_twin, from_twin, mine, in_x, in_y, c_send, c_recv,
):
    _, near, here, other = place()
    rows, width = total.shape
    ff = weight.shape[1]
    plan = [other[0], other[1], here[0], other[2], here[1], other[3], here[2], here[3]]

    def load(i):
        at = i % 2
        return fetch(
            (cots.at[plan[i]], slope.at[block_rows(plan[i], rows)]),
            (cots_in.at[at], slope_in.at[at]),
            sems.at[at],
        )

    loads = [load(0)]
    normed_load = pltpu.make_async_copy(normed_ref, normed, n_sem)
    normed_load.start()
    sums[...] = jnp.zeros_like(sums)
    bias[...] = jnp.zeros_like(bias)
    meet(near)

    def prepare(block):
        i = len(loads) - 1
        for made in loads[i]:
            made.wait()
        loads.append(load(i + 1) if i + 1 < len(plan) else [])

        def tile(t, carry):
            at = pl.ds(pl.multiple_of(t * FF_TILE, FF_TILE), FF_TILE)
            made = against(cots_in[i % 2], proj[at, :]) * slope_in[i % 2, :, at].astype(F32)
            low = made.astype(BF)
            inner_grad[block_rows(block, rows), at] = low
            bias[0:1, at] += row_sum(low.astype(F32))
            return carry

        lax.fori_loop(0, ff // FF_TILE, tile, 0)

    def multiply(block, cols):
        return against(rows_of(inner_grad, block, rows), weight[cols, :])

    def fc_tile(t, carry):
        at = pl.ds(pl.multiple_of(t * FC_TILE, FC_TILE), FC_TILE)
        fc_grad[at, :] = transposed(normed[:, at], inner_grad[...]).astype(BF)
        return carry

    moving = collect(
        multiply, total, to_twin, from_twin, mine, in_x, in_y, c_send, c_recv, prepare
    )
    next(moving)
    next(moving)
    normed_load.wait()
    lax.fori_loop(0, width // FC_TILE, fc_tile, 0)
    run(moving)
    inner, outer, lanes = order[1], order[0], order[2]

    def chunk(at):
        grad = reorder(total[at], inner, outer, lanes)
        back, by_gain = norm_back(grad, hid[at], gain[...])
        passed = cot[at].astype(F32)
        back = back + passed
        grad_hidden[at] = back
        low = back.astype(BF)
        own[at] = low
        sums[0:1] += row_sum(by_gain)
        sums[1:2] += row_sum(grad)
        sums[2:3] += row_sum(low.astype(F32))
        sums[3:4] += row_sum(passed)

    each_chunk(rows, chunk)


def back_feed(cots, slope, normed, proj, weight, hid, cot, gain, order):
    rows, width = cot.shape
    ff = weight.shape[1]
    return pl.pallas_call(
        functools.partial(back_feed_kernel, order),
        name="back_feed",
        out_shape=(
            jax.ShapeDtypeStruct((width, ff), BF),
            jax.ShapeDtypeStruct((rows, width), F32),
            jax.ShapeDtypeStruct((rows, width), BF),
            jax.ShapeDtypeStruct((8, width), F32),
            jax.ShapeDtypeStruct((8, ff), F32),
        ),
        in_specs=[ANY] * 3 + [VMEM] * 5,
        out_specs=(VMEM,) * 5,
        scratch_shapes=[
            pltpu.VMEM((slope.shape[0], ff), BF),
            pltpu.VMEM(normed.shape, BF),
            pltpu.VMEM((2, rows, width), BF),
            pltpu.VMEM((2, rows, ff), BF),
            pltpu.SemaphoreType.DMA((2, 2)),
            pltpu.SemaphoreType.DMA,
        ]
        + collect_scratch(rows, width),
        compiler_params=pltpu.CompilerParams(
            collective_id=4, has_side_effects=True, vmem_limit_bytes=GRANT
        ),
        cost_estimate=pl.CostEstimate(flops=0, bytes_accessed=MIB, transcendentals=0),
    )(cots, slope, normed, proj, weight, hid, cot, gain)


def branch_kernel(
    own, weight, low, act_ref, proj_ref, out, heads_grad, weight_grad, mine, total,
    act, proj, rows_in, acc, sems, to_twin, from_twin, c_send, c_recv, a_sems, send, recv, local,
):
    _, near, _, _ = place()
    rows, width = own.shape
    loading = fetch((act_ref, proj_ref), (act, proj), a_sems)
    meet(near)
    moving = Spread(own, out, send, recv, local)

    def multiply(block, cols):
        return product(rows_of(act, block, rows), proj[:, cols])

    chip = ChipSums(multiply, total, to_twin, from_twin, mine, c_send, c_recv)
    for i, (left, right) in enumerate(pairs_of(moving)):
        fetched = fetch(
            (out.at[left], out.at[right]),
            (rows_in.at[pl.ds(0, rows)], rows_in.at[pl.ds(rows, rows)]),
            sems,
        )
        for made in fetched:
            made.wait()
        grads = against(rows_in[...], weight[...]).astype(BF)
        heads_grad[block_rows(left, rows)] = grads[:rows]
        heads_grad[block_rows(right, rows)] = grads[rows:]
        kept = jnp.concatenate(
            [low[block_rows(left, rows), :], low[block_rows(right, rows), :]], axis=0
        )
        for cut in range(0, width, 1024):
            cols = pl.ds(cut, 1024)
            term = transposed(kept, rows_in[:, cols])
            if i == 0:
                acc[:, cols] = term
            elif i < 3:
                acc[:, cols] += term
            else:
                weight_grad[:, cols] = (acc[:, cols] + term).astype(BF)
        if i == 0:
            for made in loading:
                made.wait()
            for k in range(4):
                chip.for_twin(k)
        elif i == 1:
            for k in range(4):
                chip.for_here(k)
    chip.close()


def branch_spread(own, weight, low, act, proj, plane):
    rows, width = own.shape
    share = weight.shape[0]
    return pl.pallas_call(
        branch_kernel,
        name="branch_spread",
        out_shape=(
            jax.ShapeDtypeStruct((plane, rows, width), BF),
            jax.ShapeDtypeStruct((plane * rows, share), BF),
            jax.ShapeDtypeStruct((share, width), BF),
            jax.ShapeDtypeStruct((3, rows, width), BF),
            jax.ShapeDtypeStruct((rows, width), F32),
        ),
        in_specs=[VMEM] * 3 + [ANY] * 2,
        out_specs=(ANY, VMEM, VMEM, VMEM, VMEM),
        scratch_shapes=[
            pltpu.VMEM(act.shape, BF),
            pltpu.VMEM(proj.shape, BF),
            pltpu.VMEM((2 * rows, width), BF),
            pltpu.VMEM((share, width), F32),
            pltpu.SemaphoreType.DMA((2,)),
        ]
        + chip_scratch(rows, width)
        + [pltpu.SemaphoreType.DMA((4,))] * 2
        + [pltpu.SemaphoreType.DMA((2,))]
        + spread_scratch(),
        compiler_params=pltpu.CompilerParams(
            collective_id=9, has_side_effects=True, vmem_limit_bytes=GRANT
        ),
        cost_estimate=pl.CostEstimate(flops=0, bytes_accessed=MIB, transcendentals=0),
    )(own, weight, low, act, proj)


def inputs_kernel(
    sizes, order, act, weight, tok, grad_hidden, gain, fc_ref, sums_two, sums_fc, sums_qkv,
    small, out, fc, sums, stacked, parts, gathered, partial, arrived,
    s_send, s_recv, b_send, b_recv, s_local,
    total, to_twin, from_twin, mine, in_x, in_y, c_send, c_recv, own,
    send, recv, local, f_send, f_recv, f_local,
):
    n_seq, n_blk, n_uly, runs = sizes
    rows = total.shape[0]
    me, friends = plane_peers(n_seq * n_uly)
    meet([peer for _, peer in friends] + blk_peers(n_blk))

    def multiply(block, cols):
        return against(rows_of(act, block, rows), weight[cols, :])

    run(collect(multiply, total, to_twin, from_twin, mine, in_x, in_y, c_send, c_recv))
    spans = feed_spans(fc, fc_ref, me, sizes)
    leaving = return_columns(home(f_local), 0, spans, me, None)
    for j, (p, peer) in enumerate(friends):
        leaving += return_columns(sender(f_send, f_recv), runs * j, spans, p, peer)
    sums[...] = jnp.zeros_like(sums)
    inner, outer, lanes = order[1], order[0], order[2]

    def chunk(at):
        grad = reorder(total[at], inner, outer, lanes)
        back, by_gain = norm_back(grad, tok[at].astype(F32), gain[...])
        own[at] = (grad_hidden[at] + back).astype(BF)
        sums[0:1] += row_sum(by_gain)
        sums[1:2] += row_sum(grad)

    each_chunk(rows, chunk)
    leaving += return_rows(own, out, n_blk, send, recv, local)
    width = total.shape[1]
    share = sums_qkv.shape[1] // 3
    mine_at = pl.ds(pl.multiple_of(me * share, share), share)
    stacked[0:2] = sums[0:2]
    stacked[2:4] = jnp.zeros((2, width), F32)
    stacked[2:3, mine_at] = sums_qkv[:, :share]
    stacked[3:4, mine_at] = sums_qkv[:, 2 * share :]
    stacked[4:5] = sums_two[2:3]
    stacked[5:7] = sums_two[0:2]
    stacked[7:8] = sums_two[3:4]
    parts[...] = jnp.zeros_like(parts)
    lanes = width // (n_seq * n_blk * n_uly)
    for s in range(n_seq):
        for b in range(n_blk):
            for u in range(n_uly):
                at = ((s * n_blk + b) * n_uly + u) * lanes
                parts[s * n_uly + u, b, 0:8, 0:lanes] = stacked[:, at : at + lanes]
    hidden_rows = sums_fc.shape[1] // n_blk
    lanes = min(128, hidden_rows)
    for b in range(n_blk):
        for i in range(hidden_rows // lanes):
            at = b * hidden_rows + i * lanes
            parts[me, b, 8 + i : 9 + i, 0:lanes] = sums_fc[0:1, at : at + lanes]
    here_blk = lax.axis_index("blk")
    at_home, to_plane, to_blk = home(s_local), sender(s_send, s_recv), sender(b_send, b_recv)
    moved = [at_home(0, parts.at[me], gathered.at[me], None)]
    moved += [
        to_plane(j, parts.at[p], gathered.at[me], peer) for j, (p, peer) in enumerate(friends)
    ]
    for made in moved:
        made.wait()
    partial[...] = jnp.sum(gathered[...], axis=0)
    moved = [at_home(1, partial.at[here_blk], arrived.at[here_blk], None)]
    moved += [
        to_blk(j, partial.at[peer[1]], arrived.at[here_blk], peer)
        for j, peer in enumerate(blk_peers(n_blk))
    ]
    for made in moved:
        made.wait()
    small[...] = jnp.sum(arrived[...], axis=0)
    for made in leaving:
        made.wait()


def inputs_return(
    act, weight, tok, grad_hidden, gain, fc, sums_two, sums_fc, sums_qkv, sizes, order
):
    rows, width = tok.shape
    n_blk, runs = sizes[1], sizes[3]
    plane = fc.shape[0]
    return pl.pallas_call(
        functools.partial(inputs_kernel, sizes, order),
        name="inputs_return",
        out_shape=(
            jax.ShapeDtypeStruct((SMALL, 128), F32),
            jax.ShapeDtypeStruct((n_blk, rows // n_blk, width), BF),
            jax.ShapeDtypeStruct((fc.shape[1], plane * fc.shape[2]), BF),
        ),
        in_specs=[VMEM] * 5 + [ANY] + [VMEM] * 3,
        out_specs=(VMEM, ANY, ANY),
        scratch_shapes=[
            pltpu.VMEM((8, width), F32),
            pltpu.VMEM((8, width), F32),
            pltpu.VMEM((plane, n_blk, SMALL, 128), F32),
            pltpu.VMEM((plane, n_blk, SMALL, 128), F32),
            pltpu.VMEM((n_blk, SMALL, 128), F32),
            pltpu.VMEM((n_blk, SMALL, 128), F32),
        ]
        + [pltpu.SemaphoreType.DMA((plane - 1,))] * 2
        + [pltpu.SemaphoreType.DMA((n_blk - 1,))] * 2
        + [pltpu.SemaphoreType.DMA((2,))]
        + collect_scratch(rows, width)
        + [pltpu.VMEM((rows, width), BF)]
        + [pltpu.SemaphoreType.DMA((n_blk - 1,))] * 2
        + [pltpu.SemaphoreType.DMA]
        + [pltpu.SemaphoreType.DMA((runs * (plane - 1),))] * 2
        + [pltpu.SemaphoreType.DMA((runs,))],
        compiler_params=pltpu.CompilerParams(
            collective_id=6, has_side_effects=True, vmem_limit_bytes=GRANT
        ),
        cost_estimate=pl.CostEstimate(flops=0, bytes_accessed=MIB, transcendentals=0),
    )(act, weight, tok, grad_hidden, gain, fc, sums_two, sums_fc, sums_qkv)


def weight_terms(left, right, mixed, out):
    wide = right.shape[1]
    share = out.shape[1] - wide
    pieces = left.shape[1] // share
    rows = mixed.shape[1]

    def tile(t, carry):
        at = pl.ds(pl.multiple_of(t * FC_TILE, FC_TILE), FC_TILE)
        out[at, :wide] = transposed(left[:, at], right[...]).astype(BF)
        return carry

    lax.fori_loop(0, out.shape[0] // FC_TILE, tile, 0)
    for at in range(0, mixed.shape[0] * rows, rows):
        b, first = at // rows, at * pieces
        for j in range(pieces):
            to = first + j * rows
            out[to : to + rows, wide:] = mixed[b, :, j * share : (j + 1) * share]


def weight_grad(left, right, mixed):
    width = left.shape[1]
    return pl.pallas_call(
        weight_terms,
        name="weight_grad",
        out_shape=jax.ShapeDtypeStruct((width, 4 * right.shape[1] // 3), BF),
        in_specs=[VMEM] * 3,
        out_specs=VMEM,
        compiler_params=pltpu.CompilerParams(vmem_limit_bytes=GRANT),
        cost_estimate=pl.CostEstimate(flops=0, bytes_accessed=MIB, transcendentals=0),
    )(left, right, mixed)


def end_kernel(
    sizes, qkv_ref, result_ref, gq, gk, gv, result,
    plane_send, plane_recv, local, r_send, r_recv, r_local,
):
    n_seq, n_blk, n_uly, _ = sizes
    me, friends = plane_peers(n_seq * n_uly)
    meet([peer for _, peer in friends] + blk_peers(n_blk))
    spans = projection_spans((gq, gk, gv), qkv_ref, me, sizes)
    started = return_rows(result_ref, result, n_blk, r_send, r_recv, r_local)
    for j, (p, peer) in enumerate(friends):
        started += return_columns(sender(plane_send, plane_recv), 3 * j, spans, p, peer)
    started += return_columns(home(local), 0, spans, me, None)
    for made in started:
        made.wait()


def finish(qkv, result, sizes):
    n_seq, n_blk, n_uly, _ = sizes
    plane = n_seq * n_uly
    rows, share = qkv.shape[1], qkv.shape[2] // 4
    whole = jax.ShapeDtypeStruct((rows, plane * share), BF)
    back = jax.ShapeDtypeStruct((n_blk, result.shape[0] // n_blk, result.shape[1]), BF)
    return pl.pallas_call(
        functools.partial(end_kernel, sizes),
        name="finish",
        out_shape=(whole, whole, whole, back),
        in_specs=[ANY] * 2,
        out_specs=(ANY,) * 4,
        scratch_shapes=[pltpu.SemaphoreType.DMA((3 * (plane - 1),))] * 2
        + [pltpu.SemaphoreType.DMA((3,))]
        + [pltpu.SemaphoreType.DMA((n_blk - 1,))] * 2
        + [pltpu.SemaphoreType.DMA],
        compiler_params=pltpu.CompilerParams(
            collective_id=7, has_side_effects=True, vmem_limit_bytes=16 * MIB
        ),
        cost_estimate=pl.CostEstimate(flops=0, bytes_accessed=MIB, transcendentals=0),
    )(qkv, result)


def on_device(
    inputs,
    doc_lengths,
    ln1_gain,
    ln1_shift,
    w_query,
    b_query,
    w_key,
    w_value,
    b_value,
    w_out,
    b_out,
    ln2_gain,
    ln2_shift,
    w_fc,
    b_fc,
    w_proj,
    b_proj,
    cotangent,
):
    seqs, tok, width = inputs.shape
    n_seq, n_blk, n_uly = (lax.axis_size(a) for a in ALL)
    plane = n_seq * n_uly
    here_seq, here_blk, here_uly = (lax.axis_index(a) for a in ALL)
    here = here_seq * n_uly + here_uly
    scale = 1.0 / math.sqrt(HD)
    rows = w_query.shape[0]
    hidden_rows = w_proj.shape[0]
    share = width // plane
    heads = share // HD
    ff_share = hidden_rows * n_blk
    sharing = max(1, n_blk // seqs)
    held = seqs * sharing // n_blk
    part = tok // sharing
    n_rows = n_blk * held * part
    order = (n_seq, n_blk, n_uly * rows)

    def by_plane(block):
        block = block.reshape(n_blk // sharing, held, sharing, part, width)
        return block.transpose(0, 2, 1, 3, 4).reshape(n_blk, held * part, width)

    def from_plane(block):
        block = block.reshape(n_blk // sharing, sharing, held, part, width)
        return block.transpose(0, 2, 1, 3, 4).reshape(seqs, tok, width)

    vectors = (ln1_gain, ln1_shift, b_query, b_value, b_out, ln2_gain, ln2_shift, b_proj)
    vectors += (b_fc, doc_lengths.reshape(-1))
    runs = n_blk if hidden_rows % 128 == 0 else 1
    sizes = (n_seq, n_blk, n_uly, runs)
    by_block = (rows, n_seq, n_blk, n_uly, hidden_rows)
    by_device = (rows, n_seq, n_uly, n_blk, hidden_rows)
    if runs == 1:
        w_fc = w_fc.reshape(by_block).transpose(0, 1, 3, 2, 4).reshape(rows, -1)
    tokens, qkv, fc, small = enter(
        by_plane(inputs), (w_query, w_key, w_value), w_fc, [v.reshape(1, -1) for v in vectors], sizes
    )
    tokens = tokens.reshape(n_rows, width)

    def over_blk(matrix):
        return lax.all_gather(matrix, "blk", axis=0, tiled=True)

    out_part = over_blk(w_out)
    tokens, out_part = lax.optimization_barrier((tokens, out_part))
    qkv = over_blk(qkv.reshape(plane * rows, 3 * share))
    small = small.reshape(n_seq, n_uly, n_blk, SMALL, 128)
    flat = small[:, :, :, :8, :rows].transpose(3, 0, 2, 1, 4).reshape(8, 1, width)
    whole = [flat[i] for i in range(8)]
    lanes = min(128, hidden_rows)
    bias_fc = lax.dynamic_slice(
        small, (here_seq, here_uly, 0, 8, 0), (1, 1, n_blk, hidden_rows // lanes, lanes)
    ).reshape(1, ff_share)
    lengths = small[:, 0, 0, SMALL - 1, : doc_lengths.size].astype(jnp.int32)
    lengths = lengths.reshape(n_seq, *doc_lengths.shape)
    gain_one, shift_one, bias_q, bias_v, bias_out, gain_two, shift_two, bias_proj = whole
    mine = lambda v: lax.dynamic_slice(v, (0, here * share), (1, share))
    bias_q, bias_v = mine(bias_q), mine(bias_v)

    normed, grad_out, grad_all = norm_gather(
        tokens, gain_one, shift_one, by_plane(cotangent), plane, order
    )
    fc = over_blk(fc.reshape(plane * rows, ff_share))
    normed = normed.reshape(plane * n_rows, width)
    made = product(normed, qkv)
    bias_all = jnp.concatenate([bias_q, jnp.zeros_like(bias_q), bias_v], axis=1)
    scales = jnp.repeat(jnp.array([[scale, 1.0, 1.0]], F32), share, axis=1)
    made = ((made + bias_all) * scales).astype(BF)

    made, w_proj = lax.optimization_barrier((made, w_proj))
    proj = over_blk(w_proj)

    groups = [
        [g * sharing + i for i in range(sharing)] for g in range(n_blk // sharing)
    ]
    pairs = n_seq * held * heads // sharing
    length = n_blk * n_uly * tok
    if sharing == held == 1:
        layout = (n_seq, n_uly, n_blk, part, heads)
    else:
        layout = (pairs, 1, 1, length, 1)

    def to_heads(matrix, kinds):
        if sharing == held == 1:
            return matrix
        matrix = matrix.reshape(n_seq, n_uly, n_blk, held, part, kinds, heads, HD)
        matrix = matrix.transpose(0, 3, 6, 2, 1, 4, 5, 7)
        matrix = matrix.reshape(n_seq * held * heads, n_blk, n_uly, 1, part, kinds * HD)
        if sharing > 1:
            matrix = lax.all_to_all(
                matrix, "blk", split_axis=0, concat_axis=3, axis_index_groups=groups, tiled=True
            )
        return matrix.reshape(pairs * length, kinds * HD)

    def from_heads(matrix, kinds):
        if sharing == held == 1:
            return matrix
        matrix = matrix.reshape(pairs, n_blk, n_uly, sharing, part, kinds * HD)
        if sharing > 1:
            matrix = lax.all_to_all(
                matrix, "blk", split_axis=3, concat_axis=0, axis_index_groups=groups, tiled=True
            )
        matrix = matrix.reshape(n_seq, held, heads, n_blk, n_uly, part, kinds, HD)
        matrix = matrix.transpose(0, 4, 3, 1, 5, 6, 2, 7)
        return matrix.reshape(plane * n_rows, kinds * share)

    turn = here_blk % sharing
    pair_at = turn * pairs + jnp.arange(layout[0]) * layout[4]
    seq_of = pair_at // (held * heads)
    held_of = (pair_at // heads) % held
    which = (here_blk // sharing) * held + held_of
    own_lengths = lengths[seq_of, which]
    first = own_lengths[:, 0:1]
    bounds = jnp.concatenate([first, first + own_lengths[:, 1:2]], axis=1).reshape(-1)

    out_part = out_part.reshape(n_uly, n_blk // n_uly * rows, width)
    attended_low, natural, attended, logs, out_part = attend(
        bounds, to_heads(made, 3), out_part, layout
    )
    out_part = out_part.reshape(n_uly, n_blk // n_uly, rows, width)
    out_part = out_part.transpose(1, 0, 2, 3).reshape(share, width)
    attended_low = from_heads(attended_low, 1)
    hidden, own_two = hidden_norm(
        attended_low, out_part, tokens, bias_out, gain_two, shift_two, order
    )
    normed_two, active, slope, grad_proj = feed(own_two, fc, bias_fc, grad_all)

    def sum_blk(matrix):
        return lax.psum_scatter(matrix, "blk", scatter_dimension=0, tiled=True)

    grad_w_proj = sum_blk(grad_proj)
    grad_fc, grad_hidden, branch, sums_two, sums_fc = back_feed(
        grad_all, slope, normed_two.reshape(plane * n_rows, width), proj, fc, hidden, grad_out, gain_two, order
    )
    _, grad_heads, grad_w_out, chip_sums, own_sum = branch_spread(
        branch, out_part, attended_low, active, proj, plane
    )
    grad_fc = sum_blk(grad_fc)
    grad_w_out = grad_w_out.reshape(n_blk // n_uly, n_uly, rows, width).transpose(1, 0, 2, 3)
    grad_w_out = grad_w_out.reshape(n_uly, n_blk // n_uly * rows, width)
    grad_heads, grad_w_proj = lax.optimization_barrier((grad_heads, grad_w_proj))
    grad_heads = to_heads(grad_heads, 1)
    fused = sharing == held == 1
    backs, result, grad_w_out, *grads = attend_back(
        bounds,
        grad_heads,
        natural,
        attended,
        logs,
        chip_sums,
        own_sum,
        hidden,
        bias_proj,
        grad_w_out,
        normed,
        layout,
        scale,
        fused,
    )
    backs = from_heads(backs, 3)
    if fused:
        grads = grads[0]
    else:
        grads = weight_grad(normed, backs, grad_w_out.reshape(n_blk, rows, width))
    sums_qkv = jnp.sum(backs.astype(F32), axis=0, keepdims=True)
    grads = sum_blk(grads).reshape(plane, rows, 4 * share)
    grad_w_out = grads[:, :, 3 * share :].transpose(1, 0, 2).reshape(rows, width)
    last, grad_fc = lax.optimization_barrier((backs, grad_fc))
    sums, grad_inputs, grad_fc = inputs_return(
        last,
        qkv,
        tokens,
        grad_hidden,
        gain_one,
        grad_fc.reshape(plane, rows, ff_share),
        sums_two,
        sums_fc,
        sums_qkv,
        sizes,
        order,
    )
    *grad_qkv, result = finish(grads, result, sizes)
    grad_w_proj, grad_fc, grad_w_out, result = lax.optimization_barrier(
        (grad_w_proj, grad_fc, grad_w_out, result)
    )
    grad_w_out = grad_w_out.astype(F32)
    grad_qkv = [g.astype(F32) for g in grad_qkv]
    if runs == 1:
        grad_fc = grad_fc.reshape(by_device).transpose(0, 1, 3, 2, 4).reshape(rows, -1)
    grad_fc = grad_fc.astype(F32)
    grad_w_proj = grad_w_proj.astype(F32)
    each = [sums[i, :rows] for i in range(8)]
    lanes = min(128, hidden_rows)
    grad_b_fc = sums[8 : 8 + hidden_rows // lanes, :lanes].reshape(-1)
    return (
        from_plane(result),
        from_plane(grad_inputs),
        each[0],
        each[1],
        grad_qkv[0],
        each[2],
        grad_qkv[1],
        grad_qkv[2],
        each[3],
        grad_w_out,
        each[4],
        each[5],
        each[6],
        grad_fc,
        grad_b_fc,
        grad_w_proj,
        each[7],
    )


def solution(mesh):
    tokens = P("seq", ("blk", "uly"), None)
    vector = P(ALL)
    matrix = P(ALL, None)
    return jax.shard_map(
        on_device,
        mesh=mesh,
        in_specs=(
            tokens, P("seq", None), vector, vector, matrix, vector, matrix, matrix, vector,
            matrix, vector, vector, vector, matrix, vector, matrix, vector, tokens,
        ),
        out_specs=(
            tokens, tokens, vector, vector, matrix, vector, matrix, matrix, vector,
            matrix, vector, vector, vector, matrix, vector, matrix, vector,
        ),
        check_vma=False,
    )
```
